128 devices in a mesh: batch: 32 (over x, z, core), mp: 4 (over y).
Axes of the slice: x: 4, y: 4, z: 4, core: 2. Of those that a mesh axis runs over, the one named last changes fastest.
Arguments:
- dense_feats: bfloat16 [4, 8192, 13], P('mp', 'batch'), may hold values from -6 to 6
- labels: int32 [4, 8192], P('mp', 'batch'), may hold values from 0 to 1
- session_lengths: int32 [4, 32, 32], P('mp', 'batch'), may hold values from 1 to 64, 256 in all within a row
- uniq_rows: int32 [32, 4, 3, 2048], P('batch', 'mp'), may hold values from 0 to 249, as said below
- dedup_map: int32 [32, 4, 8192], P('batch', 'mp'), may hold values from 0 to 2047, as said below
- core_first: bfloat16 [32, 200, 128], P('batch'), may hold values from -2.09375 to 2.09375
- core_mid: bfloat16 [32, 220, 4096], P('batch'), may hold values from -1 to 1
- core_last: bfloat16 [32, 250, 128], P('batch'), may hold values from -1 to 1
- bot_w1: bfloat16 [13, 512], replicated, may hold values from -1.75 to 1.75
- bot_b1: bfloat16 [512], replicated, may hold values from -3 to 3
- bot_w2: bfloat16 [512, 256], replicated, may hold values from -0.25 to 0.25
- bot_b2: bfloat16 [256], replicated, may hold values from -3 to 3
- bot_w3: bfloat16 [256, 64], replicated, may hold values from -0.375 to 0.375
- bot_b3: bfloat16 [64], replicated, may hold values from -3 to 3
- top_w1: bfloat16 [415, 512], P(None, 'mp'), may hold values from -0.3125 to 0.3125
- top_b1: bfloat16 [512], P('mp'), may hold values from -3 to 3
- top_w2: bfloat16 [512, 512], P('mp'), may hold values from -0.25 to 0.25
- top_b2: bfloat16 [512], replicated, may hold values from -3 to 3
- top_w3: bfloat16 [512, 256], replicated, may hold values from -0.25 to 0.25
- top_b3: bfloat16 [256], replicated, may hold values from -3 to 3
- top_w4: bfloat16 [256, 1], replicated, may hold values from -0.375 to 0.375
- top_b4: bfloat16 [1], replicated, may hold values from -3 to 3
Outputs:
- batch_loss: float32 [], replicated
- grad_core_first: float32 [32, 200, 128], P('batch')
- grad_core_mid: float32 [32, 220, 4096], P('batch')
- grad_core_last: float32 [32, 250, 128], P('batch')
- grad_bot_w1: float32 [13, 512], replicated
- grad_bot_b1: float32 [512], replicated
- grad_bot_w2: float32 [512, 256], replicated
- grad_bot_b2: float32 [256], replicated
- grad_bot_w3: float32 [256, 64], replicated
- grad_bot_b3: float32 [64], replicated
- grad_top_w1: float32 [415, 512], P(None, 'mp')
- grad_top_b1: float32 [512], P('mp')
- grad_top_w2: float32 [512, 512], P('mp')
- grad_top_b2: float32 [512], replicated
- grad_top_w3: float32 [512, 256], replicated
- grad_top_b3: float32 [256], replicated
- grad_top_w4: float32 [256, 1], replicated
- grad_top_b4: float32 [1], replicated
The draws below stay inside these ranges and needn't reach their ends.
Inputs may be any that keep to these rules, and one draw needn't show every extreme that they name: `uniq_rows`: component 0 is under 200, component 1 under 220, component 2 under 250. `dedup_map`: every row slot of a table slot and group is named by some lookup.
All inputs are finite; a program needn't handle non-finite values.
Results may differ from the reference program's by a relative error of at most 0.02.
Values may be sent and summed in bfloat16 or wider, within the bound.
No kernel may reach another device: no remote copies, remote signals or barrier semaphores. Data moves between devices by JAX's collectives and lax.ppermute only.
A program may use at most 128 MiB of HBM per device.

```python
import math
import jax
import jax.numpy as jnp
import numpy as np
from jax import lax

DENSE = 13
B1 = 512
B2 = 256
T1 = 4
T2 = 4
T3 = 4
EMB = 64
RANK = 32
R1 = 200
R2 = 220
R3 = 250
H1 = 512
H2 = 512
H3 = 256
TABLES = 26
SLOTS = 32
TOPIN = 415
EV_DEV = 256
EV_GRP = 8192
UNIQ = 2048
SESS_DEV = 32
SESS_MOST = 64
SESSIONS = 4096
N_BATCH = 32
N_MP = 4


def draw_uniq_rows(key, part):
    key = jax.random.fold_in(key, 11)
    key_first, key_mid, key_last = jax.random.split(key, 3)
    shape = (SLOTS, N_MP, UNIQ)
    first_ids = jax.random.randint(key_first, shape, 0, R1)
    mid_ids = jax.random.randint(key_mid, shape, 0, R2)
    last_ids = jax.random.randint(key_last, shape, 0, R3)
    return jnp.stack([first_ids, mid_ids, last_ids], axis=2).astype(jnp.int32)


def draw_dedup_map(key, part):
    key = jax.random.fold_in(key, 23)
    key_order, key_fill = jax.random.split(key)
    filler = jax.random.randint(key_fill, (SLOTS, N_MP, EV_GRP), 0, UNIQ)
    row_keys = jax.random.split(key_order, SLOTS * N_MP)
    orders = jax.vmap(lambda row_key: jax.random.permutation(row_key, EV_GRP))(row_keys)
    orders = orders.reshape(SLOTS, N_MP, EV_GRP)
    return jnp.where(orders < UNIQ, orders, filler).astype(jnp.int32)


def with_ends(drawn, own_key, smallest, largest):
    dims = drawn.shape
    place = [jax.random.randint(jax.random.fold_in(own_key, axis), (), 0, dims[axis]) for axis in range(len(dims))]
    drawn = drawn.at[tuple(place)].set(smallest)
    longest = dims.index(max(dims))
    place[longest] = (place[longest] + 1) % dims[longest]
    return drawn.at[tuple(place)].set(largest)


def block_levels(stream_key, shape, cuts, low, largest):
    def one(dim, parts):
        steps = jax.random.uniform(jax.random.fold_in(jax.random.fold_in(stream_key, 6), dim), (parts,), jnp.float32, low / len(cuts), largest / len(cuts))
        return jnp.repeat(jnp.exp(steps), shape[dim] // parts).reshape((-1,) + (1,) * (len(shape) - dim - 1))

    factor_of = one(*cuts[0])
    for cut in cuts[1:]:
        factor_of = factor_of * one(*cut)
    return factor_of


def length_profile(count, total, reach, skew):
    weights = [(1 << 20) // math.isqrt(grade ** skew) + 1 for grade in range(2, count + 1)]
    spare, counts = total - reach - (count - 1), [1] * (count - 1)
    while spare > 0:
        candidates = [i for i in range(count - 1) if counts[i] < reach]
        whole, remaining = sum([weights[i] for i in candidates]), spare
        for i in candidates:
            addition = min(reach - counts[i], max(1, remaining * weights[i] // whole), spare)
            counts[i] = counts[i] + addition
            spare = spare - addition
    return np.array([reach] + counts)


def uneven(stream_key, amount, total, bound, skew):
    if amount == 2:
        one = jax.random.randint(stream_key, (), max(1, total - bound), min(bound, total - 1) + 1)
        return jnp.stack([one, total - one])
    tallies = jnp.asarray(length_profile(amount, total, bound, skew), jnp.int32)
    couples = (amount - 1) // 2
    giver, sink = tallies[1:1 + 2 * couples:2], tallies[2:2 + 2 * couples:2]
    room = jnp.minimum(giver - 1, bound - sink)
    shifted = jax.random.randint(jax.random.fold_in(stream_key, 1), (couples,), 0, 1 << 20) % (room + 1)
    tallies = tallies.at[1:1 + 2 * couples:2].set(giver - shifted).at[2:2 + 2 * couples:2].set(sink + shifted)
    return tallies[jax.random.permutation(jax.random.fold_in(stream_key, 2), amount)]


def centred(key, dims, deviation, bound, cuts=(), kind=jnp.bfloat16):
    result = jax.random.normal(key, dims, jnp.float32) * deviation
    if len(cuts) > 0:
        result = block_levels(key, dims, cuts, -0.22, 0.18) * result
    return jnp.clip(result, min=-bound, max=bound).astype(kind)


def setup_inputs(seed: int = 0) -> dict:
    streams_of = jax.random.split(jax.random.key(seed), 23)
    dense_feats = centred(streams_of[0], (N_MP, EV_GRP, DENSE), 1.0, 6.0, ((0, 4), (1, 32)))
    labels = with_ends(jax.random.randint(streams_of[1], (N_MP, EV_GRP), 0, 2), jax.random.fold_in(streams_of[1], 1), 0, 1).astype(jnp.int32)
    session_lengths = jax.vmap(lambda own: uneven(own, SESS_DEV, EV_DEV, SESS_MOST, 2))(jax.random.split(streams_of[2], N_MP * N_BATCH)).reshape((N_MP, N_BATCH, SESS_DEV)).astype(jnp.int32)
    uniq_rows = draw_uniq_rows(jax.random.fold_in(streams_of[22], 71), 0)
    dedup_map = draw_dedup_map(jax.random.fold_in(streams_of[22], 71), 0)
    core_first = centred(streams_of[5], (SLOTS, R1, T1 * RANK), 0.35, 2.09375, ((0, 32),))
    core_mid = centred(streams_of[6], (SLOTS, R2, RANK * T2 * RANK), RANK ** -0.5, 1.0, ((0, 32),))
    core_last = centred(streams_of[7], (SLOTS, R3, RANK * T3), RANK ** -0.5, 1.0, ((0, 32),))
    bot_w1 = centred(streams_of[8], (DENSE, B1), DENSE ** -0.5, 1.75)
    bot_b1 = centred(streams_of[9], (B1,), 0.5, 3.0)
    bot_w2 = centred(streams_of[10], (B1, B2), B1 ** -0.5, 0.25)
    bot_b2 = centred(streams_of[11], (B2,), 0.5, 3.0)
    bot_w3 = centred(streams_of[12], (B2, EMB), B2 ** -0.5, 0.375)
    bot_b3 = centred(streams_of[13], (EMB,), 0.5, 3.0)
    top_w1 = centred(streams_of[14], (TOPIN, H1), TOPIN ** -0.5, 0.3125, ((1, 4),))
    top_b1 = centred(streams_of[15], (H1,), 0.5, 3.0, ((0, 4),))
    top_w2 = centred(streams_of[16], (H1, H2), H1 ** -0.5, 0.25, ((0, 4),))
    top_b2 = centred(streams_of[17], (H2,), 0.5, 3.0)
    top_w3 = centred(streams_of[18], (H2, H3), H2 ** -0.5, 0.25)
    top_b3 = centred(streams_of[19], (H3,), 0.5, 3.0)
    top_w4 = centred(streams_of[20], (H3, 1), H3 ** -0.5, 0.375)
    top_b4 = centred(streams_of[21], (1,), 0.5, 3.0)
    return dict(dense_feats=dense_feats, labels=labels, session_lengths=session_lengths, uniq_rows=uniq_rows, dedup_map=dedup_map, core_first=core_first, core_mid=core_mid, core_last=core_last, bot_w1=bot_w1, bot_b1=bot_b1, bot_w2=bot_w2, bot_b2=bot_b2, bot_w3=bot_w3, bot_b3=bot_b3, top_w1=top_w1, top_b1=top_b1, top_w2=top_w2, top_b2=top_b2, top_w3=top_w3, top_b3=top_b3, top_w4=top_w4, top_b4=top_b4)


@jax.custom_vjp
def low(v):
    return lax.optimization_barrier(v.astype(jnp.bfloat16)).astype(jnp.float32)

@jax.custom_vjp
def low_back(v):
    return v

def low_keep(v):
    return (low(v), None)

def low_pass(kept, grad):
    return (grad,)

def back_keep(v):
    return (v, None)

def back_low(kept, grad):
    return (low(grad),)
low.defvjp(low_keep, low_pass)
low_back.defvjp(back_keep, back_low)

def product(left, right):
    return jnp.dot(left, right, precision=lax.Precision.HIGHEST)

def smooth(value):
    return value * jax.nn.sigmoid(value)

def pair_flat(count):
    upper, right = np.triu_indices(count, 1)
    return upper * count + right

def session_weights(lengths):
    ends = jnp.cumsum(lengths, axis=-1)
    starts = ends - lengths
    position = jnp.arange(EV_DEV, dtype=jnp.int32)[:, None]
    inside = (position >= starts[..., None, :]) & (position < ends[..., None, :])
    inverse = 1.0 / lengths.astype(jnp.float32)
    return lax.optimization_barrier(jnp.sum(jnp.where(inside, inverse[..., None, :], 0.0), axis=-1))

def rebuild(block_item):
    core_first, core_mid, core_last, row_ids = block_item
    first_rows = core_first[row_ids[0]].reshape(-1, T1, RANK)
    mid_rows = core_mid[row_ids[1]].reshape(-1, RANK, T2 * RANK)
    inner_part = low(low_back(jnp.einsum('nar,nrs->nas', first_rows, mid_rows, precision=lax.Precision.HIGHEST)))
    last_rows = core_last[row_ids[2]].reshape(-1, RANK, T3)
    row_vecs = jnp.einsum('nkr,nrt->nkt', inner_part.reshape(-1, T1 * T2, RANK), last_rows, precision=lax.Precision.HIGHEST)
    return low(low_back(row_vecs.reshape(-1, EMB)))

def group_loss(params, group):
    core_first, core_mid, core_last, bot_w1, bot_b1, bot_w2, bot_b2, bot_w3, bot_b3, top_w1, top_b1, top_w2, top_b2, top_w3, top_b3, top_w4, top_b4 = params
    features, targets, weights, row_ids, slot_map = group
    row_table = lax.map(jax.checkpoint(rebuild), (core_first, core_mid, core_last, row_ids))
    pooled = jax.vmap(lambda table_rows, table_slots: table_rows[table_slots])(row_table, slot_map)
    pooled = low_back(pooled[:TABLES])
    hidden = low(smooth(low_back(product(features, bot_w1) + bot_b1)))
    hidden = low(smooth(low_back(product(hidden, bot_w2) + bot_b2)))
    bottom = low(smooth(low_back(product(hidden, bot_w3) + bot_b3)))
    feats = jnp.concatenate([bottom[:, None, :], jnp.transpose(pooled, (1, 0, 2))], axis=1)
    gram = jnp.einsum('etd,esd->ets', feats, feats, precision=lax.Precision.HIGHEST).reshape(EV_GRP, -1)
    top_in = low(jnp.concatenate([bottom, gram[:, pair_flat(TABLES + 1)]], axis=1))
    hid_one = low(smooth(low_back(product(top_in, top_w1) + top_b1)))
    hid_two = low(smooth(low_back(product(hid_one, top_w2) + top_b2)))
    hid_three = low(smooth(low_back(product(hid_two, top_w3) + top_b3)))
    logit = product(hid_three, top_w4)[:, 0] + top_b4[0]
    entropy = jax.nn.softplus(logit) - targets * logit
    return jnp.sum(weights * entropy) / SESSIONS

def reference(dense_feats, labels, session_lengths, uniq_rows, dedup_map, core_first, core_mid, core_last, bot_w1, bot_b1, bot_w2, bot_b2, bot_w3, bot_b3, top_w1, top_b1, top_w2, top_b2, top_w3, top_b3, top_w4, top_b4):
    params = tuple((item.astype(jnp.float32) for item in (core_first, core_mid, core_last, bot_w1, bot_b1, bot_w2, bot_b2, bot_w3, bot_b3, top_w1, top_b1, top_w2, top_b2, top_w3, top_b3, top_w4, top_b4)))
    features = dense_feats.astype(jnp.float32)
    targets = labels.astype(jnp.float32)
    weights = session_weights(session_lengths).reshape(N_MP, EV_GRP)
    row_ids = jnp.transpose(uniq_rows, (1, 0, 2, 3))
    slot_map = jnp.transpose(dedup_map, (1, 0, 2))

    def overall(values):

        def group_term(group):
            return jax.checkpoint(group_loss)(values, group)
        return jnp.sum(lax.map(group_term, (features, targets, weights, row_ids, slot_map)))
    batch_loss, pullback = jax.vjp(overall, params)
    gradients = pullback(jnp.ones_like(batch_loss))[0]
    return (batch_loss, gradients[0], gradients[1], gradients[2], gradients[3], gradients[4], gradients[5], gradients[6], gradients[7], gradients[8], gradients[9], gradients[10], gradients[11], gradients[12], gradients[13], gradients[14], gradients[15], gradients[16])
```

```python
import jax
import jax.numpy as jnp
from jax import lax
from jax.experimental import pallas as pl
from jax.experimental.pallas import tpu as pltpu
from jax.sharding import PartitionSpec as P

BF = jnp.bfloat16
F32 = jnp.float32
I32 = jnp.int32

R1, R2, R3 = 200, 220, 250
RANK = 32
EMB = 64
TABLES = 26
SLOTS = 32
UNIQ = 2048
EV_GRP = 8192
EV = 256
WIN = 16
MIDROWS = (R2 + WIN) * RANK
CH = 128
CHUNKS = UNIQ // CH
VMEM = pltpu.MemorySpace.VMEM


def iota(shape, dim):
    return lax.broadcasted_iota(I32, shape, dim)


def dot_nn(left, right):
    return lax.dot_general(left, right, (((1,), (0,)), ((), ())), preferred_element_type=F32)


def dot_nt(left, right):
    return lax.dot_general(left, right, (((1,), (1,)), ((), ())), preferred_element_type=F32)


def dot_tn(left, right):
    return lax.dot_general(left, right, (((0,), (0,)), ((), ())), preferred_element_type=F32)


def one_hot(row, count):
    return (iota((count, row.shape[1]), 0) == row).astype(F32).astype(BF)


def sum_rows_of_eight(parts):
    sub = iota(parts[0].shape, 0)
    step = 1
    while len(parts) > 1:
        keep = (sub & step) == 0
        merged = []
        for x, y in zip(parts[0::2], parts[1::2]):
            merged.append(jnp.where(keep, x, y) + pltpu.roll(jnp.where(keep, y, x), step, 0))
        parts = merged
        step *= 2
    return parts[0]


def pick_columns(table, row, groups):
    picked = dot_nn(table, one_hot(row & 511, 512))
    high = row >> 9
    total = jnp.where(high == 0, picked[0:EMB], 0.0)
    for g in range(1, groups):
        total = total + jnp.where(high == g, picked[g * EMB : (g + 1) * EMB], 0.0)
    return total


def masked_block(first, q_row, base):
    hit = (iota((WIN, CH), 0) + base == q_row).astype(F32)
    rows = []
    for q in range(WIN):
        flag = jnp.broadcast_to(hit[q : q + 1], (RANK, CH)).astype(BF)
        rows.append(
            jnp.concatenate([first[a * RANK : (a + 1) * RANK] * flag for a in range(4)], axis=1)
        )
    return jnp.concatenate(rows, axis=0)


def rebuild_kernel(
    uniq, dedup, cf, cm, cl, pooled, inner, ids, rank_out, mid_out, bounds,
    midf, pad, first_s, last_s, rows_s, acc, table, bounds_s, sem,
):
    for r in range(RANK):
        midf[pl.ds(r, R2, stride=RANK), :] = cm[0, :, r * 128 : (r + 1) * 128].astype(F32)
    mid_out[R2 * RANK :, :] = jnp.zeros((MIDROWS - R2 * RANK, 128), BF)

    def pack(k, _):
        at = pl.ds(pl.multiple_of(k * 640, 640), 640)
        mid_out[at, :] = midf[at, :].astype(BF)
        return 0

    lax.fori_loop(0, R2 * RANK // 640, pack, 0)

    q_row = uniq[0, 0, 1:2, :]
    q_index = iota((224, 1), 0)
    start = jnp.sum((q_row < q_index).astype(F32), axis=1, keepdims=True)
    before = (iota((256, 256), 0) < iota((256, 256), 1)).astype(F32).astype(BF)
    running = start
    ranks = []
    for b in range(UNIQ // 256):
        hit = (q_index == q_row[:, b * 256 : (b + 1) * 256]).astype(F32)
        place = dot_nn(hit.astype(BF), before) + running
        ranks.append(jnp.sum(hit * place, axis=0, keepdims=True))
        running = running + jnp.sum(hit, axis=1, keepdims=True)
    rank = jnp.concatenate(ranks, axis=1).astype(I32)
    rank_out[...] = rank

    lane = iota((1, 128), 1).astype(F32) * CH
    border = q_index > 0
    first_tile = jnp.sum((border & (start <= lane)).astype(F32), axis=0, keepdims=True)
    last_tile = jnp.sum((border & (start <= lane + (CH - 1))).astype(F32), axis=0, keepdims=True)
    first_tile, last_tile = jnp.minimum(first_tile, R2 - 1), jnp.minimum(last_tile, R2 - 1)
    sub = iota((8, 128), 0)
    bounds[...] = jnp.where(sub == 0, first_tile, jnp.where(sub == 1, last_tile, 0.0)).astype(I32)
    copy = pltpu.make_async_copy(bounds, bounds_s, sem)
    copy.start()

    high, low = rank >> 8, rank & 255
    spread = []
    for k in range(3):
        row = uniq[0, 0, k : k + 1, :].astype(F32)
        spread.append(jnp.where(iota((8, UNIQ), 0) == high, row, 0.0))
    spread.append(jnp.zeros((8, UNIQ), F32))
    spread = jnp.concatenate(spread, axis=0).astype(BF)
    by_low = dot_nt(spread, one_hot(low, 256))
    sorted_rows = []
    for k in range(3):
        sorted_rows.append(
            jnp.concatenate([by_low[8 * k + h : 8 * k + h + 1] for h in range(8)], axis=1)
        )
    edge = bounds[...].astype(F32)
    blank = jnp.zeros((1, UNIQ - 128), F32)
    for k in range(2):
        sorted_rows.append(jnp.concatenate([edge[k : k + 1], blank], axis=1))
    ids[...] = jnp.concatenate(sorted_rows + [jnp.zeros((3, UNIQ), F32)], axis=0)

    pad[...] = jnp.zeros((256, 128), BF)
    pad[0:R1, :] = cf[0]
    first_s[...] = dot_tn(pad[...], one_hot(ids[0:1, :].astype(I32), 256)).astype(BF)
    pad[0:R3, :] = cl[0]
    i, k = iota((128, 128), 0), iota((128, 128), 1)
    swap = ((i % 4) * RANK + i // 4 == k).astype(F32).astype(BF)
    last_rows = dot_nn(pad[...], swap).astype(BF)
    last_s[...] = dot_tn(last_rows, one_hot(ids[2:3, :].astype(I32), 256))
    copy.wait()

    def chunk(c, _):
        at = pl.ds(pl.multiple_of(c * CH, CH), CH)
        first = first_s[:, at]
        q_here = ids[1:2, at].astype(I32)
        acc[...] = jnp.zeros((128, 512), F32)

        low_q = bounds_s[0, c]

        def block(j, _):
            base = low_q + j * WIN
            mid = mid_out[pl.ds(pl.multiple_of(base * RANK, RANK), WIN * RANK), :]
            acc[...] += dot_tn(mid, masked_block(first, q_here, base))
            return 0

        lax.fori_loop(0, (bounds_s[1, c] - low_q) // WIN + 1, block, 0)
        inner_c = acc[...].astype(BF)
        inner[c] = inner_c
        wide = inner_c.astype(F32)
        last = last_s[:, at]
        for a in range(4):
            for h in range(2):
                parts = []
                for s2 in (2 * h, 2 * h + 1):
                    left = wide[s2 * RANK : (s2 + 1) * RANK, a * CH : (a + 1) * CH]
                    for t in range(4):
                        prod = left * last[t * RANK : (t + 1) * RANK]
                        parts.append((prod[0:8] + prod[8:16]) + (prod[16:24] + prod[24:32]))
                rows_s[a * 16 + h * 8 : a * 16 + h * 8 + 8, at] = sum_rows_of_eight(parts)
        return 0

    lax.fori_loop(0, CHUNKS, chunk, 0)

    sorted_table = jnp.concatenate(
        [rows_s[:, g * 512 : (g + 1) * 512].astype(BF) for g in range(4)], axis=0
    )
    for g in range(4):
        table[g * EMB : (g + 1) * EMB, :] = pick_columns(
            sorted_table, rank[:, g * 512 : (g + 1) * 512], 4
        ).astype(BF)

    def pool(k, _):
        row = dedup[0, :, pl.ds(pl.multiple_of(k * 512, 512), 512)]
        out = pick_columns(table[...], row, 4).astype(BF)
        pooled[2 * k] = out[:, 0:EV]
        pooled[2 * k + 1] = out[:, EV:]
        return 0

    lax.fori_loop(0, EV_GRP // 512, pool, 0)


def whole(count):
    return [pl.BlockSpec(memory_space=VMEM)] * count


def params(limit=56):
    return pltpu.CompilerParams(vmem_limit_bytes=limit * 2**20)


def cost(flops, size):
    return pl.CostEstimate(flops=flops, bytes_accessed=size, transcendentals=0)


def rebuild(uniq, dedup, cf, cm, cl):
    return pl.pallas_call(
        rebuild_kernel,
        out_shape=(
            jax.ShapeDtypeStruct((SLOTS, EMB, EV), BF),
            jax.ShapeDtypeStruct((CHUNKS, 128, 512), BF),
            jax.ShapeDtypeStruct((8, UNIQ), F32),
            jax.ShapeDtypeStruct((1, UNIQ), I32),
            jax.ShapeDtypeStruct((MIDROWS, 128), BF),
            jax.ShapeDtypeStruct((8, 128), I32),
        ),
        in_specs=whole(5),
        out_specs=tuple(whole(6)),
        scratch_shapes=[
            pltpu.VMEM((MIDROWS, 128), F32),
            pltpu.VMEM((256, 128), BF),
            pltpu.VMEM((128, UNIQ), BF),
            pltpu.VMEM((128, UNIQ), F32),
            pltpu.VMEM((EMB, UNIQ), F32),
            pltpu.VMEM((128, 512), F32),
            pltpu.VMEM((256, 512), BF),
            pltpu.SMEM((8, 128), I32),
            pltpu.SemaphoreType.DMA,
        ],
        compiler_params=params(),
        cost_estimate=cost(20_000_000_000, 10_000_000),
        name="rebuild",
    )(uniq, dedup, cf, cm, cl)


W1_ROWS = 416
W2_AT, ID_AT = W1_ROWS, W1_ROWS + 512
SHARE_ROWS = ID_AT + CHUNKS * 16
COPY_AT = ID_AT
GRAD_ROWS = 1536
COPY_ROWS = GRAD_ROWS - COPY_AT
PAIRS = [(a, c) for a in range(TABLES + 1) for c in range(a + 1, TABLES + 1)]


def silu(v):
    return v * jax.nn.sigmoid(v)


def slope(v):
    s = jax.nn.sigmoid(v)
    return s * (1.0 + v * (1.0 - s))


def spread_bias(row):
    return dot_tn(row, jnp.ones((1, EV), BF))


def share_kernel(w1, b1, w2, ids, rank, dedup, share, place):
    for m in range(4):
        share[m, 0:W1_ROWS, :] = jnp.zeros((W1_ROWS, 128), BF)
        share[m, 0:415, :] = w1[...]
        share[m, 415:416, :] = b1[...]
        for c in range(4):
            share[m, W2_AT + 128 * c : W2_AT + 128 * (c + 1), :] = w2[:, 128 * c : 128 * (c + 1)]
        for k in range(CHUNKS):
            tile = jnp.concatenate([ids[:, k * CH : (k + 1) * CH], jnp.zeros((8, CH), F32)], axis=0)
            share[m, ID_AT + 16 * k : ID_AT + 16 * (k + 1), :] = tile.astype(BF)

    order = rank[...]
    halves = []
    for g in range(4):
        part = order[:, g * 512 : (g + 1) * 512]
        halves += [(part >> 8).astype(F32), (part & 255).astype(F32)]
    halves = jnp.concatenate(halves + [jnp.zeros((8, 512), F32)], axis=0).astype(BF)

    def block(k, _):
        at = pl.ds(pl.multiple_of(k * 512, 512), 512)
        row = dedup[0, :, at]
        got = dot_nn(halves, one_hot(row & 511, 512))
        high = row >> 9
        total = jnp.zeros((1, 512), F32)
        for g in range(4):
            value = got[2 * g : 2 * g + 1] * 256.0 + got[2 * g + 1 : 2 * g + 2]
            total = total + jnp.where(high == g, value, 0.0)
        place[:, at] = total.astype(I32)
        return 0

    lax.fori_loop(0, EV_GRP // 512, block, 0)


def share_prep(w1, b1, w2, ids, rank, dedup):
    return pl.pallas_call(
        share_kernel,
        out_shape=(
            jax.ShapeDtypeStruct((4, SHARE_ROWS, 128), BF),
            jax.ShapeDtypeStruct((1, EV_GRP), I32),
        ),
        in_specs=whole(6),
        out_specs=tuple(whole(2)),
        compiler_params=params(),
        cost_estimate=cost(4_000_000_000, 3_000_000),
        name="share_prep",
    )(w1, b1, w2, ids, rank, dedup)


def bottom_kernel(x, w1, b1, w2, b2, w3, b3, feats, hid1, hid2, pre1, pre2, pre3, bottom):
    eye = (iota((16, 13), 0) == iota((16, 13), 1)).astype(F32).astype(BF)
    x_cols = dot_nt(eye, x[0])
    feats[...] = jnp.where(iota((16, EV), 0) == 13, 1.0, x_cols).astype(BF)
    v = dot_tn(w1[...], x_cols[0:13].astype(BF)) + spread_bias(b1[...])
    pre1[...] = v
    h = silu(v).astype(BF)
    hid1[...] = h
    v = dot_tn(w2[...], h) + spread_bias(b2[...])
    pre2[...] = v
    h = silu(v).astype(BF)
    hid2[...] = h
    v = dot_tn(w3[...], h) + spread_bias(b3[...])
    pre3[...] = v
    bottom[...] = silu(v).astype(BF)


def bottom_forward(x, w1, b1, w2, b2, w3, b3):
    shapes = (
        jax.ShapeDtypeStruct((16, EV), BF),
        jax.ShapeDtypeStruct((512, EV), BF),
        jax.ShapeDtypeStruct((256, EV), BF),
        jax.ShapeDtypeStruct((512, EV), F32),
        jax.ShapeDtypeStruct((256, EV), F32),
        jax.ShapeDtypeStruct((64, EV), F32),
        jax.ShapeDtypeStruct((64, EV), BF),
    )
    return pl.pallas_call(
        bottom_kernel,
        out_shape=shapes,
        in_specs=whole(7),
        out_specs=tuple(whole(7)),
        compiler_params=params(),
        cost_estimate=cost(2_000_000_000, 2_000_000),
        name="bottom_forward",
    )(x, w1, b1, w2, b2, w3, b3)


def session_weights(lens):
    i, k = iota((32, 32), 0), iota((32, 32), 1)
    ends = jnp.sum(jnp.where(k <= i, lens, 0.0), axis=1, keepdims=True)
    own = jnp.sum(jnp.where(k == i, lens, 0.0), axis=1, keepdims=True)
    position = iota((1, EV), 1).astype(F32)
    inside = (position >= ends - own) & (position < ends)
    return jnp.sum(jnp.where(inside, 1.0 / own, 0.0), axis=0, keepdims=True)


def event_kernel(
    arrived, bottom, share, w3, w4, b2, b3, b4, labels, lens,
    d_pooled, top_in, hid1, hid2, hid3, d_act1, d_act2, d_act3, d_bottom, scalars,
    feats, w1, w2, d_top, pair_grads,
):
    for m in range(4):
        w1[:, 128 * m : 128 * (m + 1)] = share[m, 0:W1_ROWS, :]
        for c in range(4):
            w2[128 * m : 128 * (m + 1), 128 * c : 128 * (c + 1)] = share[
                m, W2_AT + 128 * c : W2_AT + 128 * (c + 1), :
            ]
    feats[0] = bottom[...].astype(F32)

    def widen(t, _):
        feats[t + 1] = arrived[t].astype(F32)
        return 0

    lax.fori_loop(0, TABLES, widen, 0)

    top_in[0:EMB, :] = bottom[...]

    def gram_half(half, _):
        at = pl.ds(pl.multiple_of(half * 128, 128), 128)
        parts, row, held = [], EMB, []
        for a, c in PAIRS:
            prod = feats[a, :, at] * feats[c, :, at]
            part = prod[0:8]
            for k in range(1, 8):
                part = part + prod[8 * k : 8 * k + 8]
            parts.append(part)
            if (a, c) == PAIRS[-1]:
                parts.append(jnp.full((8, 128), 0.125, F32))
            if len(parts) == 8:
                held.append(sum_rows_of_eight(parts))
                parts = []
                if len(held) == 2:
                    top_in[row : row + 16, at] = jnp.concatenate(held, axis=0).astype(BF)
                    row += 16
                    held = []
        return 0

    lax.fori_loop(0, 2, gram_half, 0)

    act1 = dot_tn(w1[...], top_in[...])
    h = silu(act1).astype(BF)
    hid1[...] = h
    act2 = dot_tn(w2[...], h) + spread_bias(b2[...])
    h = silu(act2).astype(BF)
    hid2[...] = h
    act3 = dot_tn(w3[...], h) + spread_bias(b3[...])
    h = silu(act3).astype(BF)
    hid3[...] = h
    logit = dot_tn(w4[...], h) + b4[...].astype(F32)

    weight = session_weights(lens[0].astype(F32)) * (1.0 / 4096.0)
    target = labels[...].astype(F32)
    entropy = jnp.maximum(logit, 0.0) + jnp.log1p(jnp.exp(-jnp.abs(logit))) - target * logit
    d_logit = (jax.nn.sigmoid(logit) - target) * weight
    scalars[...] = jnp.concatenate(
        [d_logit, weight * entropy, jnp.zeros((6, EV), F32)], axis=0
    )

    d = ((w4[...].astype(F32) * d_logit) * slope(act3)).astype(BF)
    d_act3[...] = d
    d = (dot_nn(w3[...], d) * slope(act2)).astype(BF)
    d_act2[...] = d
    d = (dot_nn(w2[...], d) * slope(act1)).astype(BF)
    d_act1[...] = d
    d_top[...] = dot_nn(w1[...], d)

    at = EMB
    for a in range(TABLES):
        count = TABLES - a
        block = d_top[at : at + count, :]
        for half in range(2):
            part = block[:, 128 * half : 128 * half + 128]
            pair_grads[half, a * 32 + a + 1 : a * 32 + a + 1 + count, :] = part
            pair_grads[half, pl.ds((a + 1) * 32 + a, count, stride=32), :] = part
        at += count
    for a in range(TABLES + 1):
        for half in range(2):
            pair_grads[half, a * 32 + a : a * 32 + a + 1, :] = jnp.zeros((1, 128), F32)

    def vector_grad(a, half, lanes):
        grads = pair_grads[half, pl.ds(pl.multiple_of(a * 32, 32), 32), :]
        total = grads[0:1] * feats[0, :, lanes]
        for c in range(1, TABLES + 1):
            total = total + grads[c : c + 1] * feats[c, :, lanes]
        return total

    for half in range(2):
        lanes = slice(128 * half, 128 * half + 128)
        d_bottom[:, lanes] = d_top[0:EMB, lanes] + vector_grad(0, half, lanes)

        def table_grad(t, _):
            d_pooled[t, :, lanes] = vector_grad(t + 1, half, lanes).astype(BF)
            return 0

        lax.fori_loop(0, TABLES, table_grad, 0)
    d_pooled[TABLES:] = jnp.zeros((SLOTS - TABLES, EMB, EV), BF)


def event_step(arrived, bottom, share, w3, w4, b2, b3, b4, labels, lens):
    shapes = (
        jax.ShapeDtypeStruct((SLOTS, EMB, EV), BF),
        jax.ShapeDtypeStruct((W1_ROWS, EV), BF),
        jax.ShapeDtypeStruct((512, EV), BF),
        jax.ShapeDtypeStruct((512, EV), BF),
        jax.ShapeDtypeStruct((256, EV), BF),
        jax.ShapeDtypeStruct((512, EV), BF),
        jax.ShapeDtypeStruct((512, EV), BF),
        jax.ShapeDtypeStruct((256, EV), BF),
        jax.ShapeDtypeStruct((EMB, EV), F32),
        jax.ShapeDtypeStruct((8, EV), F32),
    )
    return pl.pallas_call(
        event_kernel,
        out_shape=shapes,
        in_specs=whole(10),
        out_specs=tuple(whole(10)),
        scratch_shapes=[
            pltpu.VMEM((TABLES + 1, EMB, EV), F32),
            pltpu.VMEM((W1_ROWS, 512), BF),
            pltpu.VMEM((512, 512), BF),
            pltpu.VMEM((W1_ROWS, EV), F32),
            pltpu.VMEM((2, (TABLES + 1) * 32, 128), F32),
        ],
        compiler_params=params(),
        cost_estimate=cost(10_000_000_000, 6_000_000),
        name="event_step",
    )(arrived, bottom, share, w3, w4, b2, b3, b4, labels, lens)


def weight_grad_kernel(
    feats, hb1, hb2, pre1, pre2, pre3, bw2, bw3, d_bottom,
    top_in, hid1, hid2, hid3, d_act1, d_act2, d_act3, scalars, out,
):
    ones = jnp.ones((16, EV), BF)
    g = dot_nt(top_in[...], d_act1[...]).astype(BF)
    for m in range(4):
        out[m, 0:W1_ROWS, :] = g[:, 128 * m : 128 * (m + 1)]
    g = dot_nt(hid1[...], d_act2[...]).astype(BF)
    for m in range(4):
        for c in range(4):
            out[m, W2_AT + 128 * c : W2_AT + 128 * (c + 1), :] = g[
                128 * m : 128 * (m + 1), 128 * c : 128 * (c + 1)
            ]
    g = dot_nt(hid2[...], d_act3[...]).astype(BF)
    for m in range(4):
        for c in range(2):
            at = COPY_AT + 256 + 128 * c
            out[m, at : at + 128, :] = g[128 * m : 128 * (m + 1), 128 * c : 128 * (c + 1)]

    d3 = (d_bottom[...] * slope(pre3[...])).astype(BF)
    d2 = (dot_nn(bw3[...], d3) * slope(pre2[...])).astype(BF)
    d1 = (dot_nn(bw2[...], d2) * slope(pre1[...])).astype(BF)
    g = dot_nt(hb1[...], d2).astype(BF)
    for m in range(4):
        for c in range(2):
            at = COPY_AT + 128 * c
            out[m, at : at + 128, :] = g[128 * m : 128 * (m + 1), 128 * c : 128 * (c + 1)]
    g = jnp.concatenate([dot_nt(hb2[...], d3), jnp.zeros((256, 64), F32)], axis=1).astype(BF)
    for m in range(4):
        out[m, COPY_AT + 512 : COPY_AT + 576, :] = g[64 * m : 64 * (m + 1)]
    g = dot_nt(feats[...], d1).astype(BF)
    for m in range(2):
        for c in range(2):
            at = COPY_AT + 576 + 16 * c
            out[m, at : at + 16, :] = g[:, 128 * (2 * m + c) : 128 * (2 * m + c + 1)]

    d_logit = scalars[0:1, :]
    coarse = d_logit.astype(BF)
    fine = (d_logit - coarse.astype(F32)).astype(BF)
    sub = iota((16, EV), 0)
    both = jnp.where(sub == 0, coarse.astype(F32), jnp.where(sub == 1, fine.astype(F32), 0.0))
    g4 = dot_nt(both.astype(BF), hid3[...])
    g4 = g4[0:1] + g4[1:2]
    s2 = dot_nt(ones, d_act2[...])[0:1]
    s3 = dot_nt(ones, d_act3[...])[0:1]
    sb2 = dot_nt(ones, d2)[0:1]
    sb3 = dot_nt(ones, d3)[0:1]
    rows = [s2[:, 128 * c : 128 * (c + 1)] for c in range(4)]
    rows += [s3[:, 0:128], s3[:, 128:], g4[:, 0:128], g4[:, 128:], sb2[:, 0:128], sb2[:, 128:]]
    rows.append(jnp.concatenate([sb3, jnp.zeros((1, 64), F32)], axis=1))
    lane = iota((1, 128), 1)
    tail = jnp.zeros((1, 128), F32)
    for k in range(2):
        value = jnp.sum(scalars[k : k + 1, :], axis=1, keepdims=True)
        high = value.astype(BF).astype(F32)
        tail = jnp.where(lane == 2 * k, high, tail)
        tail = jnp.where(lane == 2 * k + 1, value - high, tail)
    rows.append(tail)
    rows.append(jnp.zeros((4, 128), F32))
    small = jnp.concatenate(rows, axis=0).astype(BF)
    empty = jnp.zeros((16, 128), BF)
    out[2, COPY_AT + 576 : COPY_AT + 592, :] = small
    out[2, COPY_AT + 592 : COPY_AT + 608, :] = empty
    out[3, COPY_AT + 576 : COPY_AT + 592, :] = empty
    out[3, COPY_AT + 592 : COPY_AT + 608, :] = empty


def weight_grads(*args):
    return pl.pallas_call(
        weight_grad_kernel,
        out_shape=jax.ShapeDtypeStruct((4, GRAD_ROWS, 128), BF),
        in_specs=whole(17),
        out_specs=whole(1)[0],
        compiler_params=params(),
        cost_estimate=cost(6_000_000_000, 5_000_000),
        name="weight_grads",
    )(*args)


def sum_kernel(parts, out):
    count = parts.shape[0]

    def step(k, total):
        for i in range(8):
            total = total + parts[k * 8 + i].astype(F32)
        return total

    total = lax.fori_loop(0, count // 8, step, jnp.zeros(parts.shape[1:], F32))
    for k in range(out.shape[0]):
        out[k] = total.astype(BF)


def sum_parts(parts, copies):
    return pl.pallas_call(
        sum_kernel,
        out_shape=jax.ShapeDtypeStruct((copies,) + parts.shape[1:], BF),
        in_specs=whole(1),
        out_specs=whole(1)[0],
        compiler_params=params(),
        cost_estimate=cost(parts.size, 2 * parts.size),
        name="sum_parts",
    )(parts)


def unpack_kernel(
    mine, copied, tw1, tb1, tw2, bw1, bb1, bw2, bb2, bw3, bb3, tb2, tw3, tb3, tw4, tail
):
    tw1[...] = mine[0:415, :].astype(F32)
    tb1[...] = mine[400:416, :].astype(F32)[15:16]
    for c in range(4):
        tw2[:, 128 * c : 128 * (c + 1)] = mine[W2_AT + 128 * c : W2_AT + 128 * (c + 1), :].astype(F32)
    for m in range(4):
        for c in range(2):
            at = slice(128 * m, 128 * (m + 1)), slice(128 * c, 128 * (c + 1))
            bw2[at] = copied[m, 128 * c : 128 * (c + 1), :].astype(F32)
            tw3[at] = copied[m, 256 + 128 * c : 256 + 128 * (c + 1), :].astype(F32)
        bw3[64 * m : 64 * (m + 1), :] = copied[m, 512:576, 0:64].astype(F32)
    for m in range(2):
        for c in range(2):
            part = copied[m, 576 + 16 * c : 592 + 16 * c, :].astype(F32)
            lanes = slice(128 * (2 * m + c), 128 * (2 * m + c + 1))
            bw1[:, lanes] = part[0:13]
            bb1[:, lanes] = part[13:14]
    small = copied[2, 576:592, :].astype(F32)
    for c in range(4):
        tb2[:, 128 * c : 128 * (c + 1)] = small[c : c + 1]
    for c in range(2):
        lanes = slice(128 * c, 128 * (c + 1))
        tb3[:, lanes] = small[4 + c : 5 + c]
        tw4[:, lanes] = small[6 + c : 7 + c]
        bb2[:, lanes] = small[8 + c : 9 + c]
    bb3[...] = small[10:11, 0:64]
    pick = small[11:12]
    lane = iota((1, 128), 1)
    for k in range(2):
        value = jnp.sum(jnp.where((lane >> 1) == k, pick, 0.0), axis=1, keepdims=True)
        tail[k : k + 1, :] = jnp.broadcast_to(value, (1, 128))


def unpack(mine, copied):
    shapes = [
        (415, 128), (1, 128), (128, 512), (13, 512), (1, 512), (512, 256), (1, 256), (256, 64), (1, 64),
        (1, 512), (512, 256), (1, 256), (1, 256), (2, 128),
    ]
    return pl.pallas_call(
        unpack_kernel,
        out_shape=tuple(jax.ShapeDtypeStruct(s, F32) for s in shapes),
        in_specs=whole(2),
        out_specs=tuple(whole(len(shapes))),
        compiler_params=params(),
        cost_estimate=cost(1_000_000, 3_000_000),
        name="unpack",
    )(mine, copied)


def scatter_kernel(returned, place, out, acc):
    acc[...] = jnp.zeros((256, 512), F32)

    def block(k, _):
        row = place[:, pl.ds(pl.multiple_of(k * 512, 512), 512)]
        grads = jnp.concatenate([returned[2 * k], returned[2 * k + 1]], axis=1).astype(F32)
        high = row >> 9
        spread = [jnp.where(high == g, grads, 0.0).astype(BF) for g in range(4)]
        acc[...] += dot_nt(jnp.concatenate(spread, axis=0), one_hot(row & 511, 512))
        return 0

    lax.fori_loop(0, EV_GRP // 512, block, 0)
    for k in range(out.shape[0]):
        for g in range(4):
            out[k, :, 512 * g : 512 * (g + 1)] = acc[EMB * g : EMB * (g + 1), :].astype(BF)


def scatter_grads(returned, place):
    return pl.pallas_call(
        scatter_kernel,
        out_shape=jax.ShapeDtypeStruct((4, EMB, UNIQ), BF),
        in_specs=whole(2),
        out_specs=whole(1)[0],
        scratch_shapes=[pltpu.VMEM((256, 512), F32)],
        compiler_params=params(),
        cost_estimate=cost(4_000_000_000, 3_000_000),
        name="scatter_grads",
    )(returned, place)


def inner_grad(row_grads, last):
    columns = []
    for a in range(4):
        blocks = []
        for s2 in range(4):
            total = None
            for t in range(4):
                k = a * 16 + s2 * 4 + t
                term = row_grads[k : k + 1] * last[t * RANK : (t + 1) * RANK]
                total = term if total is None else total + term
            blocks.append(total)
        columns.append(jnp.concatenate(blocks, axis=0))
    return jnp.concatenate(columns, axis=1).astype(BF)


def swap_last(rows):
    i, k = iota((128, 128), 0), iota((128, 128), 1)
    return dot_nn(rows, ((i % 4) * RANK + i // 4 == k).astype(F32).astype(BF)).astype(BF)


def own_kernel(
    row_grads, inner, ids, bounds, mid, cl, out,
    pad, last_s, d_last, d_first, d_inner, acc,
):
    pad[...] = jnp.zeros((256, 128), BF)
    pad[0:R3, :] = cl[0]
    hot_last = one_hot(ids[2:3, :].astype(I32), 256)
    last_s[...] = dot_tn(swap_last(pad[...]), hot_last)

    def chunk(c, _):
        at = pl.ds(pl.multiple_of(c * CH, CH), CH)
        grads = row_grads[0, :, at].astype(F32)
        d_inner[...] = inner_grad(grads, last_s[:, at])
        wide = inner[c].astype(F32)
        for t in range(4):
            total = jnp.zeros((RANK, CH), F32)
            for a in range(4):
                for s2 in range(4):
                    k = a * 16 + s2 * 4 + t
                    total = total + grads[k : k + 1] * wide[
                        s2 * RANK : (s2 + 1) * RANK, a * CH : (a + 1) * CH
                    ]
            d_last[t * RANK : (t + 1) * RANK, at] = total.astype(BF)

        q_here = ids[1:2, at].astype(I32)
        low_q = bounds[0, c]
        acc[...] = jnp.zeros((RANK, 512), F32)

        def block(j, _):
            base = low_q + j * WIN
            rows = mid[pl.ds(pl.multiple_of(base * RANK, RANK), WIN * RANK), :]
            product = dot_nn(rows, d_inner[...])
            hit = jnp.concatenate([iota((WIN, CH), 0) + base == q_here] * 4, axis=1)
            total = acc[...]
            for q in range(WIN):
                total = total + jnp.where(
                    hit[q : q + 1], product[q * RANK : (q + 1) * RANK], 0.0
                )
            acc[...] = total
            return 0

        lax.fori_loop(0, (bounds[1, c] - low_q) // WIN + 1, block, 0)
        for a in range(4):
            d_first[a * RANK : (a + 1) * RANK, at] = acc[:, a * CH : (a + 1) * CH].astype(BF)
        return 0

    lax.fori_loop(0, CHUNKS, chunk, 0)
    g_first = dot_nt(one_hot(ids[0:1, :].astype(I32), 256), d_first[...]).astype(BF)
    g_last = dot_nt(hot_last, d_last[...]).astype(BF)
    i, k = iota((128, 128), 0), iota((128, 128), 1)
    back = ((k % 4) * RANK + k // 4 == i).astype(F32).astype(BF)
    g_last = dot_nn(g_last, back).astype(BF)
    for m in range(4):
        out[m, 0:256, :] = g_first
        out[m, 256:512, :] = g_last


def own_core_grads(row_grads, inner, ids, bounds, mid, cl):
    specs = whole(6)
    specs[3] = pl.BlockSpec(memory_space=pltpu.MemorySpace.SMEM)
    return pl.pallas_call(
        own_kernel,
        out_shape=jax.ShapeDtypeStruct((4, 512, 128), BF),
        in_specs=specs,
        out_specs=whole(1)[0],
        scratch_shapes=[
            pltpu.VMEM((256, 128), BF),
            pltpu.VMEM((128, UNIQ), F32),
            pltpu.VMEM((128, UNIQ), BF),
            pltpu.VMEM((128, UNIQ), BF),
            pltpu.VMEM((128, 512), BF),
            pltpu.VMEM((RANK, 512), F32),
        ],
        compiler_params=params(),
        cost_estimate=cost(10_000_000_000, 6_000_000),
        name="own_core_grads",
    )(row_grads, inner, ids, bounds, mid, cl)


def mid_grad_kernel(row_grads, share, edges, cf, cl, out, pad, lasts, first_s, last_s, acc):
    pad[...] = jnp.zeros((256, 128), BF)
    pad[0:R3, :] = cl[0]
    lasts[...] = swap_last(pad[...])
    pad[...] = jnp.zeros((256, 128), BF)
    pad[0:R1, :] = cf[0]

    def clear(k, _):
        acc[pl.ds(pl.multiple_of(k * 512, 512), 512), :] = jnp.zeros((512, 128), F32)
        return 0

    lax.fori_loop(0, MIDROWS // 512 + 1, clear, 0)

    def group(g, _):
        tiles = [
            share[g, ID_AT + 16 * k : ID_AT + 16 * (k + 1), :].astype(F32) for k in range(CHUNKS)
        ]
        p_row = jnp.concatenate([tile[0:1] for tile in tiles], axis=1).astype(I32)
        first_s[...] = dot_tn(pad[...], one_hot(p_row, 256)).astype(BF)
        r_row = jnp.concatenate([tile[2:3] for tile in tiles], axis=1).astype(I32)
        last_s[...] = dot_tn(lasts[...], one_hot(r_row, 256))

        def chunk(c, _):
            at = pl.ds(pl.multiple_of(c * CH, CH), CH)
            d_inner = inner_grad(row_grads[g, :, at].astype(F32), last_s[:, at])
            here = share[g, pl.ds(pl.multiple_of(ID_AT + 16 * c, 16), 16), :].astype(F32)
            q_here = here[1:2].astype(I32)
            first = first_s[:, at]
            low_q = edges[g, 0, c]

            def block(j, _):
                base = low_q + j * WIN
                rows = pl.ds(pl.multiple_of(base * RANK, RANK), WIN * RANK)
                acc[rows, :] += dot_nt(masked_block(first, q_here, base), d_inner)
                return 0

            lax.fori_loop(0, (edges[g, 1, c] - low_q) // WIN + 1, block, 0)
            return 0

        lax.fori_loop(0, CHUNKS, chunk, 0)
        return 0

    lax.fori_loop(0, 4, group, 0)
    for r in range(RANK):
        out[0, :, 128 * r : 128 * (r + 1)] = acc[pl.ds(r, R2, stride=RANK), :]


def mid_core_grad(row_grads, share, edges, cf, cl):
    specs = whole(5)
    specs[2] = pl.BlockSpec(memory_space=pltpu.MemorySpace.SMEM)
    return pl.pallas_call(
        mid_grad_kernel,
        out_shape=jax.ShapeDtypeStruct((1, R2, 4096), F32),
        in_specs=specs,
        out_specs=whole(1)[0],
        scratch_shapes=[
            pltpu.VMEM((256, 128), BF),
            pltpu.VMEM((256, 128), BF),
            pltpu.VMEM((128, UNIQ), BF),
            pltpu.VMEM((128, UNIQ), F32),
            pltpu.VMEM(((MIDROWS // 512 + 1) * 512, 128), F32),
        ],
        compiler_params=params(),
        cost_estimate=cost(40_000_000_000, 10_000_000),
        name="mid_core_grad",
    )(row_grads, share, edges, cf, cl)


def small_core_kernel(parts, first, last):
    total = parts[0].astype(F32)
    for m in range(1, 4):
        total = total + parts[m].astype(F32)
    first[0] = total[0:R1]
    last[0] = total[256 : 256 + R3]


def small_core_sum(parts):
    return pl.pallas_call(
        small_core_kernel,
        out_shape=(
            jax.ShapeDtypeStruct((1, R1, 128), F32),
            jax.ShapeDtypeStruct((1, R3, 128), F32),
        ),
        in_specs=whole(1),
        out_specs=tuple(whole(2)),
        compiler_params=params(),
        cost_estimate=cost(400_000, 1_000_000),
        name="small_core_sum",
    )(parts)


def exchange(value, axis):
    return lax.all_to_all(value, axis, 0, 0, tiled=True)


def body(
    dense_feats, labels, session_lengths, uniq_rows, dedup_map, core_first, core_mid, core_last,
    bot_w1, bot_b1, bot_w2, bot_b2, bot_w3, bot_b3,
    top_w1, top_b1, top_w2, top_b2, top_w3, top_b3, top_w4, top_b4,
):
    row = lambda v: v.reshape(1, -1)
    pooled, inner, ids, rank, mid, bounds = rebuild(
        uniq_rows, dedup_map, core_first, core_mid, core_last
    )
    arrived = exchange(pooled, "batch")
    share_out, place = share_prep(top_w1, row(top_b1), top_w2, ids, rank, dedup_map)
    share = exchange(share_out, "mp")
    feats, hb1, hb2, pre1, pre2, pre3, bottom = bottom_forward(
        dense_feats, bot_w1, row(bot_b1), bot_w2, row(bot_b2), bot_w3, row(bot_b3)
    )
    d_pooled, top_in, hid1, hid2, hid3, d_act1, d_act2, d_act3, d_bottom, scalars = event_step(
        arrived, bottom, share, top_w3, top_w4, row(top_b2), row(top_b3), row(top_b4),
        labels, session_lengths,
    )
    returned = exchange(d_pooled, "batch")
    grads = weight_grads(
        feats, hb1, hb2, pre1, pre2, pre3, bot_w2, bot_w3, d_bottom,
        top_in, hid1, hid2, hid3, d_act1, d_act2, d_act3, scalars,
    )
    parts = exchange(grads.reshape(128, GRAD_ROWS // 32, 128), ("mp", "batch"))

    row_grads = scatter_grads(returned, place)
    all_rows = exchange(row_grads, "mp")
    small = exchange(own_core_grads(row_grads, inner, ids, bounds, mid, core_last), "mp")
    edges = share[:, ID_AT + 3 : ID_AT + 5, 0:CHUNKS].astype(I32)
    grad_mid = mid_core_grad(all_rows, share, edges, core_first, core_last)
    grad_first, grad_last = small_core_sum(small)

    mine = exchange(sum_parts(parts, 32), "batch").reshape(GRAD_ROWS, 128)
    copied = exchange(jnp.broadcast_to(mine[COPY_AT:][None], (4, COPY_ROWS, 128)), "mp")
    tw1, tb1, tw2, bw1, bb1, bw2, bb2, bw3, bb3, tb2, tw3, tb3, tw4, tail = unpack(mine, copied)
    flat = lambda v: v.reshape(-1)
    return (
        tail[1, 0], grad_first, grad_mid, grad_last,
        bw1, flat(bb1), bw2, flat(bb2), bw3, flat(bb3),
        tw1, flat(tb1), tw2, flat(tb2), tw3, flat(tb3), tw4.reshape(256, 1), tail[0, 0:1],
    )


def solution(mesh):
    split = (
        P("mp", "batch", None), P("mp", "batch"), P("mp", "batch", None),
        P("batch", "mp", None, None), P("batch", "mp", None),
        P("batch", None, None), P("batch", None, None), P("batch", None, None),
        P(), P(), P(), P(), P(), P(),
        P(None, "mp"), P("mp"), P("mp", None), P(), P(), P(), P(), P(),
    )
    out = (
        P(), P("batch", None, None), P("batch", None, None), P("batch", None, None),
        P(), P(), P(), P(), P(), P(),
        P(None, "mp"), P("mp"), P("mp", None), P(), P(), P(), P(), P(),
    )
    return jax.shard_map(body, mesh=mesh, in_specs=split, out_specs=out, check_vma=False)
```

```python
import functools

import jax
import jax.numpy as jnp
from jax import lax
from jax.experimental import pallas as pl
from jax.experimental.pallas import tpu as pltpu
from jax.sharding import PartitionSpec as P

BF = jnp.bfloat16
F32 = jnp.float32
I32 = jnp.int32

R1, R2, R3 = 200, 220, 250
RANK = 32
EMB = 64
TABLES = 26
SLOTS = 32
UNIQ = 2048
EV_GRP = 8192
EV = 256
CH = 128
CHUNKS = UNIQ // CH
HALF = CH // 2
WIN = 16
HWIN = 10
PARTS = 4
UNROLL = 4
VMEM = pltpu.MemorySpace.VMEM
LIMITS = {
    "scatter_grads": 24, "sum_parts": 24, "unpack": 24, "core_rows": 24,
    "bottom_forward": 24, "lookup_places": 24, "share_prep": 24,
}


def iota(shape, dim):
    return lax.broadcasted_iota(I32, shape, dim)


def dot_nn(left, right):
    return lax.dot_general(left, right, (((1,), (0,)), ((), ())), preferred_element_type=F32)


def dot_nt(left, right):
    return lax.dot_general(left, right, (((1,), (1,)), ((), ())), preferred_element_type=F32)


def dot_tn(left, right):
    return lax.dot_general(left, right, (((0,), (0,)), ((), ())), preferred_element_type=F32)


def one_hot(row, count):
    return (iota((count, row.shape[1]), 0) == row).astype(F32).astype(BF)


def sum_rows_of_eight(parts):
    sub = iota(parts[0].shape, 0)
    step = 1
    while len(parts) > 1:
        keep = (sub & step) == 0
        merged = []
        for x, y in zip(parts[0::2], parts[1::2]):
            merged.append(jnp.where(keep, x, y) + pltpu.roll(jnp.where(keep, y, x), step, 0))
        parts = merged
        step *= 2
    return parts[0]


def pick_columns(table, row, groups):
    picked = dot_nn(table, one_hot(row & 511, 512))
    high = row >> 9
    total = jnp.where(high == 0, picked[0:EMB], 0.0)
    for g in range(1, groups):
        total = total + jnp.where(high == g, picked[g * EMB : (g + 1) * EMB], 0.0)
    return total


def window_start(low, count):
    return jnp.minimum(low, R2 - count)


def window_hits(q_row, low, count):
    hit = iota((count, q_row.shape[1]), 0) + window_start(low, count) == q_row
    return hit & (q_row >= low)


def masked_block(first, q_row, low, count):
    hit = window_hits(q_row, low, count).astype(F32)
    rows = []
    for q in range(count):
        flag = jnp.broadcast_to(hit[q : q + 1], (RANK, hit.shape[1])).astype(BF)
        rows.append(first * flag)
    return jnp.concatenate(rows, axis=0)


def window_rows(low, count):
    return pl.ds(pl.multiple_of(window_start(low, count) * RANK, RANK), count * RANK)


def side_by_side(block):
    return jnp.concatenate([block[a * RANK : (a + 1) * RANK] for a in range(4)], axis=1)


def half_lanes(block, h):
    pieces = [block[:, a * CH + h * HALF : a * CH + (h + 1) * HALF] for a in range(4)]
    return jnp.concatenate(pieces, axis=1)


def rebuild_kernel(
    uniq, dedup, cf, cm_far, cl, pooled, inner_far, ids, rank_out, mid_far, bounds,
    cm, midf, mid_out, inner, pad, first_s, last_s, rows_s, acc, table, bounds_s, sems,
):
    get_mid = pltpu.make_async_copy(cm_far, cm, sems.at[0])
    get_mid.start()

    q_row = uniq[0, 1]
    q_index = iota((224, 1), 0)
    start = jnp.sum((q_row < q_index).astype(F32), axis=1, keepdims=True)
    before = (iota((256, 256), 0) < iota((256, 256), 1)).astype(F32).astype(BF)
    running = start
    ranks = []
    for b in range(UNIQ // 256):
        hit = (q_index == q_row[:, b * 256 : (b + 1) * 256]).astype(F32)
        place = dot_nn(hit.astype(BF), before) + running
        ranks.append(jnp.sum(hit * place, axis=0, keepdims=True))
        running = running + jnp.sum(hit, axis=1, keepdims=True)
    rank = jnp.concatenate(ranks, axis=1).astype(I32)
    rank_out[...] = rank

    lane = iota((1, 128), 1).astype(F32) * HALF
    border = q_index > 0
    first_tile = jnp.sum((border & (start <= lane)).astype(F32), axis=0, keepdims=True)
    last_tile = jnp.sum((border & (start <= lane + (HALF - 1))).astype(F32), axis=0, keepdims=True)
    first_tile, last_tile = jnp.minimum(first_tile, R2 - 1), jnp.minimum(last_tile, R2 - 1)
    sub = iota((8, 128), 0)
    bounds[...] = jnp.where(sub == 0, first_tile, jnp.where(sub == 1, last_tile, 0.0)).astype(I32)
    copy = pltpu.make_async_copy(bounds, bounds_s, sems.at[1])
    copy.start()

    high, low = rank >> 8, rank & 255
    spread = []
    for k in range(3):
        row = uniq[0, k].astype(F32)
        spread.append(jnp.where(iota((8, UNIQ), 0) == high, row, 0.0))
    spread.append(jnp.zeros((8, UNIQ), F32))
    spread = jnp.concatenate(spread, axis=0).astype(BF)
    by_low = dot_nt(spread, one_hot(low, 256))
    sorted_rows = []
    for k in range(3):
        sorted_rows.append(
            jnp.concatenate([by_low[8 * k + h : 8 * k + h + 1] for h in range(8)], axis=1)
        )
    edge = bounds[...].astype(F32)
    blank = jnp.zeros((1, UNIQ - 128), F32)
    for k in range(2):
        sorted_rows.append(jnp.concatenate([edge[k : k + 1], blank], axis=1))
    ids[...] = jnp.concatenate(sorted_rows + [jnp.zeros((3, UNIQ), F32)], axis=0)

    pad[...] = jnp.zeros((256, 128), BF)
    pad[0:R1, :] = cf[0]
    first_s[...] = dot_tn(pad[...], one_hot(ids[0:1, :].astype(I32), 256)).astype(BF)
    pad[0:R3, :] = cl[0]
    i, k = iota((128, 128), 0), iota((128, 128), 1)
    swap = ((i % 4) * RANK + i // 4 == k).astype(F32).astype(BF)
    last_rows = dot_nn(pad[...], swap).astype(BF)
    last_s[...] = dot_tn(last_rows, one_hot(ids[2:3, :].astype(I32), 256))

    get_mid.wait()
    for r in range(RANK):
        midf[pl.ds(r, R2, stride=RANK + 1), :] = cm[0, :, r * 128 : (r + 1) * 128].astype(F32)

    def pack(k, _):
        for i in range(20):
            q = k * 20 + i
            rows = pl.ds(pl.multiple_of(q * RANK, RANK), RANK)
            mid_out[rows, :] = midf[pl.ds(q * (RANK + 1), RANK), :].astype(BF)
        return 0

    lax.fori_loop(0, R2 // 20, pack, 0)
    put_mid = pltpu.make_async_copy(mid_out, mid_far, sems.at[2])
    put_mid.start()
    copy.wait()

    def product(c, low):
        at = pl.ds(pl.multiple_of(c * CH, CH), CH)
        q_here = jnp.concatenate([ids[1:2, at].astype(I32)] * 4, axis=1)
        block = masked_block(side_by_side(first_s[:, at]), q_here, low, WIN)
        return dot_tn(mid_out[window_rows(low, WIN), :], block)

    def chunks(step, _):
        for u in range(UNROLL):
            c = step * UNROLL + u
            acc[u] = product(c, bounds_s[0, 2 * c])
        lows = [bounds_s[0, 2 * (step * UNROLL + u)] for u in range(UNROLL)]
        spans = [bounds_s[1, 2 * (step * UNROLL + u) + 1] - lows[u] for u in range(UNROLL)]

        @pl.when(functools.reduce(jnp.maximum, spans) >= WIN)
        def _():
            for u in range(UNROLL):

                def more(j, _):
                    acc[u] += product(step * UNROLL + u, lows[u] + j * WIN)
                    return 0

                lax.fori_loop(1, spans[u] // WIN + 1, more, 0)

        for u in range(UNROLL):
            c = step * UNROLL + u
            at = pl.ds(pl.multiple_of(c * CH, CH), CH)
            inner_c = acc[u].astype(BF)
            inner[c] = inner_c
            wide = inner_c.astype(F32)
            last = last_s[:, at]
            for a in range(4):
                for h in range(2):
                    parts = []
                    for s2 in (2 * h, 2 * h + 1):
                        left = wide[s2 * RANK : (s2 + 1) * RANK, a * CH : (a + 1) * CH]
                        for t in range(4):
                            prod = left * last[t * RANK : (t + 1) * RANK]
                            parts.append((prod[0:8] + prod[8:16]) + (prod[16:24] + prod[24:32]))
                    rows_s[a * 16 + h * 8 : a * 16 + h * 8 + 8, at] = sum_rows_of_eight(parts)
        return 0

    lax.fori_loop(0, CHUNKS // UNROLL, chunks, 0)
    put_inner = pltpu.make_async_copy(inner, inner_far, sems.at[3])
    put_inner.start()

    sorted_table = jnp.concatenate(
        [rows_s[:, g * 512 : (g + 1) * 512].astype(BF) for g in range(4)], axis=0
    )
    for g in range(4):
        table[g * EMB : (g + 1) * EMB, :] = pick_columns(
            sorted_table, rank[:, g * 512 : (g + 1) * 512], 4
        ).astype(BF)

    def pool(step, _):
        for u in range(8):
            k = step * 8 + u
            row = dedup[0, :, pl.ds(pl.multiple_of(k * 512, 512), 512)]
            out = pick_columns(table[...], row, 4).astype(BF)
            pooled[2 * k] = out[:, 0:EV]
            pooled[2 * k + 1] = out[:, EV:]
        return 0

    lax.fori_loop(0, EV_GRP // 4096, pool, 0)
    put_mid.wait()
    put_inner.wait()


def call(kernel, name, outs, args, scratch=(), flops=0, after=(), smem=(), left=(), out_left=()):
    args = list(args)
    if len(after):
        args[0] = lax.optimization_barrier((args[0], *after))[0]

    def spec(i, own, space):
        return pl.BlockSpec(memory_space=space if i in own else VMEM)

    specs = [
        pl.BlockSpec(memory_space=pltpu.MemorySpace.SMEM) if i in smem else spec(i, left, pl.ANY)
        for i in range(len(args))
    ]
    many = isinstance(outs, list)
    shapes = tuple(jax.ShapeDtypeStruct(*o) for o in (outs if many else [outs]))
    size = sum(a.size * a.dtype.itemsize for a in args)
    size += sum(o.size * o.dtype.itemsize for o in shapes)
    out_specs = tuple(spec(i, out_left, pltpu.MemorySpace.HBM) for i in range(len(shapes)))
    return pl.pallas_call(
        kernel,
        out_shape=shapes if many else shapes[0],
        in_specs=specs,
        out_specs=out_specs if many else out_specs[0],
        scratch_shapes=list(scratch),
        compiler_params=pltpu.CompilerParams(vmem_limit_bytes=LIMITS.get(name, 58) * 2**20),
        cost_estimate=pl.CostEstimate(flops=flops, bytes_accessed=size, transcendentals=0),
        name=name,
    )(*args)


def rebuild(*args):
    return call(
        rebuild_kernel,
        "rebuild",
        [
            ((SLOTS, EMB, EV), BF),
            ((CHUNKS, 128, 512), BF),
            ((8, UNIQ), F32),
            ((1, UNIQ), I32),
            ((R2 * RANK, 128), BF),
            ((8, 128), I32),
        ],
        args,
        [
            pltpu.VMEM((1, R2, 4096), BF),
            pltpu.VMEM((R2 * (RANK + 1), 128), F32),
            pltpu.VMEM((R2 * RANK, 128), BF),
            pltpu.VMEM((CHUNKS, 128, 512), BF),
            pltpu.VMEM((256, 128), BF),
            pltpu.VMEM((128, UNIQ), BF),
            pltpu.VMEM((128, UNIQ), F32),
            pltpu.VMEM((EMB, UNIQ), F32),
            pltpu.VMEM((UNROLL, 128, 512), F32),
            pltpu.VMEM((256, 512), BF),
            pltpu.SMEM((8, 128), I32),
            pltpu.SemaphoreType.DMA((4,)),
        ],
        flops=20_000_000_000,
        left=(3,),
        out_left=(1, 4),
    )


W1_ROWS = 416
W2_AT, ID_AT = W1_ROWS, W1_ROWS + 512
EDGE_AT = ID_AT + 48
SHARE_ROWS = EDGE_AT + 16
HALF_ROWS = 768
TAIL = 11
COPY0, COPY1 = W1_ROWS, 512
PAIRS = [(a, c) for a in range(TABLES + 1) for c in range(a + 1, TABLES + 1)]


def silu(v):
    return v * jax.nn.sigmoid(v)


def slope(v):
    s = jax.nn.sigmoid(v)
    return s * (1.0 + v * (1.0 - s))


def spread_bias(row):
    return dot_tn(row, jnp.ones((1, EV), BF))


def share_kernel(w1, b1, w2, ids, share):
    share[0:W1_ROWS, :] = jnp.zeros((W1_ROWS, 128), BF)
    share[0:415, :] = w1[...]
    share[415:416, :] = b1[...]
    for c in range(4):
        share[W2_AT + 128 * c : W2_AT + 128 * (c + 1), :] = w2[:, 128 * c : 128 * (c + 1)]
    for k in range(3):
        rows = [ids[k : k + 1, c * CH : (c + 1) * CH] for c in range(CHUNKS)]
        at = ID_AT + 16 * k
        share[at : at + 16, :] = jnp.concatenate(rows, axis=0).astype(BF)
    edges = jnp.concatenate([ids[3:5, 0:CH], jnp.zeros((14, CH), F32)], axis=0)
    share[EDGE_AT : EDGE_AT + 16, :] = edges.astype(BF)


def place_kernel(rank, dedup, place):
    order = rank[...]
    halves = []
    for g in range(4):
        part = order[:, g * 512 : (g + 1) * 512]
        halves += [(part >> 8).astype(F32), (part & 255).astype(F32)]
    halves = jnp.concatenate(halves + [jnp.zeros((8, 512), F32)], axis=0).astype(BF)

    def block(step, _):
        for u in range(4):
            at = pl.ds(pl.multiple_of(step * 4096 + u * 1024, 1024), 1024)
            row = dedup[0, :, at]
            got = dot_nn(halves, one_hot(row & 511, 512))
            high = row >> 9
            total = jnp.zeros((1, 1024), F32)
            for g in range(4):
                value = got[2 * g : 2 * g + 1] * 256.0 + got[2 * g + 1 : 2 * g + 2]
                total = total + jnp.where(high == g, value, 0.0)
            place[:, at] = total.astype(I32)
        return 0

    lax.fori_loop(0, EV_GRP // 4096, block, 0)


def share_prep(*args):
    return call(share_kernel, "share_prep", ((SHARE_ROWS, 128), BF), args)


def lookup_places(*args, after):
    return call(
        place_kernel, "lookup_places", ((1, EV_GRP), I32), args, flops=4_000_000_000, after=after
    )


def bottom_kernel(x, w1, b1, w2, b2, w3, b3, feats, hid1, hid2, pre1, pre2, pre3, bottom):
    x_cols = jnp.concatenate([x[0].astype(F32), jnp.ones((1, EV), F32), jnp.zeros((2, EV), F32)], axis=0)
    feats[...] = x_cols.astype(BF)
    v = dot_tn(w1[...], x[0]) + spread_bias(b1[...])
    pre1[...] = v
    h = silu(v).astype(BF)
    hid1[...] = h
    v = dot_tn(w2[...], h) + spread_bias(b2[...])
    pre2[...] = v
    h = silu(v).astype(BF)
    hid2[...] = h
    v = dot_nn(w3[...], h) + spread_bias(b3[...])
    pre3[...] = v
    bottom[...] = silu(v).astype(BF)


def bottom_forward(*args):
    outs = [
        ((16, EV), BF), ((512, EV), BF), ((256, EV), BF), ((512, EV), F32), ((256, EV), F32),
        ((64, EV), F32), ((64, EV), BF),
    ]
    return call(bottom_kernel, "bottom_forward", outs, args, flops=2_000_000_000)


def session_weights(lens):
    i, k = iota((32, 32), 0), iota((32, 32), 1)
    ends = jnp.sum(jnp.where(k <= i, lens, 0.0), axis=1, keepdims=True)
    own = jnp.sum(jnp.where(k == i, lens, 0.0), axis=1, keepdims=True)
    position = iota((1, EV), 1).astype(F32)
    inside = (position >= ends - own) & (position < ends)
    return jnp.sum(jnp.where(inside, 1.0 / own, 0.0), axis=0, keepdims=True)


def event_kernel(
    arrived_far, bottom, share0, share1, share2, share3, w3, w4, b2, b3, b4, labels, lens,
    d_pooled, top_in, hid1, hid2, hid3, d_act1, d_act2, d_act3, d_bottom, scalars,
    arrived, feats, w1, w2, d_top, pair_grads, sems,
):
    get_vectors = pltpu.make_async_copy(arrived_far.at[0:TABLES], arrived, sems.at[0])
    get_vectors.start()
    me = lax.axis_index("mp")
    get_weights = []
    for k, share in enumerate((share0, share1, share2, share3)):
        at = pl.ds(pl.multiple_of(lax.rem(me + 4 - k, 4) * 128, 128), 128)
        parts = [(share.at[0:W1_ROWS, :], w1.at[:, at])]
        for c in range(4):
            rows = slice(W2_AT + 128 * c, W2_AT + 128 * (c + 1))
            parts.append((share.at[rows, :], w2.at[at, 128 * c : 128 * (c + 1)]))
        for source, target in parts:
            copy = pltpu.make_async_copy(source, target, sems.at[1 + len(get_weights)])
            copy.start()
            get_weights.append(copy)
    get_vectors.wait()
    feats[0] = bottom[...].astype(F32)

    def widen(t, _):
        feats[t + 1] = arrived[t].astype(F32)
        return 0

    lax.fori_loop(0, TABLES, widen, 0)

    top_in[0:EMB, :] = bottom[...]

    def gram_half(half, _):
        at = pl.ds(pl.multiple_of(half * 128, 128), 128)
        parts, row, held = [], EMB, []
        for a, c in PAIRS:
            prod = feats[a, :, at] * feats[c, :, at]
            part = prod[0:8]
            for k in range(1, 8):
                part = part + prod[8 * k : 8 * k + 8]
            parts.append(part)
            if (a, c) == PAIRS[-1]:
                parts.append(jnp.full((8, 128), 0.125, F32))
            if len(parts) == 8:
                held.append(sum_rows_of_eight(parts))
                parts = []
                if len(held) == 2:
                    top_in[row : row + 16, at] = jnp.concatenate(held, axis=0).astype(BF)
                    row += 16
                    held = []
        return 0

    lax.fori_loop(0, 2, gram_half, 0)
    for copy in get_weights:
        copy.wait()

    act1 = dot_tn(w1[...], top_in[...])
    h = silu(act1).astype(BF)
    hid1[...] = h
    act2 = dot_tn(w2[...], h) + spread_bias(b2[...])
    h = silu(act2).astype(BF)
    hid2[...] = h
    act3 = dot_tn(w3[...], h) + spread_bias(b3[...])
    h = silu(act3).astype(BF)
    hid3[...] = h
    logit = dot_nn(w4[...], h) + b4[...].astype(F32)

    weight = session_weights(lens[0].astype(F32)) * (1.0 / 4096.0)
    target = labels[...].astype(F32)
    entropy = jnp.maximum(logit, 0.0) + jnp.log1p(jnp.exp(-jnp.abs(logit))) - target * logit
    d_logit = (jax.nn.sigmoid(logit) - target) * weight
    scalars[...] = jnp.concatenate(
        [d_logit, weight * entropy, jnp.zeros((6, EV), F32)], axis=0
    )

    d = (dot_tn(w4[...], jnp.ones((1, EV), BF)) * d_logit * slope(act3)).astype(BF)
    d_act3[...] = d
    d = (dot_nn(w3[...], d) * slope(act2)).astype(BF)
    d_act2[...] = d
    d = (dot_nn(w2[...], d) * slope(act1)).astype(BF)
    d_act1[...] = d
    d_top[...] = dot_nn(w1[...], d)

    at = EMB
    for a in range(TABLES):
        count = TABLES - a
        block = d_top[at : at + count, :]
        for half in range(2):
            part = block[:, 128 * half : 128 * half + 128]
            pair_grads[half, a * 33 + a + 1 : a * 33 + a + 1 + count, :] = part
            pair_grads[half, pl.ds((a + 1) * 33 + a, count, stride=33), :] = part
        at += count
    for a in range(TABLES + 1):
        for half in range(2):
            pair_grads[half, a * 33 + a : a * 33 + a + 1, :] = jnp.zeros((1, 128), F32)

    def vector_grads(places, half, lanes):
        grads = [pair_grads[half, pl.ds(a * 33, 32), :] for a in places]
        vector = feats[0, :, lanes]
        totals = [grad[0:1] * vector for grad in grads]
        for c in range(1, TABLES + 1):
            vector = feats[c, :, lanes]
            totals = [total + grad[c : c + 1] * vector for total, grad in zip(totals, grads)]
        return totals

    for half in range(2):
        lanes = slice(128 * half, 128 * half + 128)

        def table_grads(step, _):
            for i, total in enumerate(vector_grads([4 * step + i for i in range(1, 5)], half, lanes)):
                d_pooled[4 * step + i, :, lanes] = total.astype(BF)
            return 0

        lax.fori_loop(0, TABLES // 4, table_grads, 0)
        rest = vector_grads([0, TABLES - 1, TABLES], half, lanes)
        d_bottom[:, lanes] = d_top[0:EMB, lanes] + rest[0]
        d_pooled[TABLES - 2, :, lanes] = rest[1].astype(BF)
        d_pooled[TABLES - 1, :, lanes] = rest[2].astype(BF)
    d_pooled[TABLES:] = jnp.zeros((SLOTS - TABLES, EMB, EV), BF)


def event_step(*args, after):
    outs = [
        ((SLOTS, EMB, EV), BF), ((W1_ROWS, EV), BF), ((512, EV), BF), ((512, EV), BF), ((256, EV), BF),
        ((512, EV), BF), ((512, EV), BF), ((256, EV), BF), ((EMB, EV), F32), ((8, EV), F32),
    ]
    scratch = [
        pltpu.VMEM((TABLES, EMB, EV), BF),
        pltpu.VMEM((TABLES + 1, EMB, EV), F32),
        pltpu.VMEM((W1_ROWS, 512), BF),
        pltpu.VMEM((512, 512), BF),
        pltpu.VMEM((W1_ROWS, EV), F32),
        pltpu.VMEM((2, (TABLES + 1) * 33, 128), F32),
        pltpu.SemaphoreType.DMA((21,)),
    ]
    return call(
        event_kernel, "event_step", outs, args, scratch, flops=10_000_000_000, after=after,
        left=(0, 2, 3, 4, 5),
    )


def weight_grad_kernel(
    feats, hb1, hb2, pre1, pre2, pre3, bw2, bw3, d_bottom,
    top_in, hid1, hid2, hid3, d_act1, d_act2, d_act3, scalars, keep, send, out,
):
    def blocks(grad, half, at, count):
        for m in range(4):
            for c in range(count):
                out[half, m, at + 128 * c : at + 128 * (c + 1), :] = grad[
                    128 * m : 128 * (m + 1), 128 * c : 128 * (c + 1)
                ]

    ones = jnp.ones((16, EV), BF)
    g = dot_nt(top_in[...], d_act1[...]).astype(BF)
    for m in range(4):
        out[0, m, 0:W1_ROWS, :] = g[:, 128 * m : 128 * (m + 1)]
    blocks(dot_nt(hid1[...], d_act2[...]).astype(BF), 1, 0, 4)
    blocks(dot_nt(hid2[...], d_act3[...]).astype(BF), 1, COPY1, 2)

    d3 = (d_bottom[...] * slope(pre3[...])).astype(BF)
    d2 = (dot_tn(bw3[...], d3) * slope(pre2[...])).astype(BF)
    d1 = (dot_nn(bw2[...], d2) * slope(pre1[...])).astype(BF)
    blocks(dot_nt(hb1[...], d2).astype(BF), 0, COPY0, 2)
    at = COPY0 + 256
    g = dot_nt(d3, hb2[...]).astype(BF)
    for m in range(4):
        column = 128 * (m // 2)
        out[0, m, at : at + 64, :] = g[:, column : column + 128]
    at += 64
    g = dot_nt(feats[...], d1).astype(BF)
    for m in range(2):
        for c in range(2):
            out[0, m, at + 16 * c : at + 16 * (c + 1), :] = g[
                :, 128 * (2 * m + c) : 128 * (2 * m + c + 1)
            ]

    d_logit = scalars[0:1, :]
    coarse = d_logit.astype(BF)
    fine = (d_logit - coarse.astype(F32)).astype(BF)
    sub = iota((16, EV), 0)
    both = jnp.where(sub == 0, coarse.astype(F32), jnp.where(sub == 1, fine.astype(F32), 0.0))
    g4 = dot_nt(both.astype(BF), hid3[...])
    g4 = g4[0:1] + g4[1:2]
    s2 = dot_nt(ones, d_act2[...])[0:1]
    s3 = dot_nt(ones, d_act3[...])[0:1]
    sb2 = dot_nt(ones, d2)[0:1]
    sb3 = dot_nt(ones, d3)[0:1]
    rows = [s2[:, 128 * c : 128 * (c + 1)] for c in range(4)]
    rows += [s3[:, 0:128], s3[:, 128:], g4[:, 0:128], g4[:, 128:], sb2[:, 0:128], sb2[:, 128:]]
    rows.append(jnp.concatenate([sb3, jnp.zeros((1, 64), F32)], axis=1))
    lane = iota((1, 128), 1)
    tail = jnp.zeros((1, 128), F32)
    for k in range(2):
        value = jnp.sum(scalars[k : k + 1, :], axis=1, keepdims=True)
        high = value.astype(BF).astype(F32)
        tail = jnp.where(lane == 2 * k, high, tail)
        tail = jnp.where(lane == 2 * k + 1, value - high, tail)
    rows.append(tail)
    rows.append(jnp.zeros((4, 128), F32))
    empty = jnp.zeros((16, 128), BF)
    out[0, 2, at : at + 16, :] = jnp.concatenate(rows, axis=0).astype(BF)
    out[0, 2, at + 16 : at + 32, :] = empty
    out[0, 3, at : at + 16, :] = empty
    out[0, 3, at + 16 : at + 32, :] = empty

    core = lax.axis_index("core")
    for m in range(4):
        keep[m] = out[core, m]
        send[m] = out[1 - core, m]


def weight_grads(*args, after):
    shape = (4, HALF_ROWS, 128)
    return call(
        weight_grad_kernel, "weight_grads", [(shape, BF), (shape, BF)], args,
        [pltpu.VMEM((2,) + shape, BF)], flops=6_000_000_000, after=after,
    )


def pair_kernel(keep, got, out):
    for m in range(4):
        out[m] = (keep[m].astype(F32) + got[m].astype(F32)).astype(BF)

    @pl.when(lax.axis_index("core") == 0)
    def _():
        rows = slice(COPY0 + 320, COPY0 + 336)
        total = keep[2, rows, :].astype(F32) + got[2, rows, :].astype(F32)
        sub, lane = iota((16, 128), 0), iota((16, 128), 1)
        fixed = total
        for k in range(2):
            here = (sub == TAIL) & ((lane >> 1) == k)
            value = jnp.sum(jnp.where(here, total, 0.0))
            high = value.astype(BF).astype(F32)
            fixed = jnp.where(here, jnp.where(lane == 2 * k, high, value - high), fixed)
        out[2, rows, :] = fixed.astype(BF)


def sum_pair(keep, got):
    return call(pair_kernel, "sum_pair", (keep.shape, BF), [keep, got])


def sum_kernel(parts, out):
    def step(k, total):
        for i in range(8):
            total = total + parts[k * 8 + i].astype(F32)
        return total

    total = lax.fori_loop(0, parts.shape[0] // 8, step, jnp.zeros(parts.shape[1:], F32)).astype(BF)

    def put(k, _):
        for i in range(8):
            out[k * 8 + i] = total
        return 0

    lax.fori_loop(0, out.shape[0] // 8, put, 0)


def sum_parts(parts, copies, after):
    return call(sum_kernel, "sum_parts", ((copies,) + parts.shape[1:], BF), [parts], after=after)


def unpack_kernel(
    own, other, n0, n1, n2, n3,
    tw1, tb1, tw2, bw1, bb1, bw2, bb2, bw3, bb3, tb2, tw3, tb3, tw4, tb4, loss, core_first, core_last,
    halves, sems,
):
    core = lax.axis_index("core")
    copies = [
        pltpu.make_async_copy(own, halves.at[core], sems.at[0]),
        pltpu.make_async_copy(other, halves.at[1 - core], sems.at[1]),
    ]
    for copy in copies:
        copy.start()
    total = (n0[...].astype(F32) + n1[...].astype(F32)) + (n2[...].astype(F32) + n3[...].astype(F32))
    core_first[0] = total[0:R1]
    core_last[:, 0, :] = total[256 : 256 + R3]
    for copy in copies:
        copy.wait()

    me = lax.axis_index("mp")
    tw1[...] = halves[0, me, 0:415, :].astype(F32)
    tb1[...] = halves[0, me, 400:416, :].astype(F32)[15:16]
    for c in range(4):
        tw2[:, 128 * c : 128 * (c + 1)] = halves[1, me, 128 * c : 128 * (c + 1), :].astype(F32)
    for m in range(4):
        for c in range(2):
            at = slice(128 * m, 128 * (m + 1)), slice(128 * c, 128 * (c + 1))
            bw2[at] = halves[0, m, COPY0 + 128 * c : COPY0 + 128 * (c + 1), :].astype(F32)
            tw3[at] = halves[1, m, COPY1 + 128 * c : COPY1 + 128 * (c + 1), :].astype(F32)
    for m in range(2):
        bw3[:, 128 * m : 128 * (m + 1)] = halves[0, 2 * m, COPY0 + 256 : COPY0 + 320, :].astype(F32)
        for c in range(2):
            at = COPY0 + 320 + 16 * c
            part = halves[0, m, at : at + 16, :].astype(F32)
            lanes = slice(128 * (2 * m + c), 128 * (2 * m + c + 1))
            bw1[:, lanes] = part[0:13]
            bb1[:, lanes] = part[13:14]
    small = halves[0, 2, COPY0 + 320 : COPY0 + 336, :].astype(F32)
    for c in range(4):
        tb2[:, 128 * c : 128 * (c + 1)] = small[c : c + 1]
    for c in range(2):
        lanes = slice(128 * c, 128 * (c + 1))
        tb3[:, lanes] = small[4 + c : 5 + c]
        tw4[:, lanes] = small[6 + c : 7 + c]
        bb2[:, lanes] = small[8 + c : 9 + c]
    bb3[...] = small[10:11, 0:64]
    pick = small[11:12]
    half = iota((1, 128), 1) >> 1
    tb4[...] = jnp.sum(jnp.where(half == 0, pick, 0.0), axis=1, keepdims=True)
    loss[...] = jnp.sum(jnp.where(half == 1, pick, 0.0), axis=1, keepdims=True)


def unpack(args, after):
    shapes = [
        (415, 128), (1, 128), (128, 512), (13, 512), (1, 512), (512, 256), (1, 256), (64, 256), (1, 64),
        (1, 512), (512, 256), (1, 256), (1, 256), (1, 1), (1, 1), (1, R1, 128), (R3, 1, 128),
    ]
    scratch = [pltpu.VMEM((2, 4, HALF_ROWS, 128), BF), pltpu.SemaphoreType.DMA((2,))]
    return call(
        unpack_kernel, "unpack", [(s, F32) for s in shapes], args, scratch, after=after, left=(0, 1)
    )


def scatter_kernel(returned, place, out, acc):
    acc[...] = jnp.zeros((256, 512), F32)

    def block(k, _):
        row = place[:, pl.ds(pl.multiple_of(k * 4096, 4096), 4096)]
        grads = jnp.concatenate([returned[16 * k + i] for i in range(16)], axis=1).astype(F32)
        high = row >> 9
        spread = [jnp.where(high == g, grads, 0.0).astype(BF) for g in range(4)]
        acc[...] += dot_nt(jnp.concatenate(spread, axis=0), one_hot(row & 511, 512))
        return 0

    lax.fori_loop(0, EV_GRP // 4096, block, 0)
    for g in range(4):
        out[:, 512 * g : 512 * (g + 1)] = acc[EMB * g : EMB * (g + 1), :].astype(BF)


def scatter_grads(*args):
    return call(
        scatter_kernel, "scatter_grads", ((EMB, UNIQ), BF), args, [pltpu.VMEM((256, 512), F32)],
        flops=4_000_000_000,
    )


def inner_grad(row_grads, last):
    columns = []
    for a in range(4):
        blocks = []
        for s2 in range(4):
            total = None
            for t in range(4):
                k = a * 16 + s2 * 4 + t
                term = row_grads[k : k + 1] * last[t * RANK : (t + 1) * RANK]
                total = term if total is None else total + term
            blocks.append(total)
        columns.append(jnp.concatenate(blocks, axis=0))
    return jnp.concatenate(columns, axis=1).astype(BF)


def swap_last(rows):
    i, k = iota((128, 128), 0), iota((128, 128), 1)
    return dot_nn(rows, ((i % 4) * RANK + i // 4 == k).astype(F32).astype(BF)).astype(BF)


def core_rows_kernel(s0, s1, s2, s3, cf, cl, first, last, middle, edges, pad, lasts):
    pad[...] = jnp.zeros((256, 128), BF)
    pad[0:R3, :] = cl[0]
    lasts[...] = swap_last(pad[...])
    pad[...] = jnp.zeros((256, 128), BF)
    pad[0:R1, :] = cf[0]
    for g, share in enumerate((s0, s1, s2, s3)):
        factors = []
        for k in (0, 2):
            block = share[ID_AT + 16 * k : ID_AT + 16 * (k + 1), :].astype(F32)
            row = jnp.concatenate([block[c : c + 1] for c in range(CHUNKS)], axis=1)
            factors.append(row.astype(I32))
        first[g] = dot_tn(pad[...], one_hot(factors[0], 256)).astype(BF)
        last[g] = dot_tn(lasts[...], one_hot(factors[1], 256)).astype(BF)
        middle[g] = share[ID_AT + 16 : ID_AT + 32, :].astype(F32)
        edges[8 * g : 8 * (g + 1), :] = share[EDGE_AT : EDGE_AT + 16, :].astype(F32)[0:8].astype(I32)


def core_rows(*args, after):
    outs = [
        ((4, 128, UNIQ), BF), ((4, 128, UNIQ), BF), ((4, CHUNKS, CH), F32), ((32, 128), I32),
    ]
    scratch = [pltpu.VMEM((256, 128), BF), pltpu.VMEM((256, 128), BF)]
    return call(
        core_rows_kernel, "core_rows", outs, args, scratch, flops=6_000_000_000, after=after
    )


def own_kernel(
    row_grads, inner_far, ids, bounds, mid_far, lasts_far, out,
    inner, mid, last_s, d_last, d_first, d_halves, acc, hot_first, hot_last, sems,
):
    copies = [
        pltpu.make_async_copy(lasts_far.at[0], last_s, sems.at[0]),
        pltpu.make_async_copy(mid_far, mid, sems.at[1]),
    ]

    def get_inner(step):
        at = pl.ds(step * UNROLL, UNROLL)
        return pltpu.make_async_copy(inner_far.at[at], inner.at[at], sems.at[2 + step])

    for copy in copies:
        copy.start()
    for step in range(CHUNKS // UNROLL):
        get_inner(step).start()
    hot_first[...] = one_hot(ids[0:1, :].astype(I32), 256)
    hot_last[...] = one_hot(ids[2:3, :].astype(I32), 256)
    for copy in copies:
        copy.wait()

    def first_grad(c, h, low, d_half):
        at = pl.ds(pl.multiple_of(c * CH, CH), CH)
        q_here = jnp.concatenate([ids[1:2, at].astype(I32)[:, h * HALF : (h + 1) * HALF]] * 4, axis=1)
        hit = window_hits(q_here, low, HWIN)
        product = dot_nn(mid[window_rows(low, HWIN), :], d_half)
        total = jnp.where(hit[0:1], product[0:RANK], 0.0)
        for q in range(1, HWIN):
            total = total + jnp.where(hit[q : q + 1], product[q * RANK : (q + 1) * RANK], 0.0)
        return total

    def chunks(step, _):
        for u in range(UNROLL):
            c = step * UNROLL + u
            at = pl.ds(pl.multiple_of(c * CH, CH), CH)
            grads = row_grads[:, at].astype(F32)
            d_inner = inner_grad(grads, last_s[:, at].astype(F32))
            for h in range(2):
                d_half = half_lanes(d_inner, h)
                d_halves[2 * u + h] = d_half
                acc[2 * u + h] = first_grad(c, h, bounds[0, 2 * c + h], d_half)
        get_inner(step).wait()
        for u in range(UNROLL):
            c = step * UNROLL + u
            at = pl.ds(pl.multiple_of(c * CH, CH), CH)
            grads = row_grads[:, at].astype(F32)
            wide = inner[c].astype(F32)
            for t in range(4):
                total = None
                for a in range(4):
                    for s2 in range(4):
                        k = a * 16 + s2 * 4 + t
                        term = grads[k : k + 1] * wide[
                            s2 * RANK : (s2 + 1) * RANK, a * CH : (a + 1) * CH
                        ]
                        total = term if total is None else total + term
                d_last[t * RANK : (t + 1) * RANK, at] = total.astype(BF)
        lows = [bounds[0, step * 2 * UNROLL + i] for i in range(2 * UNROLL)]
        spans = [bounds[1, step * 2 * UNROLL + i] - lows[i] for i in range(2 * UNROLL)]

        @pl.when(functools.reduce(jnp.maximum, spans) >= HWIN)
        def _():
            for i in range(2 * UNROLL):

                def more(j, _):
                    low = lows[i] + j * HWIN
                    acc[i] += first_grad(step * UNROLL + i // 2, i % 2, low, d_halves[i])
                    return 0

                lax.fori_loop(1, spans[i] // HWIN + 1, more, 0)

        for u in range(UNROLL):
            c = step * UNROLL + u
            at = pl.ds(pl.multiple_of(c * CH, CH), CH)
            both = [acc[2 * u], acc[2 * u + 1]]
            for a in range(4):
                d_first[a * RANK : (a + 1) * RANK, at] = jnp.concatenate(
                    [part[:, a * HALF : (a + 1) * HALF] for part in both], axis=1
                ).astype(BF)
        return 0

    lax.fori_loop(0, CHUNKS // UNROLL, chunks, 0)
    g_first = dot_nt(hot_first[...], d_first[...]).astype(BF)
    g_last = dot_nt(hot_last[...], d_last[...]).astype(BF)
    i, k = iota((128, 128), 0), iota((128, 128), 1)
    back = ((k % 4) * RANK + k // 4 == i).astype(F32).astype(BF)
    g_last = dot_nn(g_last, back).astype(BF)
    out[0:256, :] = g_first
    out[256:512, :] = g_last


def own_core_grads(*args):
    scratch = [
        pltpu.VMEM((CHUNKS, 128, 512), BF),
        pltpu.VMEM((R2 * RANK, 128), BF),
        pltpu.VMEM((128, UNIQ), BF),
        pltpu.VMEM((128, UNIQ), BF),
        pltpu.VMEM((128, UNIQ), BF),
        pltpu.VMEM((2 * UNROLL, 128, 256), BF),
        pltpu.VMEM((2 * UNROLL, RANK, 256), F32),
        pltpu.VMEM((256, UNIQ), BF),
        pltpu.VMEM((256, UNIQ), BF),
        pltpu.SemaphoreType.DMA((2 + CHUNKS // UNROLL,)),
    ]
    return call(
        own_kernel, "own_core_grads", ((512, 128), BF), args, scratch, flops=10_000_000_000, smem=(3,),
        left=(1, 4, 5),
    )


def mid_grad_kernel(
    g0, g1, g2, g3, firsts_far, lasts_far, middle, edges, out_far,
    out, grads, firsts, lasts, d_halves, sems,
):
    copies = []
    for g, far in enumerate((g0, g1, g2, g3)):
        pairs = ((far, grads), (firsts_far.at[g], firsts), (lasts_far.at[g], lasts))
        copies.append([
            pltpu.make_async_copy(source, target.at[g], sems.at[3 * g + k])
            for k, (source, target) in enumerate(pairs)
        ])
    for group in copies:
        for copy in group:
            copy.start()

    def clear(k, _):
        at = pl.ds(pl.multiple_of(k * 640, 640), 640)
        out[at, :] = jnp.zeros((640, 128), F32)
        return 0

    lax.fori_loop(0, R2 * RANK // 640, clear, 0)

    def put(k):
        at = pl.ds(k * (R2 // PARTS) * RANK, R2 // PARTS * RANK)
        return pltpu.make_async_copy(out.at[at, :], out_far.at[at, :], sems.at[12 + k])

    for g in range(4):
        for copy in copies[g]:
            copy.wait()

        def mid_grad(c, h, low, d_half):
            at = pl.ds(pl.multiple_of(c * CH, CH), CH)
            q_here = middle[g, pl.ds(c, 1), :].astype(I32)
            q_here = jnp.concatenate([q_here[:, h * HALF : (h + 1) * HALF]] * 4, axis=1)
            first = half_lanes(side_by_side(firsts[g, :, at]), h)
            return dot_nt(masked_block(first, q_here, low, HWIN), d_half)

        def chunks(step, _):
            products = []
            for u in range(UNROLL):
                c = step * UNROLL + u
                at = pl.ds(pl.multiple_of(c * CH, CH), CH)
                d_inner = inner_grad(grads[g, :, at].astype(F32), lasts[g, :, at].astype(F32))
                for h in range(2):
                    d_half = half_lanes(d_inner, h)
                    d_halves[2 * u + h] = d_half
                    low_q = edges[8 * g, 2 * c + h]
                    products.append((low_q, mid_grad(c, h, low_q, d_half)))
            for low_q, product in products:
                out[window_rows(low_q, HWIN), :] += product
            lows = [edges[8 * g, step * 2 * UNROLL + v] for v in range(2 * UNROLL)]
            spans = [edges[8 * g + 1, step * 2 * UNROLL + v] - lows[v] for v in range(2 * UNROLL)]

            @pl.when(functools.reduce(jnp.maximum, spans) >= HWIN)
            def _():
                for v in range(2 * UNROLL):

                    def more(j, _):
                        low = lows[v] + j * HWIN
                        out[window_rows(low, HWIN), :] += mid_grad(
                            step * UNROLL + v // 2, v % 2, low, d_halves[v]
                        )
                        return 0

                    lax.fori_loop(1, spans[v] // HWIN + 1, more, 0)

            if g == 3:
                after = jnp.minimum(step + 1, CHUNKS // UNROLL - 1)
                done = jnp.where(step == CHUNKS // UNROLL - 1, R2, edges[8 * g, after * 2 * UNROLL])
                for k in range(PARTS):

                    @pl.when((lows[0] < (k + 1) * R2 // PARTS) & (done >= (k + 1) * R2 // PARTS))
                    def _():
                        put(k).start()

            return 0

        if g == 3:
            for k in range(PARTS):

                @pl.when(edges[8 * g, 0] >= (k + 1) * R2 // PARTS)
                def _():
                    put(k).start()

        lax.fori_loop(0, CHUNKS // UNROLL, chunks, 0)

    for k in range(PARTS):
        put(k).wait()


def mid_core_grad(row_grads, rows, after):
    scratch = [
        pltpu.VMEM((R2 * RANK, 128), F32),
        pltpu.VMEM((4, EMB, UNIQ), BF),
        pltpu.VMEM((4, 128, UNIQ), BF),
        pltpu.VMEM((4, 128, UNIQ), BF),
        pltpu.VMEM((2 * UNROLL, 128, 256), BF),
        pltpu.SemaphoreType.DMA((12 + PARTS,)),
    ]
    return call(
        mid_grad_kernel, "mid_core_grad", ((R2 * RANK, 128), F32), [*row_grads, *rows], scratch,
        flops=40_000_000_000, after=after, smem=(7,), left=(0, 1, 2, 3, 4, 5), out_left=(0,),
    )


BATCH = ("xz", "core")


def exchange(value, axes=BATCH):
    return lax.all_to_all(value, axes, 0, 0, tiled=True)


def from_before(value, places):
    return lax.ppermute(value, "mp", [(i, (i + places) % 4) for i in range(4)])


def gather_mp(value):
    return [value] + [from_before(value, k) for k in (1, 2, 3)]


def from_other_core(value):
    return lax.ppermute(value, "core", [(0, 1), (1, 0)])


def body(
    dense_feats, labels, session_lengths, uniq_rows, dedup_map, core_first, core_mid, core_last,
    bot_w1, bot_b1, bot_w2, bot_b2, bot_w3, bot_b3,
    top_w1, top_b1, top_w2, top_b2, top_w3, top_b3, top_w4, top_b4,
):
    row = lambda v: v.reshape(1, -1)
    pooled, inner, ids, rank, mid, bounds = rebuild(
        uniq_rows.transpose(0, 2, 1, 3), dedup_map, core_first, core_mid, core_last
    )
    arrived = exchange(pooled)
    share = share_prep(top_w1, row(top_b1), top_w2, ids)
    shares = gather_mp(share)
    place = lookup_places(rank, dedup_map, after=[share])
    feats, hb1, hb2, pre1, pre2, pre3, bottom = bottom_forward(
        dense_feats.transpose(0, 2, 1), bot_w1, row(bot_b1), bot_w2, row(bot_b2), bot_w3.T, row(bot_b3)
    )
    d_pooled, top_in, hid1, hid2, hid3, d_act1, d_act2, d_act3, d_bottom, scalars = event_step(
        arrived, bottom, *shares, top_w3, top_w4.T, row(top_b2), row(top_b3), row(top_b4),
        labels, session_lengths, after=[place],
    )
    returned = exchange(d_pooled)
    rows = core_rows(*shares, core_first, core_last, after=[d_pooled])
    keep, send = weight_grads(
        feats, hb1, hb2, pre1, pre2, pre3, bot_w2, bot_w3.T, d_bottom,
        top_in, hid1, hid2, hid3, d_act1, d_act2, d_act3, scalars, after=[rows[0]],
    )
    grads = sum_pair(keep, from_other_core(send))
    parts = exchange(grads.reshape(64, HALF_ROWS // 16, 128), ("mp", "xz"))

    row_grads = scatter_grads(returned, place)
    all_rows = gather_mp(row_grads)
    own = own_core_grads(row_grads, inner, ids, bounds, mid, rows[1])
    small = gather_mp(own)
    summed = sum_parts(parts, 64, after=[own, all_rows[1], all_rows[3]])
    half = exchange(summed, ("mp", "xz")).reshape(4, HALF_ROWS, 128)
    grad_mid = mid_core_grad(all_rows, rows, after=[summed, *small[1:]])
    half, grad_mid = lax.optimization_barrier((half, grad_mid))
    outs = unpack([half, from_other_core(half), *small], after=[grad_mid])
    tw1, tb1, tw2, bw1, bb1, bw2, bb2, bw3, bb3, tb2, tw3, tb3, tw4, tb4, loss, grad_first, grad_last = outs

    flat = lambda v: v.reshape(-1)
    return (
        loss[0, 0], grad_first, grad_mid.reshape(R2, 1, 4096).transpose(1, 0, 2),
        grad_last.transpose(1, 0, 2),
        bw1, flat(bb1), bw2, flat(bb2), bw3.T, flat(bb3),
        tw1, flat(tb1), tw2, flat(tb2), tw3, flat(tb3), tw4.T, flat(tb4),
    )


def solution(mesh):
    fine = jax.sharding.Mesh(mesh.devices.reshape(16, 2, 4), ("xz", "core", "mp"))
    split = (
        P("mp", BATCH, None), P("mp", BATCH), P("mp", BATCH, None),
        P(BATCH, "mp", None, None), P(BATCH, "mp", None),
        P(BATCH, None, None), P(BATCH, None, None), P(BATCH, None, None),
        P(), P(), P(), P(), P(), P(),
        P(None, "mp"), P("mp"), P("mp", None), P(), P(), P(), P(), P(),
    )
    out = (
        P(), P(BATCH, None, None), P(BATCH, None, None), P(BATCH, None, None),
        P(), P(), P(), P(), P(), P(),
        P(None, "mp"), P("mp"), P("mp", None), P(), P(), P(), P(), P(),
    )
    return jax.shard_map(body, mesh=fine, in_specs=split, out_specs=out, check_vma=False)
```

```python
import functools

import jax
import jax.numpy as jnp
from jax import lax
from jax.experimental import pallas as pl
from jax.experimental.pallas import tpu as pltpu
from jax.sharding import PartitionSpec as P

BF = jnp.bfloat16
F32 = jnp.float32
I32 = jnp.int32

R1, R2, R3 = 200, 220, 250
RANK = 32
EMB = 64
TABLES = 26
SLOTS = 32
UNIQ = 2048
EV_GRP = 8192
EV = 256
CH = 128
CHUNKS = UNIQ // CH
HALF = CH // 2
WIN = 16
HWIN = 10
PARTS = 4
UNROLL = 8
VMEM = pltpu.MemorySpace.VMEM
LIMITS = {
    "scatter_grads": 24, "sum_parts": 24, "unpack": 24, "core_rows": 24,
    "bottom_forward": 24, "lookup_places": 24, "share_prep": 24,
}


def iota(shape, dim):
    return lax.broadcasted_iota(I32, shape, dim)


def dot_nn(left, right):
    return lax.dot_general(left, right, (((1,), (0,)), ((), ())), preferred_element_type=F32)


def dot_nt(left, right):
    return lax.dot_general(left, right, (((1,), (1,)), ((), ())), preferred_element_type=F32)


def dot_tn(left, right):
    return lax.dot_general(left, right, (((0,), (0,)), ((), ())), preferred_element_type=F32)


def one_hot(row, count):
    return (iota((count, row.shape[1]), 0) == row).astype(F32).astype(BF)


def sum_rows_of_eight(parts):
    sub = iota(parts[0].shape, 0)
    step = 1
    while len(parts) > 1:
        keep = (sub & step) == 0
        merged = []
        for x, y in zip(parts[0::2], parts[1::2]):
            merged.append(jnp.where(keep, x, y) + pltpu.roll(jnp.where(keep, y, x), step, 0))
        parts = merged
        step *= 2
    return parts[0]


def pick_columns(table, row, groups):
    picked = dot_nn(table, one_hot(row & 511, 512))
    high = row >> 9
    total = jnp.where(high == 0, picked[0:EMB], 0.0)
    for g in range(1, groups):
        total = total + jnp.where(high == g, picked[g * EMB : (g + 1) * EMB], 0.0)
    return total


def window_start(low, count):
    return jnp.minimum(low, R2 - count)


def window_hits(q_row, low, count):
    hit = iota((count, q_row.shape[1]), 0) + window_start(low, count) == q_row
    return hit & (q_row >= low)


def masked_block(first, q_row, low, count):
    hit = window_hits(q_row, low, count).astype(F32)
    rows = []
    for q in range(count):
        flag = jnp.broadcast_to(hit[q : q + 1], (RANK, hit.shape[1])).astype(BF)
        rows.append(first * flag)
    return jnp.concatenate(rows, axis=0)


def window_rows(low, count):
    return pl.ds(pl.multiple_of(window_start(low, count) * RANK, RANK), count * RANK)


def side_by_side(block):
    return jnp.concatenate([block[a * RANK : (a + 1) * RANK] for a in range(4)], axis=1)


def half_lanes(block, h):
    pieces = [block[:, a * CH + h * HALF : a * CH + (h + 1) * HALF] for a in range(4)]
    return jnp.concatenate(pieces, axis=1)


def rebuild_kernel(
    uniq, dedup, cf, cm_far, cl, pooled, inner_far, ids, rank_out, mid_far, bounds,
    cm, midf, mid_out, inner, pad, first_s, last_s, rows_s, acc, table, bounds_s, sems,
):
    get_mid = pltpu.make_async_copy(cm_far, cm, sems.at[0])
    get_mid.start()

    q_row = uniq[0, 1]
    q_index = iota((224, 1), 0)
    start = jnp.sum((q_row < q_index).astype(F32), axis=1, keepdims=True)
    before = (iota((256, 256), 0) < iota((256, 256), 1)).astype(F32).astype(BF)
    running = start
    ranks = []
    for b in range(UNIQ // 256):
        hit = (q_index == q_row[:, b * 256 : (b + 1) * 256]).astype(F32)
        place = dot_nn(hit.astype(BF), before) + running
        ranks.append(jnp.sum(hit * place, axis=0, keepdims=True))
        running = running + jnp.sum(hit, axis=1, keepdims=True)
    rank = jnp.concatenate(ranks, axis=1).astype(I32)
    rank_out[...] = rank

    lane = iota((1, 128), 1).astype(F32) * HALF
    border = q_index > 0
    first_tile = jnp.sum((border & (start <= lane)).astype(F32), axis=0, keepdims=True)
    last_tile = jnp.sum((border & (start <= lane + (HALF - 1))).astype(F32), axis=0, keepdims=True)
    first_tile, last_tile = jnp.minimum(first_tile, R2 - 1), jnp.minimum(last_tile, R2 - 1)
    sub = iota((8, 128), 0)
    bounds[...] = jnp.where(sub == 0, first_tile, jnp.where(sub == 1, last_tile, 0.0)).astype(I32)
    copy = pltpu.make_async_copy(bounds, bounds_s, sems.at[1])
    copy.start()

    high, low = rank >> 8, rank & 255
    spread = []
    for k in range(3):
        row = uniq[0, k].astype(F32)
        spread.append(jnp.where(iota((8, UNIQ), 0) == high, row, 0.0))
    spread.append(jnp.zeros((8, UNIQ), F32))
    spread = jnp.concatenate(spread, axis=0).astype(BF)
    by_low = dot_nt(spread, one_hot(low, 256))
    sorted_rows = []
    for k in range(3):
        sorted_rows.append(
            jnp.concatenate([by_low[8 * k + h : 8 * k + h + 1] for h in range(8)], axis=1)
        )
    edge = bounds[...].astype(F32)
    blank = jnp.zeros((1, UNIQ - 128), F32)
    for k in range(2):
        sorted_rows.append(jnp.concatenate([edge[k : k + 1], blank], axis=1))
    ids[...] = jnp.concatenate(sorted_rows + [jnp.zeros((3, UNIQ), F32)], axis=0)

    pad[...] = jnp.zeros((256, 128), BF)
    pad[0:R1, :] = cf[0]
    first_s[...] = dot_tn(pad[...], one_hot(ids[0:1, :].astype(I32), 256)).astype(BF)
    pad[0:R3, :] = cl[0]
    i, k = iota((128, 128), 0), iota((128, 128), 1)
    swap = ((i % 4) * RANK + i // 4 == k).astype(F32).astype(BF)
    last_rows = dot_nn(pad[...], swap).astype(BF)
    last_s[...] = dot_tn(last_rows, one_hot(ids[2:3, :].astype(I32), 256))

    get_mid.wait()
    for r in range(RANK):
        midf[pl.ds(r, R2, stride=RANK + 1), :] = cm[0, :, r * 128 : (r + 1) * 128].astype(F32)

    def pack(k, _):
        for i in range(20):
            q = k * 20 + i
            rows = pl.ds(pl.multiple_of(q * RANK, RANK), RANK)
            mid_out[rows, :] = midf[pl.ds(q * (RANK + 1), RANK), :].astype(BF)
        return 0

    lax.fori_loop(0, R2 // 20, pack, 0)
    put_mid = pltpu.make_async_copy(mid_out, mid_far, sems.at[2])
    put_mid.start()
    copy.wait()

    def product(c, low):
        at = pl.ds(pl.multiple_of(c * CH, CH), CH)
        q_here = jnp.concatenate([ids[1:2, at].astype(I32)] * 4, axis=1)
        block = masked_block(side_by_side(first_s[:, at]), q_here, low, WIN)
        return dot_tn(mid_out[window_rows(low, WIN), :], block)

    def chunks(step, _):
        for u in range(UNROLL):
            c = step * UNROLL + u
            acc[u] = product(c, bounds_s[0, 2 * c])
        lows = [bounds_s[0, 2 * (step * UNROLL + u)] for u in range(UNROLL)]
        spans = [bounds_s[1, 2 * (step * UNROLL + u) + 1] - lows[u] for u in range(UNROLL)]

        @pl.when(functools.reduce(jnp.maximum, spans) >= WIN)
        def _():
            for u in range(UNROLL):

                def more(j, _):
                    acc[u] += product(step * UNROLL + u, lows[u] + j * WIN)
                    return 0

                lax.fori_loop(1, spans[u] // WIN + 1, more, 0)

        for u in range(UNROLL):
            c = step * UNROLL + u
            at = pl.ds(pl.multiple_of(c * CH, CH), CH)
            inner_c = acc[u].astype(BF)
            inner[c] = inner_c
            wide = inner_c.astype(F32)
            last = last_s[:, at]
            for a in range(4):
                for h in range(2):
                    parts = []
                    for s2 in (2 * h, 2 * h + 1):
                        left = wide[s2 * RANK : (s2 + 1) * RANK, a * CH : (a + 1) * CH]
                        for t in range(4):
                            prod = left * last[t * RANK : (t + 1) * RANK]
                            parts.append((prod[0:8] + prod[8:16]) + (prod[16:24] + prod[24:32]))
                    rows_s[a * 16 + h * 8 : a * 16 + h * 8 + 8, at] = sum_rows_of_eight(parts)
        return 0

    lax.fori_loop(0, CHUNKS // UNROLL, chunks, 0)
    put_inner = pltpu.make_async_copy(inner, inner_far, sems.at[3])
    put_inner.start()

    sorted_table = jnp.concatenate(
        [rows_s[:, g * 512 : (g + 1) * 512].astype(BF) for g in range(4)], axis=0
    )
    for g in range(4):
        table[g * EMB : (g + 1) * EMB, :] = pick_columns(
            sorted_table, rank[:, g * 512 : (g + 1) * 512], 4
        ).astype(BF)

    def pool(step, _):
        for u in range(8):
            k = step * 8 + u
            row = dedup[0, :, pl.ds(pl.multiple_of(k * 512, 512), 512)]
            out = pick_columns(table[...], row, 4).astype(BF)
            pooled[2 * k] = out[:, 0:EV]
            pooled[2 * k + 1] = out[:, EV:]
        return 0

    lax.fori_loop(0, EV_GRP // 4096, pool, 0)
    put_mid.wait()
    put_inner.wait()


def call(kernel, name, outs, args, scratch=(), flops=0, after=(), smem=(), left=(), near=(), out_left=()):
    args = list(args)
    if len(after):
        args[0] = lax.optimization_barrier((args[0], *after))[0]

    def spec(i, far, anywhere=()):
        space = pltpu.MemorySpace.HBM if i in far else pl.ANY if i in anywhere else VMEM
        return pl.BlockSpec(memory_space=space)

    specs = [
        pl.BlockSpec(memory_space=pltpu.MemorySpace.SMEM) if i in smem else spec(i, left, near)
        for i in range(len(args))
    ]
    many = isinstance(outs, list)
    shapes = tuple(jax.ShapeDtypeStruct(*o) for o in (outs if many else [outs]))
    size = sum(a.size * a.dtype.itemsize for a in args)
    size += sum(o.size * o.dtype.itemsize for o in shapes)
    out_specs = tuple(spec(i, out_left) for i in range(len(shapes)))
    return pl.pallas_call(
        kernel,
        out_shape=shapes if many else shapes[0],
        in_specs=specs,
        out_specs=out_specs if many else out_specs[0],
        scratch_shapes=list(scratch),
        compiler_params=pltpu.CompilerParams(vmem_limit_bytes=LIMITS.get(name, 58) * 2**20),
        cost_estimate=pl.CostEstimate(flops=flops, bytes_accessed=size, transcendentals=0),
        name=name,
    )(*args)


def rebuild(*args):
    return call(
        rebuild_kernel,
        "rebuild",
        [
            ((SLOTS, EMB, EV), BF),
            ((CHUNKS, 128, 512), BF),
            ((8, UNIQ), F32),
            ((1, UNIQ), I32),
            ((R2 * RANK, 128), BF),
            ((8, 128), I32),
        ],
        args,
        [
            pltpu.VMEM((1, R2, 4096), BF),
            pltpu.VMEM((R2 * (RANK + 1), 128), F32),
            pltpu.VMEM((R2 * RANK, 128), BF),
            pltpu.VMEM((CHUNKS, 128, 512), BF),
            pltpu.VMEM((256, 128), BF),
            pltpu.VMEM((128, UNIQ), BF),
            pltpu.VMEM((128, UNIQ), F32),
            pltpu.VMEM((EMB, UNIQ), F32),
            pltpu.VMEM((UNROLL, 128, 512), F32),
            pltpu.VMEM((256, 512), BF),
            pltpu.SMEM((8, 128), I32),
            pltpu.SemaphoreType.DMA((4,)),
        ],
        flops=20_000_000_000,
        left=(3,),
        out_left=(1, 4),
    )


W1_ROWS = 416
W2_AT, ID_AT = W1_ROWS, W1_ROWS + 512
EDGE_AT = ID_AT + 48
SHARE_ROWS = EDGE_AT + 16
HALF_ROWS = 768
TAIL = 11
COPY0, COPY1 = W1_ROWS, 512
PAIRS = [(a, c) for a in range(TABLES + 1) for c in range(a + 1, TABLES + 1)]


def silu(v):
    return v * jax.nn.sigmoid(v)


def slope(v):
    s = jax.nn.sigmoid(v)
    return s * (1.0 + v * (1.0 - s))


def spread_bias(row):
    return dot_tn(row, jnp.ones((1, EV), BF))


def share_kernel(w1, b1, w2, ids, share):
    share[0:W1_ROWS, :] = jnp.zeros((W1_ROWS, 128), BF)
    share[0:415, :] = w1[...]
    share[415:416, :] = b1[...]
    for c in range(4):
        share[W2_AT + 128 * c : W2_AT + 128 * (c + 1), :] = w2[:, 128 * c : 128 * (c + 1)]
    for k in range(3):
        rows = [ids[k : k + 1, c * CH : (c + 1) * CH] for c in range(CHUNKS)]
        at = ID_AT + 16 * k
        share[at : at + 16, :] = jnp.concatenate(rows, axis=0).astype(BF)
    edges = jnp.concatenate([ids[3:5, 0:CH], jnp.zeros((14, CH), F32)], axis=0)
    share[EDGE_AT : EDGE_AT + 16, :] = edges.astype(BF)


def place_kernel(rank, dedup, place):
    order = rank[...]
    halves = []
    for g in range(4):
        part = order[:, g * 512 : (g + 1) * 512]
        halves += [(part >> 8).astype(F32), (part & 255).astype(F32)]
    halves = jnp.concatenate(halves + [jnp.zeros((8, 512), F32)], axis=0).astype(BF)

    def block(step, _):
        for u in range(4):
            at = pl.ds(pl.multiple_of(step * 4096 + u * 1024, 1024), 1024)
            row = dedup[0, :, at]
            got = dot_nn(halves, one_hot(row & 511, 512))
            high = row >> 9
            total = jnp.zeros((1, 1024), F32)
            for g in range(4):
                value = got[2 * g : 2 * g + 1] * 256.0 + got[2 * g + 1 : 2 * g + 2]
                total = total + jnp.where(high == g, value, 0.0)
            place[:, at] = total.astype(I32)
        return 0

    lax.fori_loop(0, EV_GRP // 4096, block, 0)


def share_prep(*args):
    return call(share_kernel, "share_prep", ((SHARE_ROWS, 128), BF), args)


def lookup_places(*args, after):
    return call(
        place_kernel, "lookup_places", ((1, EV_GRP), I32), args, flops=4_000_000_000, after=after
    )


def bottom_kernel(x, w1, b1, w2, b2, w3, b3, feats, hid1, hid2, slope1, slope2, slope3, bottom):
    x_cols = jnp.concatenate([x[0].astype(F32), jnp.ones((1, EV), F32), jnp.zeros((2, EV), F32)], axis=0)
    feats[...] = x_cols.astype(BF)
    v = dot_tn(w1[...], x[0]) + spread_bias(b1[...])
    slope1[...] = slope(v)
    h = silu(v).astype(BF)
    hid1[...] = h
    v = dot_tn(w2[...], h) + spread_bias(b2[...])
    slope2[...] = slope(v)
    h = silu(v).astype(BF)
    hid2[...] = h
    v = dot_nn(w3[...], h) + spread_bias(b3[...])
    slope3[...] = slope(v)
    bottom[...] = silu(v).astype(BF)


def bottom_forward(*args):
    outs = [
        ((16, EV), BF), ((512, EV), BF), ((256, EV), BF), ((512, EV), F32), ((256, EV), F32),
        ((64, EV), F32), ((64, EV), BF),
    ]
    return call(bottom_kernel, "bottom_forward", outs, args, flops=2_000_000_000)


def session_weights(lens):
    i, k = iota((32, 32), 0), iota((32, 32), 1)
    ends = jnp.sum(jnp.where(k <= i, lens, 0.0), axis=1, keepdims=True)
    own = jnp.sum(jnp.where(k == i, lens, 0.0), axis=1, keepdims=True)
    position = iota((1, EV), 1).astype(F32)
    inside = (position >= ends - own) & (position < ends)
    return jnp.sum(jnp.where(inside, 1.0 / own, 0.0), axis=0, keepdims=True)


def event_kernel(
    arrived_far, bottom, share0, share1, share2, share3, w3, w4, b2, b3, b4, labels, lens,
    d_pooled_far, top_in_far, hid1_far, hid2_far, hid3_far, d_act1_far, d_act2_far, d_act3_far,
    d_bottom, scalars,
    d_pooled, top_in, hid1, hid2, hid3, d_act1, d_act2, d_act3,
    arrived, feats, w1, w2, d_top, pair_grads, sems, out_sems,
):
    d_pooled[TABLES:] = jnp.zeros((SLOTS - TABLES, EMB, EV), BF)

    def put_tables(first, count, sem):
        at = pl.ds(first, count)
        return pltpu.make_async_copy(d_pooled.at[at], d_pooled_far.at[at], out_sems.at[sem])

    put_tables(TABLES, SLOTS - TABLES, 0).start()
    get_vectors = pltpu.make_async_copy(arrived_far.at[0:TABLES], arrived, sems.at[0])
    get_vectors.start()
    me = lax.axis_index("mp")
    get_weights = []
    for k, share in enumerate((share0, share1, share2, share3)):
        at = pl.ds(pl.multiple_of(lax.rem(me + 4 - k, 4) * 128, 128), 128)
        parts = [(share.at[0:W1_ROWS, :], w1.at[:, at])]
        for c in range(4):
            rows = slice(W2_AT + 128 * c, W2_AT + 128 * (c + 1))
            parts.append((share.at[rows, :], w2.at[at, 128 * c : 128 * (c + 1)]))
        for source, target in parts:
            copy = pltpu.make_async_copy(source, target, sems.at[1 + len(get_weights)])
            copy.start()
            get_weights.append(copy)
    get_vectors.wait()
    feats[0] = bottom[...].astype(F32)

    def widen(t, _):
        feats[t + 1] = arrived[t].astype(F32)
        return 0

    lax.fori_loop(0, TABLES, widen, 0)

    top_in[0:EMB, :] = bottom[...]

    def gram_half(half, _):
        at = pl.ds(pl.multiple_of(half * 128, 128), 128)
        parts, row, held = [], EMB, []
        for a, c in PAIRS:
            prod = feats[a, :, at] * feats[c, :, at]
            part = prod[0:8]
            for k in range(1, 8):
                part = part + prod[8 * k : 8 * k + 8]
            parts.append(part)
            if (a, c) == PAIRS[-1]:
                parts.append(jnp.full((8, 128), 0.125, F32))
            if len(parts) == 8:
                held.append(sum_rows_of_eight(parts))
                parts = []
                if len(held) == 2:
                    top_in[row : row + 16, at] = jnp.concatenate(held, axis=0).astype(BF)
                    row += 16
                    held = []
        return 0

    lax.fori_loop(0, 2, gram_half, 0)
    for copy in get_weights:
        copy.wait()

    act1 = dot_tn(w1[...], top_in[...])
    h = silu(act1).astype(BF)
    hid1[...] = h
    act2 = dot_tn(w2[...], h) + spread_bias(b2[...])
    h = silu(act2).astype(BF)
    hid2[...] = h
    act3 = dot_tn(w3[...], h) + spread_bias(b3[...])
    h = silu(act3).astype(BF)
    hid3[...] = h
    logit = dot_nn(w4[...], h) + b4[...].astype(F32)

    weight = session_weights(lens[0].astype(F32)) * (1.0 / 4096.0)
    target = labels[...].astype(F32)
    entropy = jnp.maximum(logit, 0.0) + jnp.log1p(jnp.exp(-jnp.abs(logit))) - target * logit
    d_logit = (jax.nn.sigmoid(logit) - target) * weight
    scalars[...] = jnp.concatenate(
        [d_logit, weight * entropy, jnp.zeros((6, EV), F32)], axis=0
    )

    d = (dot_tn(w4[...], jnp.ones((1, EV), BF)) * d_logit * slope(act3)).astype(BF)
    d_act3[...] = d
    d = (dot_nn(w3[...], d) * slope(act2)).astype(BF)
    d_act2[...] = d
    d = (dot_nn(w2[...], d) * slope(act1)).astype(BF)
    d_act1[...] = d
    puts = [
        pltpu.make_async_copy(near, far, out_sems.at[2 + k])
        for k, (near, far) in enumerate((
            (top_in, top_in_far), (hid1, hid1_far), (hid2, hid2_far), (hid3, hid3_far),
            (d_act1, d_act1_far), (d_act2, d_act2_far), (d_act3, d_act3_far),
        ))
    ]
    for put in puts:
        put.start()
    d_top[...] = dot_nn(w1[...], d)

    at = EMB
    for a in range(TABLES):
        count = TABLES - a
        block = d_top[at : at + count, :]
        for half in range(2):
            part = block[:, 128 * half : 128 * half + 128]
            pair_grads[half, a * 33 + a + 1 : a * 33 + a + 1 + count, :] = part
            pair_grads[half, pl.ds((a + 1) * 33 + a, count, stride=33), :] = part
        at += count
    for a in range(TABLES + 1):
        for half in range(2):
            pair_grads[half, a * 33 + a : a * 33 + a + 1, :] = jnp.zeros((1, 128), F32)

    def vector_grads(places, half, lanes):
        grads = [pair_grads[half, pl.ds(a * 33, 32), :] for a in places]
        vector = feats[0, :, lanes]
        totals = [grad[0:1] * vector for grad in grads]
        for c in range(1, TABLES + 1):
            vector = feats[c, :, lanes]
            totals = [total + grad[c : c + 1] * vector for total, grad in zip(totals, grads)]
        return totals

    halves = [(half, slice(128 * half, 128 * half + 128)) for half in range(2)]

    def table_grads(step, _):
        for half, lanes in halves:
            for i, total in enumerate(vector_grads([4 * step + i for i in range(1, 5)], half, lanes)):
                d_pooled[4 * step + i, :, lanes] = total.astype(BF)
        put_tables(4 * step, 4, 9 + step).start()
        return 0

    lax.fori_loop(0, TABLES // 4, table_grads, 0)
    for half, lanes in halves:
        rest = vector_grads([0, TABLES - 1, TABLES], half, lanes)
        d_bottom[:, lanes] = d_top[0:EMB, lanes] + rest[0]
        d_pooled[TABLES - 2, :, lanes] = rest[1].astype(BF)
        d_pooled[TABLES - 1, :, lanes] = rest[2].astype(BF)
    put_tables(TABLES - 2, 2, 1).start()
    for put in puts:
        put.wait()
    put_tables(TABLES, SLOTS - TABLES, 0).wait()
    put_tables(TABLES - 2, 2, 1).wait()
    for step in range(TABLES // 4):
        put_tables(4 * step, 4, 9 + step).wait()


def event_step(*args, after):
    outs = [
        ((SLOTS, EMB, EV), BF), ((W1_ROWS, EV), BF), ((512, EV), BF), ((512, EV), BF), ((256, EV), BF),
        ((512, EV), BF), ((512, EV), BF), ((256, EV), BF), ((EMB, EV), F32), ((8, EV), F32),
    ]
    scratch = [pltpu.VMEM(*out) for out in outs[:8]]
    scratch += [
        pltpu.VMEM((TABLES, EMB, EV), BF),
        pltpu.VMEM((TABLES + 1, EMB, EV), F32),
        pltpu.VMEM((W1_ROWS, 512), BF),
        pltpu.VMEM((512, 512), BF),
        pltpu.VMEM((W1_ROWS, EV), F32),
        pltpu.VMEM((2, (TABLES + 1) * 33, 128), F32),
        pltpu.SemaphoreType.DMA((21,)),
        pltpu.SemaphoreType.DMA((9 + TABLES // 4,)),
    ]
    return call(
        event_kernel, "event_step", outs, args, scratch, flops=10_000_000_000, after=after,
        near=(0, 2, 3, 4, 5), out_left=tuple(range(8)),
    )


def weight_grad_kernel(
    feats, hb1, hb2, slope1, slope2, slope3, bw2, bw3, d_bottom,
    top_in, hid1, hid2, hid3, d_act1, d_act2, d_act3, scalars, keep, send, out,
):
    def blocks(grad, half, at, count):
        for m in range(4):
            for c in range(count):
                out[half, m, at + 128 * c : at + 128 * (c + 1), :] = grad[
                    128 * m : 128 * (m + 1), 128 * c : 128 * (c + 1)
                ]

    ones = jnp.ones((16, EV), BF)
    g = dot_nt(top_in[...], d_act1[...]).astype(BF)
    for m in range(4):
        out[0, m, 0:W1_ROWS, :] = g[:, 128 * m : 128 * (m + 1)]
    blocks(dot_nt(hid1[...], d_act2[...]).astype(BF), 1, 0, 4)
    blocks(dot_nt(hid2[...], d_act3[...]).astype(BF), 1, COPY1, 2)

    d3 = (d_bottom[...] * slope3[...]).astype(BF)
    d2 = (dot_tn(bw3[...], d3) * slope2[...]).astype(BF)
    d1 = (dot_nn(bw2[...], d2) * slope1[...]).astype(BF)
    blocks(dot_nt(hb1[...], d2).astype(BF), 0, COPY0, 2)
    at = COPY0 + 256
    g = dot_nt(d3, hb2[...]).astype(BF)
    for m in range(4):
        column = 128 * (m // 2)
        out[0, m, at : at + 64, :] = g[:, column : column + 128]
    at += 64
    g = dot_nt(feats[...], d1).astype(BF)
    for m in range(2):
        for c in range(2):
            out[0, m, at + 16 * c : at + 16 * (c + 1), :] = g[
                :, 128 * (2 * m + c) : 128 * (2 * m + c + 1)
            ]

    d_logit = scalars[0:1, :]
    coarse = d_logit.astype(BF)
    fine = (d_logit - coarse.astype(F32)).astype(BF)
    sub = iota((16, EV), 0)
    both = jnp.where(sub == 0, coarse.astype(F32), jnp.where(sub == 1, fine.astype(F32), 0.0))
    g4 = dot_nt(both.astype(BF), hid3[...])
    g4 = g4[0:1] + g4[1:2]
    s2 = dot_nt(ones, d_act2[...])[0:1]
    s3 = dot_nt(ones, d_act3[...])[0:1]
    sb2 = dot_nt(ones, d2)[0:1]
    sb3 = dot_nt(ones, d3)[0:1]
    rows = [s2[:, 128 * c : 128 * (c + 1)] for c in range(4)]
    rows += [s3[:, 0:128], s3[:, 128:], g4[:, 0:128], g4[:, 128:], sb2[:, 0:128], sb2[:, 128:]]
    rows.append(jnp.concatenate([sb3, jnp.zeros((1, 64), F32)], axis=1))
    lane = iota((1, 128), 1)
    tail = jnp.zeros((1, 128), F32)
    for k in range(2):
        value = jnp.sum(scalars[k : k + 1, :], axis=1, keepdims=True)
        high = value.astype(BF).astype(F32)
        tail = jnp.where(lane == 2 * k, high, tail)
        tail = jnp.where(lane == 2 * k + 1, value - high, tail)
    rows.append(tail)
    rows.append(jnp.zeros((4, 128), F32))
    empty = jnp.zeros((16, 128), BF)
    out[0, 2, at : at + 16, :] = jnp.concatenate(rows, axis=0).astype(BF)
    out[0, 2, at + 16 : at + 32, :] = empty
    out[0, 3, at : at + 16, :] = empty
    out[0, 3, at + 16 : at + 32, :] = empty

    core = lax.axis_index("core")
    for m in range(4):
        keep[m] = out[core, m]
        send[m] = out[1 - core, m]


def weight_grads(*args, after):
    shape = (4, HALF_ROWS, 128)
    return call(
        weight_grad_kernel, "weight_grads", [(shape, BF), (shape, BF)], args,
        [pltpu.VMEM((2,) + shape, BF)], flops=6_000_000_000, after=after,
    )


def pair_kernel(keep, got, out):
    for m in range(4):
        out[m] = (keep[m].astype(F32) + got[m].astype(F32)).astype(BF)

    @pl.when(lax.axis_index("core") == 0)
    def _():
        rows = slice(COPY0 + 320, COPY0 + 336)
        total = keep[2, rows, :].astype(F32) + got[2, rows, :].astype(F32)
        sub, lane = iota((16, 128), 0), iota((16, 128), 1)
        fixed = total
        for k in range(2):
            here = (sub == TAIL) & ((lane >> 1) == k)
            value = jnp.sum(jnp.where(here, total, 0.0))
            high = value.astype(BF).astype(F32)
            fixed = jnp.where(here, jnp.where(lane == 2 * k, high, value - high), fixed)
        out[2, rows, :] = fixed.astype(BF)


def sum_pair(keep, got):
    return call(pair_kernel, "sum_pair", (keep.shape, BF), [keep, got])


def sum_kernel(parts, out):
    def step(k, total):
        for i in range(8):
            total = total + parts[k * 8 + i].astype(F32)
        return total

    total = lax.fori_loop(0, parts.shape[0] // 8, step, jnp.zeros(parts.shape[1:], F32)).astype(BF)

    def put(k, _):
        for i in range(8):
            out[k * 8 + i] = total
        return 0

    lax.fori_loop(0, out.shape[0] // 8, put, 0)


def sum_parts(parts, copies, after):
    return call(sum_kernel, "sum_parts", ((copies,) + parts.shape[1:], BF), [parts], after=after)


def unpack_kernel(
    own, other, n0, n1, n2, n3,
    tw1, tb1, tw2, bw1, bb1, bw2, bb2, bw3, bb3, tb2, tw3, tb3, tw4, tb4, loss, core_first, core_last,
    halves, sems,
):
    core = lax.axis_index("core")
    copies = [
        pltpu.make_async_copy(own, halves.at[core], sems.at[0]),
        pltpu.make_async_copy(other, halves.at[1 - core], sems.at[1]),
    ]
    for copy in copies:
        copy.start()
    total = (n0[...].astype(F32) + n1[...].astype(F32)) + (n2[...].astype(F32) + n3[...].astype(F32))
    core_first[0] = total[0:R1]
    core_last[:, 0, :] = total[256 : 256 + R3]
    for copy in copies:
        copy.wait()

    me = lax.axis_index("mp")
    tw1[...] = halves[0, me, 0:415, :].astype(F32)
    tb1[...] = halves[0, me, 400:416, :].astype(F32)[15:16]
    for c in range(4):
        tw2[:, 128 * c : 128 * (c + 1)] = halves[1, me, 128 * c : 128 * (c + 1), :].astype(F32)
    for m in range(4):
        for c in range(2):
            at = slice(128 * m, 128 * (m + 1)), slice(128 * c, 128 * (c + 1))
            bw2[at] = halves[0, m, COPY0 + 128 * c : COPY0 + 128 * (c + 1), :].astype(F32)
            tw3[at] = halves[1, m, COPY1 + 128 * c : COPY1 + 128 * (c + 1), :].astype(F32)
    for m in range(2):
        bw3[:, 128 * m : 128 * (m + 1)] = halves[0, 2 * m, COPY0 + 256 : COPY0 + 320, :].astype(F32)
        for c in range(2):
            at = COPY0 + 320 + 16 * c
            part = halves[0, m, at : at + 16, :].astype(F32)
            lanes = slice(128 * (2 * m + c), 128 * (2 * m + c + 1))
            bw1[:, lanes] = part[0:13]
            bb1[:, lanes] = part[13:14]
    small = halves[0, 2, COPY0 + 320 : COPY0 + 336, :].astype(F32)
    for c in range(4):
        tb2[:, 128 * c : 128 * (c + 1)] = small[c : c + 1]
    for c in range(2):
        lanes = slice(128 * c, 128 * (c + 1))
        tb3[:, lanes] = small[4 + c : 5 + c]
        tw4[:, lanes] = small[6 + c : 7 + c]
        bb2[:, lanes] = small[8 + c : 9 + c]
    bb3[...] = small[10:11, 0:64]
    pick = small[11:12]
    half = iota((1, 128), 1) >> 1
    tb4[...] = jnp.sum(jnp.where(half == 0, pick, 0.0), axis=1, keepdims=True)
    loss[...] = jnp.sum(jnp.where(half == 1, pick, 0.0), axis=1, keepdims=True)


def unpack(args, after):
    shapes = [
        (415, 128), (1, 128), (128, 512), (13, 512), (1, 512), (512, 256), (1, 256), (64, 256), (1, 64),
        (1, 512), (512, 256), (1, 256), (1, 256), (1, 1), (1, 1), (1, R1, 128), (R3, 1, 128),
    ]
    scratch = [pltpu.VMEM((2, 4, HALF_ROWS, 128), BF), pltpu.SemaphoreType.DMA((2,))]
    return call(
        unpack_kernel, "unpack", [(s, F32) for s in shapes], args, scratch, after=after, near=(0, 1)
    )


def scatter_kernel(returned, place, out, acc):
    acc[...] = jnp.zeros((256, 512), F32)

    def block(k, _):
        row = place[:, pl.ds(pl.multiple_of(k * 4096, 4096), 4096)]
        grads = jnp.concatenate([returned[16 * k + i] for i in range(16)], axis=1).astype(F32)
        high = row >> 9
        spread = [jnp.where(high == g, grads, 0.0).astype(BF) for g in range(4)]
        acc[...] += dot_nt(jnp.concatenate(spread, axis=0), one_hot(row & 511, 512))
        return 0

    lax.fori_loop(0, EV_GRP // 4096, block, 0)
    for g in range(4):
        out[:, 512 * g : 512 * (g + 1)] = acc[EMB * g : EMB * (g + 1), :].astype(BF)


def scatter_grads(*args, after):
    return call(
        scatter_kernel, "scatter_grads", ((EMB, UNIQ), BF), args, [pltpu.VMEM((256, 512), F32)],
        flops=4_000_000_000, after=after,
    )


def inner_grad(row_grads, last):
    columns = []
    for a in range(4):
        blocks = []
        for s2 in range(4):
            total = None
            for t in range(4):
                k = a * 16 + s2 * 4 + t
                term = row_grads[k : k + 1] * last[t * RANK : (t + 1) * RANK]
                total = term if total is None else total + term
            blocks.append(total)
        columns.append(jnp.concatenate(blocks, axis=0))
    return jnp.concatenate(columns, axis=1).astype(BF)


def swap_last(rows):
    i, k = iota((128, 128), 0), iota((128, 128), 1)
    return dot_nn(rows, ((i % 4) * RANK + i // 4 == k).astype(F32).astype(BF)).astype(BF)


def core_rows_kernel(s0, s1, s2, s3, cf, cl, first, last, middle, edges, pad, lasts):
    pad[...] = jnp.zeros((256, 128), BF)
    pad[0:R3, :] = cl[0]
    lasts[...] = swap_last(pad[...])
    pad[...] = jnp.zeros((256, 128), BF)
    pad[0:R1, :] = cf[0]
    for g, share in enumerate((s0, s1, s2, s3)):
        factors = []
        for k in (0, 2):
            block = share[ID_AT + 16 * k : ID_AT + 16 * (k + 1), :].astype(F32)
            row = jnp.concatenate([block[c : c + 1] for c in range(CHUNKS)], axis=1)
            factors.append(row.astype(I32))
        first[g] = dot_tn(pad[...], one_hot(factors[0], 256)).astype(BF)
        last[g] = dot_tn(lasts[...], one_hot(factors[1], 256)).astype(BF)
        middle[g] = share[ID_AT + 16 : ID_AT + 32, :].astype(F32)
        edges[8 * g : 8 * (g + 1), :] = share[EDGE_AT : EDGE_AT + 16, :].astype(F32)[0:8].astype(I32)


def core_rows(*args, after):
    outs = [
        ((4, 128, UNIQ), BF), ((4, 128, UNIQ), BF), ((4, CHUNKS, CH), F32), ((32, 128), I32),
    ]
    scratch = [pltpu.VMEM((256, 128), BF), pltpu.VMEM((256, 128), BF)]
    return call(
        core_rows_kernel, "core_rows", outs, args, scratch, flops=6_000_000_000, after=after
    )


def own_kernel(
    row_grads, inner_far, ids, bounds, mid_far, lasts_far, out,
    inner, mid, last_s, d_last, d_first, d_halves, acc, hot_first, hot_last, sems,
):
    copies = [
        pltpu.make_async_copy(lasts_far.at[0], last_s, sems.at[0]),
        pltpu.make_async_copy(mid_far, mid, sems.at[1]),
    ]

    def get_inner(step):
        at = pl.ds(step * UNROLL, UNROLL)
        return pltpu.make_async_copy(inner_far.at[at], inner.at[at], sems.at[2 + step])

    for copy in copies:
        copy.start()
    for step in range(CHUNKS // UNROLL):
        get_inner(step).start()
    hot_first[...] = one_hot(ids[0:1, :].astype(I32), 256)
    hot_last[...] = one_hot(ids[2:3, :].astype(I32), 256)
    for copy in copies:
        copy.wait()

    def first_grad(c, h, low, d_half):
        at = pl.ds(pl.multiple_of(c * CH, CH), CH)
        q_here = jnp.concatenate([ids[1:2, at].astype(I32)[:, h * HALF : (h + 1) * HALF]] * 4, axis=1)
        hit = window_hits(q_here, low, HWIN)
        product = dot_nn(mid[window_rows(low, HWIN), :], d_half)
        total = jnp.where(hit[0:1], product[0:RANK], 0.0)
        for q in range(1, HWIN):
            total = total + jnp.where(hit[q : q + 1], product[q * RANK : (q + 1) * RANK], 0.0)
        return total

    def chunks(step, _):
        for u in range(UNROLL):
            c = step * UNROLL + u
            at = pl.ds(pl.multiple_of(c * CH, CH), CH)
            grads = row_grads[:, at].astype(F32)
            d_inner = inner_grad(grads, last_s[:, at].astype(F32))
            for h in range(2):
                d_half = half_lanes(d_inner, h)
                d_halves[2 * u + h] = d_half
                acc[2 * u + h] = first_grad(c, h, bounds[0, 2 * c + h], d_half)
        get_inner(step).wait()
        for u in range(UNROLL):
            c = step * UNROLL + u
            at = pl.ds(pl.multiple_of(c * CH, CH), CH)
            grads = row_grads[:, at].astype(F32)
            wide = inner[c].astype(F32)
            for t in range(4):
                total = None
                for a in range(4):
                    for s2 in range(4):
                        k = a * 16 + s2 * 4 + t
                        term = grads[k : k + 1] * wide[
                            s2 * RANK : (s2 + 1) * RANK, a * CH : (a + 1) * CH
                        ]
                        total = term if total is None else total + term
                d_last[t * RANK : (t + 1) * RANK, at] = total.astype(BF)
        lows = [bounds[0, step * 2 * UNROLL + i] for i in range(2 * UNROLL)]
        spans = [bounds[1, step * 2 * UNROLL + i] - lows[i] for i in range(2 * UNROLL)]

        @pl.when(functools.reduce(jnp.maximum, spans) >= HWIN)
        def _():
            for i in range(2 * UNROLL):

                def more(j, _):
                    low = lows[i] + j * HWIN
                    acc[i] += first_grad(step * UNROLL + i // 2, i % 2, low, d_halves[i])
                    return 0

                lax.fori_loop(1, spans[i] // HWIN + 1, more, 0)

        for u in range(UNROLL):
            c = step * UNROLL + u
            at = pl.ds(pl.multiple_of(c * CH, CH), CH)
            both = [acc[2 * u], acc[2 * u + 1]]
            for a in range(4):
                d_first[a * RANK : (a + 1) * RANK, at] = jnp.concatenate(
                    [part[:, a * HALF : (a + 1) * HALF] for part in both], axis=1
                ).astype(BF)
        return 0

    lax.fori_loop(0, CHUNKS // UNROLL, chunks, 0)
    g_first = dot_nt(hot_first[...], d_first[...]).astype(BF)
    g_last = dot_nt(hot_last[...], d_last[...]).astype(BF)
    i, k = iota((128, 128), 0), iota((128, 128), 1)
    back = ((k % 4) * RANK + k // 4 == i).astype(F32).astype(BF)
    g_last = dot_nn(g_last, back).astype(BF)
    out[0:256, :] = g_first
    out[256:512, :] = g_last


def own_core_grads(*args):
    scratch = [
        pltpu.VMEM((CHUNKS, 128, 512), BF),
        pltpu.VMEM((R2 * RANK, 128), BF),
        pltpu.VMEM((128, UNIQ), BF),
        pltpu.VMEM((128, UNIQ), BF),
        pltpu.VMEM((128, UNIQ), BF),
        pltpu.VMEM((2 * UNROLL, 128, 256), BF),
        pltpu.VMEM((2 * UNROLL, RANK, 256), F32),
        pltpu.VMEM((256, UNIQ), BF),
        pltpu.VMEM((256, UNIQ), BF),
        pltpu.SemaphoreType.DMA((2 + CHUNKS // UNROLL,)),
    ]
    return call(
        own_kernel, "own_core_grads", ((512, 128), BF), args, scratch, flops=10_000_000_000, smem=(3,),
        left=(1, 4, 5),
    )


def mid_grad_kernel(
    g0, g1, g2, g3, firsts_far, lasts_far, middle, edges, out_far,
    out, grads, firsts, lasts, d_halves, sems,
):
    copies = []
    for g, far in enumerate((g0, g1, g2, g3)):
        pairs = ((far, grads), (firsts_far.at[g], firsts), (lasts_far.at[g], lasts))
        copies.append([
            pltpu.make_async_copy(source, target.at[g], sems.at[3 * g + k])
            for k, (source, target) in enumerate(pairs)
        ])
    for group in copies:
        for copy in group:
            copy.start()

    def clear(k, _):
        at = pl.ds(pl.multiple_of(k * 640, 640), 640)
        out[at, :] = jnp.zeros((640, 128), F32)
        return 0

    lax.fori_loop(0, R2 * RANK // 640, clear, 0)

    def put(k):
        at = pl.ds(k * (R2 // PARTS) * RANK, R2 // PARTS * RANK)
        return pltpu.make_async_copy(out.at[at, :], out_far.at[at, :], sems.at[12 + k])

    for g in range(4):
        for copy in copies[g]:
            copy.wait()

        def mid_grad(c, h, low, d_half):
            at = pl.ds(pl.multiple_of(c * CH, CH), CH)
            q_here = middle[g, pl.ds(c, 1), :].astype(I32)
            q_here = jnp.concatenate([q_here[:, h * HALF : (h + 1) * HALF]] * 4, axis=1)
            first = half_lanes(side_by_side(firsts[g, :, at]), h)
            return dot_nt(masked_block(first, q_here, low, HWIN), d_half)

        def chunks(step, _):
            products = []
            for u in range(UNROLL):
                c = step * UNROLL + u
                at = pl.ds(pl.multiple_of(c * CH, CH), CH)
                d_inner = inner_grad(grads[g, :, at].astype(F32), lasts[g, :, at].astype(F32))
                for h in range(2):
                    d_half = half_lanes(d_inner, h)
                    d_halves[2 * u + h] = d_half
                    low_q = edges[8 * g, 2 * c + h]
                    products.append((low_q, mid_grad(c, h, low_q, d_half)))
            for low_q, product in products:
                out[window_rows(low_q, HWIN), :] += product
            lows = [edges[8 * g, step * 2 * UNROLL + v] for v in range(2 * UNROLL)]
            spans = [edges[8 * g + 1, step * 2 * UNROLL + v] - lows[v] for v in range(2 * UNROLL)]

            @pl.when(functools.reduce(jnp.maximum, spans) >= HWIN)
            def _():
                for v in range(2 * UNROLL):

                    def more(j, _):
                        low = lows[v] + j * HWIN
                        out[window_rows(low, HWIN), :] += mid_grad(
                            step * UNROLL + v // 2, v % 2, low, d_halves[v]
                        )
                        return 0

                    lax.fori_loop(1, spans[v] // HWIN + 1, more, 0)

            if g == 3:
                after = jnp.minimum(step + 1, CHUNKS // UNROLL - 1)
                done = jnp.where(step == CHUNKS // UNROLL - 1, R2, edges[8 * g, after * 2 * UNROLL])
                for k in range(PARTS):

                    @pl.when((lows[0] < (k + 1) * R2 // PARTS) & (done >= (k + 1) * R2 // PARTS))
                    def _():
                        put(k).start()

            return 0

        if g == 3:
            for k in range(PARTS):

                @pl.when(edges[8 * g, 0] >= (k + 1) * R2 // PARTS)
                def _():
                    put(k).start()

        lax.fori_loop(0, CHUNKS // UNROLL, chunks, 0)

    for k in range(PARTS):
        put(k).wait()


def mid_core_grad(row_grads, rows, after):
    scratch = [
        pltpu.VMEM((R2 * RANK, 128), F32),
        pltpu.VMEM((4, EMB, UNIQ), BF),
        pltpu.VMEM((4, 128, UNIQ), BF),
        pltpu.VMEM((4, 128, UNIQ), BF),
        pltpu.VMEM((2 * UNROLL, 128, 256), BF),
        pltpu.SemaphoreType.DMA((12 + PARTS,)),
    ]
    return call(
        mid_grad_kernel, "mid_core_grad", ((R2 * RANK, 128), F32), [*row_grads, *rows], scratch,
        flops=40_000_000_000, after=after, smem=(7,), left=(4, 5), near=(0, 1, 2, 3), out_left=(0,),
    )


BATCH = ("xz", "core")


def exchange(value, axes=BATCH):
    return lax.all_to_all(value, axes, 0, 0, tiled=True)


def from_before(value, places):
    return lax.ppermute(value, "mp", [(i, (i + places) % 4) for i in range(4)])


def gather_mp(value):
    return [value] + [from_before(value, k) for k in (1, 2, 3)]


def from_other_core(value):
    return lax.ppermute(value, "core", [(0, 1), (1, 0)])


def body(
    dense_feats, labels, session_lengths, uniq_rows, dedup_map, core_first, core_mid, core_last,
    bot_w1, bot_b1, bot_w2, bot_b2, bot_w3, bot_b3,
    top_w1, top_b1, top_w2, top_b2, top_w3, top_b3, top_w4, top_b4,
):
    row = lambda v: v.reshape(1, -1)
    pooled, inner, ids, rank, mid, bounds = rebuild(
        uniq_rows.transpose(0, 2, 1, 3), dedup_map, core_first, core_mid, core_last
    )
    arrived = exchange(pooled)
    share = share_prep(top_w1, row(top_b1), top_w2, ids)
    shares = gather_mp(share)
    place = lookup_places(rank, dedup_map, after=[share])
    feats, hb1, hb2, slope1, slope2, slope3, bottom = bottom_forward(
        dense_feats.transpose(0, 2, 1), bot_w1, row(bot_b1), bot_w2, row(bot_b2), bot_w3.T, row(bot_b3)
    )
    d_pooled, top_in, hid1, hid2, hid3, d_act1, d_act2, d_act3, d_bottom, scalars = event_step(
        arrived, bottom, *shares, top_w3, top_w4.T, row(top_b2), row(top_b3), row(top_b4),
        labels, session_lengths, after=[place],
    )
    returned = exchange(d_pooled)
    rows = core_rows(*shares, core_first, core_last, after=[d_pooled])
    keep, send = weight_grads(
        feats, hb1, hb2, slope1, slope2, slope3, bot_w2, bot_w3.T, d_bottom,
        top_in, hid1, hid2, hid3, d_act1, d_act2, d_act3, scalars, after=[rows[0]],
    )
    grads = sum_pair(keep, from_other_core(send))
    parts = exchange(grads.reshape(64, HALF_ROWS // 16, 128), ("mp", "xz"))

    row_grads = scatter_grads(returned, place, after=[grads])
    one, three = from_before(row_grads, 1), from_before(row_grads, 3)
    all_rows = [row_grads, one, from_before(one, 1), three]
    own = own_core_grads(row_grads, inner, ids, bounds, mid, rows[1])
    small = gather_mp(own)
    summed = sum_parts(parts, 64, after=[own, all_rows[1], all_rows[3]])
    half = exchange(summed, ("mp", "xz")).reshape(4, HALF_ROWS, 128)
    grad_mid = mid_core_grad(all_rows, rows, after=[summed])
    half, grad_mid, *small = lax.optimization_barrier((half, grad_mid, *small))
    outs = unpack([half, from_other_core(half), *small], after=[grad_mid])
    tw1, tb1, tw2, bw1, bb1, bw2, bb2, bw3, bb3, tb2, tw3, tb3, tw4, tb4, loss, grad_first, grad_last = outs

    flat = lambda v: v.reshape(-1)
    return (
        loss[0, 0], grad_first, grad_mid.reshape(R2, 1, 4096).transpose(1, 0, 2),
        grad_last.transpose(1, 0, 2),
        bw1, flat(bb1), bw2, flat(bb2), bw3.T, flat(bb3),
        tw1, flat(tb1), tw2, flat(tb2), tw3, flat(tb3), tw4.T, flat(tb4),
    )


def solution(mesh):
    fine = jax.sharding.Mesh(mesh.devices.reshape(16, 2, 4), ("xz", "core", "mp"))
    split = (
        P("mp", BATCH, None), P("mp", BATCH), P("mp", BATCH, None),
        P(BATCH, "mp", None, None), P(BATCH, "mp", None),
        P(BATCH, None, None), P(BATCH, None, None), P(BATCH, None, None),
        P(), P(), P(), P(), P(), P(),
        P(None, "mp"), P("mp"), P("mp", None), P(), P(), P(), P(), P(),
    )
    out = (
        P(), P(BATCH, None, None), P(BATCH, None, None), P(BATCH, None, None),
        P(), P(), P(), P(), P(), P(),
        P(None, "mp"), P("mp"), P("mp", None), P(), P(), P(), P(), P(),
    )
    return jax.shard_map(body, mesh=fine, in_specs=split, out_specs=out, check_vma=False)
```

```python
import functools

import jax
import jax.numpy as jnp
from jax import lax
from jax.experimental import pallas as pl
from jax.experimental.pallas import tpu as pltpu
from jax.sharding import PartitionSpec as P

BF = jnp.bfloat16
F32 = jnp.float32
I32 = jnp.int32

R1, R2, R3 = 200, 220, 250
RANK = 32
EMB = 64
TABLES = 26
SLOTS = 32
UNIQ = 2048
EV_GRP = 8192
EV = 256
CH = 128
CHUNKS = UNIQ // CH
HALF = CH // 2
WIN = 16
HWIN = 10
PARTS = 4
UNROLL = 8
VMEM = pltpu.MemorySpace.VMEM
LIMITS = {
    "scatter_grads": 24, "sum_parts": 24, "unpack": 24, "core_rows": 24,
    "bottom_forward": 24, "lookup_places": 24, "share_prep": 24,
}


def iota(shape, dim):
    return lax.broadcasted_iota(I32, shape, dim)


def dot_nn(left, right):
    return lax.dot_general(left, right, (((1,), (0,)), ((), ())), preferred_element_type=F32)


def dot_nt(left, right):
    return lax.dot_general(left, right, (((1,), (1,)), ((), ())), preferred_element_type=F32)


def dot_tn(left, right):
    return lax.dot_general(left, right, (((0,), (0,)), ((), ())), preferred_element_type=F32)


def one_hot(row, count):
    return (iota((count, row.shape[1]), 0) == row).astype(F32).astype(BF)


def sum_rows_of_eight(parts):
    sub = iota(parts[0].shape, 0)
    step = 1
    while len(parts) > 1:
        keep = (sub & step) == 0
        merged = []
        for x, y in zip(parts[0::2], parts[1::2]):
            merged.append(jnp.where(keep, x, y) + pltpu.roll(jnp.where(keep, y, x), step, 0))
        parts = merged
        step *= 2
    return parts[0]


def pick_columns(table, row, groups):
    picked = dot_nn(table, one_hot(row & 511, 512))
    high = row >> 9
    total = jnp.where(high == 0, picked[0:EMB], 0.0)
    for g in range(1, groups):
        total = total + jnp.where(high == g, picked[g * EMB : (g + 1) * EMB], 0.0)
    return total


def window_start(low, count):
    return jnp.minimum(low, R2 - count)


def window_hits(q_row, low, count):
    hit = iota((count, q_row.shape[1]), 0) + window_start(low, count) == q_row
    return hit & (q_row >= low)


def masked_block(first, q_row, low, count):
    hit = window_hits(q_row, low, count).astype(F32)
    rows = []
    for q in range(count):
        flag = jnp.broadcast_to(hit[q : q + 1], (RANK, hit.shape[1])).astype(BF)
        rows.append(first * flag)
    return jnp.concatenate(rows, axis=0)


def window_rows(low, count):
    return pl.ds(pl.multiple_of(window_start(low, count) * RANK, RANK), count * RANK)


def side_by_side(block):
    return jnp.concatenate([block[a * RANK : (a + 1) * RANK] for a in range(4)], axis=1)


def half_lanes(block, h):
    pieces = [block[:, a * CH + h * HALF : a * CH + (h + 1) * HALF] for a in range(4)]
    return jnp.concatenate(pieces, axis=1)


def rebuild_kernel(
    uniq, dedup, cf, cm_far, cl, pooled, inner_far, ids, rank_out, mid_far, bounds,
    cm, midf, mid_out, inner, pad, first_s, last_s, rows_s, acc, table, bounds_s, sems,
):
    get_mid = pltpu.make_async_copy(cm_far, cm, sems.at[0])
    get_mid.start()

    q_row = uniq[0, 1]
    q_index = iota((224, 1), 0)
    start = jnp.sum((q_row < q_index).astype(F32), axis=1, keepdims=True)
    before = (iota((256, 256), 0) < iota((256, 256), 1)).astype(F32).astype(BF)
    running = start
    ranks = []
    for b in range(UNIQ // 256):
        hit = (q_index == q_row[:, b * 256 : (b + 1) * 256]).astype(F32)
        place = dot_nn(hit.astype(BF), before) + running
        ranks.append(jnp.sum(hit * place, axis=0, keepdims=True))
        running = running + jnp.sum(hit, axis=1, keepdims=True)
    rank = jnp.concatenate(ranks, axis=1).astype(I32)
    rank_out[...] = rank

    lane = iota((1, 128), 1).astype(F32) * HALF
    border = q_index > 0
    first_tile = jnp.sum((border & (start <= lane)).astype(F32), axis=0, keepdims=True)
    last_tile = jnp.sum((border & (start <= lane + (HALF - 1))).astype(F32), axis=0, keepdims=True)
    first_tile, last_tile = jnp.minimum(first_tile, R2 - 1), jnp.minimum(last_tile, R2 - 1)
    sub = iota((8, 128), 0)
    bounds[...] = jnp.where(sub == 0, first_tile, jnp.where(sub == 1, last_tile, 0.0)).astype(I32)
    copy = pltpu.make_async_copy(bounds, bounds_s, sems.at[1])
    copy.start()

    high, low = rank >> 8, rank & 255
    spread = []
    for k in range(3):
        row = uniq[0, k].astype(F32)
        spread.append(jnp.where(iota((8, UNIQ), 0) == high, row, 0.0))
    spread.append(jnp.zeros((8, UNIQ), F32))
    spread = jnp.concatenate(spread, axis=0).astype(BF)
    by_low = dot_nt(spread, one_hot(low, 256))
    sorted_rows = []
    for k in range(3):
        sorted_rows.append(
            jnp.concatenate([by_low[8 * k + h : 8 * k + h + 1] for h in range(8)], axis=1)
        )
    edge = bounds[...].astype(F32)
    blank = jnp.zeros((1, UNIQ - 128), F32)
    for k in range(2):
        sorted_rows.append(jnp.concatenate([edge[k : k + 1], blank], axis=1))
    ids[...] = jnp.concatenate(sorted_rows + [jnp.zeros((3, UNIQ), F32)], axis=0)

    pad[...] = jnp.zeros((256, 128), BF)
    pad[0:R1, :] = cf[0]
    first_s[...] = dot_tn(pad[...], one_hot(ids[0:1, :].astype(I32), 256)).astype(BF)
    pad[0:R3, :] = cl[0]
    i, k = iota((128, 128), 0), iota((128, 128), 1)
    swap = ((i % 4) * RANK + i // 4 == k).astype(F32).astype(BF)
    last_rows = dot_nn(pad[...], swap).astype(BF)
    last_s[...] = dot_tn(last_rows, one_hot(ids[2:3, :].astype(I32), 256))

    get_mid.wait()
    for r in range(RANK):
        midf[pl.ds(r, R2, stride=RANK + 1), :] = cm[0, :, r * 128 : (r + 1) * 128].astype(F32)

    def pack(k, _):
        for i in range(20):
            q = k * 20 + i
            rows = pl.ds(pl.multiple_of(q * RANK, RANK), RANK)
            mid_out[rows, :] = midf[pl.ds(q * (RANK + 1), RANK), :].astype(BF)
        return 0

    lax.fori_loop(0, R2 // 20, pack, 0)
    put_mid = pltpu.make_async_copy(mid_out, mid_far, sems.at[2])
    put_mid.start()
    copy.wait()

    def product(c, low):
        at = pl.ds(pl.multiple_of(c * CH, CH), CH)
        q_here = jnp.concatenate([ids[1:2, at].astype(I32)] * 4, axis=1)
        block = masked_block(side_by_side(first_s[:, at]), q_here, low, WIN)
        return dot_tn(mid_out[window_rows(low, WIN), :], block)

    def chunks(step, _):
        for u in range(UNROLL):
            c = step * UNROLL + u
            acc[u] = product(c, bounds_s[0, 2 * c])
        lows = [bounds_s[0, 2 * (step * UNROLL + u)] for u in range(UNROLL)]
        spans = [bounds_s[1, 2 * (step * UNROLL + u) + 1] - lows[u] for u in range(UNROLL)]

        @pl.when(functools.reduce(jnp.maximum, spans) >= WIN)
        def _():
            for u in range(UNROLL):

                def more(j, _):
                    acc[u] += product(step * UNROLL + u, lows[u] + j * WIN)
                    return 0

                lax.fori_loop(1, spans[u] // WIN + 1, more, 0)

        for u in range(UNROLL):
            c = step * UNROLL + u
            at = pl.ds(pl.multiple_of(c * CH, CH), CH)
            inner_c = acc[u].astype(BF)
            inner[c] = inner_c
            wide = inner_c.astype(F32)
            last = last_s[:, at]
            for a in range(4):
                for h in range(2):
                    parts = []
                    for s2 in (2 * h, 2 * h + 1):
                        left = wide[s2 * RANK : (s2 + 1) * RANK, a * CH : (a + 1) * CH]
                        for t in range(4):
                            prod = left * last[t * RANK : (t + 1) * RANK]
                            parts.append((prod[0:8] + prod[8:16]) + (prod[16:24] + prod[24:32]))
                    rows_s[a * 16 + h * 8 : a * 16 + h * 8 + 8, at] = sum_rows_of_eight(parts)
        return 0

    lax.fori_loop(0, CHUNKS // UNROLL, chunks, 0)
    put_inner = pltpu.make_async_copy(inner, inner_far, sems.at[3])
    put_inner.start()

    sorted_table = jnp.concatenate(
        [rows_s[:, g * 512 : (g + 1) * 512].astype(BF) for g in range(4)], axis=0
    )
    for g in range(4):
        table[g * EMB : (g + 1) * EMB, :] = pick_columns(
            sorted_table, rank[:, g * 512 : (g + 1) * 512], 4
        ).astype(BF)

    def pool(step, _):
        for u in range(8):
            k = step * 8 + u
            row = dedup[0, :, pl.ds(pl.multiple_of(k * 512, 512), 512)]
            out = pick_columns(table[...], row, 4).astype(BF)
            pooled[2 * k] = out[:, 0:EV]
            pooled[2 * k + 1] = out[:, EV:]
        return 0

    lax.fori_loop(0, EV_GRP // 4096, pool, 0)
    put_mid.wait()
    put_inner.wait()


def call(kernel, name, outs, args, scratch=(), flops=0, after=(), smem=(), left=(), near=(), out_left=()):
    args = list(args)
    if len(after):
        args[0] = lax.optimization_barrier((args[0], *after))[0]

    def spec(i, far, anywhere=()):
        space = pltpu.MemorySpace.HBM if i in far else pl.ANY if i in anywhere else VMEM
        return pl.BlockSpec(memory_space=space)

    specs = [
        pl.BlockSpec(memory_space=pltpu.MemorySpace.SMEM) if i in smem else spec(i, left, near)
        for i in range(len(args))
    ]
    many = isinstance(outs, list)
    shapes = tuple(jax.ShapeDtypeStruct(*o) for o in (outs if many else [outs]))
    size = sum(a.size * a.dtype.itemsize for a in args)
    size += sum(o.size * o.dtype.itemsize for o in shapes)
    out_specs = tuple(spec(i, out_left) for i in range(len(shapes)))
    return pl.pallas_call(
        kernel,
        out_shape=shapes if many else shapes[0],
        in_specs=specs,
        out_specs=out_specs if many else out_specs[0],
        scratch_shapes=list(scratch),
        compiler_params=pltpu.CompilerParams(vmem_limit_bytes=LIMITS.get(name, 58) * 2**20),
        cost_estimate=pl.CostEstimate(flops=flops, bytes_accessed=size, transcendentals=0),
        name=name,
    )(*args)


def rebuild(*args):
    return call(
        rebuild_kernel,
        "rebuild",
        [
            ((SLOTS, EMB, EV), BF),
            ((CHUNKS, 128, 512), BF),
            ((8, UNIQ), F32),
            ((1, UNIQ), I32),
            ((R2 * RANK, 128), BF),
            ((8, 128), I32),
        ],
        args,
        [
            pltpu.VMEM((1, R2, 4096), BF),
            pltpu.VMEM((R2 * (RANK + 1), 128), F32),
            pltpu.VMEM((R2 * RANK, 128), BF),
            pltpu.VMEM((CHUNKS, 128, 512), BF),
            pltpu.VMEM((256, 128), BF),
            pltpu.VMEM((128, UNIQ), BF),
            pltpu.VMEM((128, UNIQ), F32),
            pltpu.VMEM((EMB, UNIQ), F32),
            pltpu.VMEM((UNROLL, 128, 512), F32),
            pltpu.VMEM((256, 512), BF),
            pltpu.SMEM((8, 128), I32),
            pltpu.SemaphoreType.DMA((4,)),
        ],
        flops=20_000_000_000,
        left=(3,),
        out_left=(1, 4),
    )


W1_ROWS = 416
W2_AT, ID_AT = W1_ROWS, W1_ROWS + 512
EDGE_AT = ID_AT + 48
SHARE_ROWS = EDGE_AT + 16
HALF_ROWS = 768
TAIL = 11
COPY0, COPY1 = W1_ROWS, 512
PAIRS = [(a, c) for a in range(TABLES + 1) for c in range(a + 1, TABLES + 1)]


def silu(v):
    return v * jax.nn.sigmoid(v)


def slope(v):
    s = jax.nn.sigmoid(v)
    return s * (1.0 + v * (1.0 - s))


def spread_bias(row):
    return dot_tn(row, jnp.ones((1, EV), BF))


def share_kernel(w1, b1, w2, ids, share):
    share[0:W1_ROWS, :] = jnp.zeros((W1_ROWS, 128), BF)
    share[0:415, :] = w1[...]
    share[415:416, :] = b1[...]
    for c in range(4):
        share[W2_AT + 128 * c : W2_AT + 128 * (c + 1), :] = w2[:, 128 * c : 128 * (c + 1)]
    for k in range(3):
        rows = [ids[k : k + 1, c * CH : (c + 1) * CH] for c in range(CHUNKS)]
        at = ID_AT + 16 * k
        share[at : at + 16, :] = jnp.concatenate(rows, axis=0).astype(BF)
    edges = jnp.concatenate([ids[3:5, 0:CH], jnp.zeros((14, CH), F32)], axis=0)
    share[EDGE_AT : EDGE_AT + 16, :] = edges.astype(BF)


def place_kernel(rank, dedup, place):
    order = rank[...]
    halves = []
    for g in range(4):
        part = order[:, g * 512 : (g + 1) * 512]
        halves += [(part >> 8).astype(F32), (part & 255).astype(F32)]
    halves = jnp.concatenate(halves + [jnp.zeros((8, 512), F32)], axis=0).astype(BF)

    def block(step, _):
        for u in range(4):
            at = pl.ds(pl.multiple_of(step * 4096 + u * 1024, 1024), 1024)
            row = dedup[0, :, at]
            got = dot_nn(halves, one_hot(row & 511, 512))
            high = row >> 9
            total = jnp.zeros((1, 1024), F32)
            for g in range(4):
                value = got[2 * g : 2 * g + 1] * 256.0 + got[2 * g + 1 : 2 * g + 2]
                total = total + jnp.where(high == g, value, 0.0)
            place[:, at] = total.astype(I32)
        return 0

    lax.fori_loop(0, EV_GRP // 4096, block, 0)


def share_prep(*args):
    return call(share_kernel, "share_prep", ((SHARE_ROWS, 128), BF), args)


def lookup_places(*args, after):
    return call(
        place_kernel, "lookup_places", ((1, EV_GRP), I32), args, flops=4_000_000_000, after=after
    )


def bottom_kernel(x, w1, b1, w2, b2, w3, b3, feats, hid1, hid2, slope1, slope2, slope3, bottom):
    x_cols = jnp.concatenate([x[0].astype(F32), jnp.ones((1, EV), F32), jnp.zeros((2, EV), F32)], axis=0)
    feats[...] = x_cols.astype(BF)
    v = dot_tn(w1[...], x[0]) + spread_bias(b1[...])
    slope1[...] = slope(v)
    h = silu(v).astype(BF)
    hid1[...] = h
    v = dot_tn(w2[...], h) + spread_bias(b2[...])
    slope2[...] = slope(v)
    h = silu(v).astype(BF)
    hid2[...] = h
    v = dot_nn(w3[...], h) + spread_bias(b3[...])
    slope3[...] = slope(v)
    bottom[...] = silu(v).astype(BF)


def bottom_forward(*args):
    outs = [
        ((16, EV), BF), ((512, EV), BF), ((256, EV), BF), ((512, EV), F32), ((256, EV), F32),
        ((64, EV), F32), ((64, EV), BF),
    ]
    return call(bottom_kernel, "bottom_forward", outs, args, flops=2_000_000_000)


def session_weights(lens):
    i, k = iota((32, 32), 0), iota((32, 32), 1)
    ends = jnp.sum(jnp.where(k <= i, lens, 0.0), axis=1, keepdims=True)
    own = jnp.sum(jnp.where(k == i, lens, 0.0), axis=1, keepdims=True)
    position = iota((1, EV), 1).astype(F32)
    inside = (position >= ends - own) & (position < ends)
    return jnp.sum(jnp.where(inside, 1.0 / own, 0.0), axis=0, keepdims=True)


def event_kernel(
    arrived_far, bottom, share0, share1, share2, share3, w3, w4, b2, b3, b4, labels, lens,
    d_pooled_far, top_in_far, hid1_far, hid2_far, hid3_far, d_act1_far, d_act2_far, d_act3_far,
    d_bottom, scalars,
    d_pooled, top_in, hid1, hid2, hid3, d_act1, d_act2, d_act3,
    arrived, feats, w1, w2, d_top, pair_grads, sems, out_sems,
):
    d_pooled[TABLES:] = jnp.zeros((SLOTS - TABLES, EMB, EV), BF)

    def put_tables(first, count, sem):
        at = pl.ds(first, count)
        return pltpu.make_async_copy(d_pooled.at[at], d_pooled_far.at[at], out_sems.at[sem])

    put_tables(TABLES, SLOTS - TABLES, 0).start()
    get_vectors = pltpu.make_async_copy(arrived_far.at[0:TABLES], arrived, sems.at[0])
    get_vectors.start()
    me = lax.axis_index("mp")
    get_weights = []
    for k, share in enumerate((share0, share1, share2, share3)):
        at = pl.ds(pl.multiple_of(lax.rem(me + 4 - k, 4) * 128, 128), 128)
        parts = [(share.at[0:W1_ROWS, :], w1.at[:, at])]
        for c in range(4):
            rows = slice(W2_AT + 128 * c, W2_AT + 128 * (c + 1))
            parts.append((share.at[rows, :], w2.at[at, 128 * c : 128 * (c + 1)]))
        for source, target in parts:
            copy = pltpu.make_async_copy(source, target, sems.at[1 + len(get_weights)])
            copy.start()
            get_weights.append(copy)
    get_vectors.wait()
    feats[0] = bottom[...].astype(F32)

    def widen(t, _):
        feats[t + 1] = arrived[t].astype(F32)
        return 0

    lax.fori_loop(0, TABLES, widen, 0)

    top_in[0:EMB, :] = bottom[...]

    def gram_half(half, _):
        at = pl.ds(pl.multiple_of(half * 128, 128), 128)
        parts, row, held = [], EMB, []
        for a, c in PAIRS:
            prod = feats[a, :, at] * feats[c, :, at]
            part = prod[0:8]
            for k in range(1, 8):
                part = part + prod[8 * k : 8 * k + 8]
            parts.append(part)
            if (a, c) == PAIRS[-1]:
                parts.append(jnp.full((8, 128), 0.125, F32))
            if len(parts) == 8:
                held.append(sum_rows_of_eight(parts))
                parts = []
                if len(held) == 2:
                    top_in[row : row + 16, at] = jnp.concatenate(held, axis=0).astype(BF)
                    row += 16
                    held = []
        return 0

    lax.fori_loop(0, 2, gram_half, 0)
    for copy in get_weights:
        copy.wait()

    act1 = dot_tn(w1[...], top_in[...])
    h = silu(act1).astype(BF)
    hid1[...] = h
    act2 = dot_tn(w2[...], h) + spread_bias(b2[...])
    h = silu(act2).astype(BF)
    hid2[...] = h
    act3 = dot_tn(w3[...], h) + spread_bias(b3[...])
    h = silu(act3).astype(BF)
    hid3[...] = h
    logit = dot_nn(w4[...], h) + b4[...].astype(F32)

    weight = session_weights(lens[0].astype(F32)) * (1.0 / 4096.0)
    target = labels[...].astype(F32)
    entropy = jnp.maximum(logit, 0.0) + jnp.log1p(jnp.exp(-jnp.abs(logit))) - target * logit
    d_logit = (jax.nn.sigmoid(logit) - target) * weight
    scalars[...] = jnp.concatenate(
        [d_logit, weight * entropy, jnp.zeros((6, EV), F32)], axis=0
    )

    d = (dot_tn(w4[...], jnp.ones((1, EV), BF)) * d_logit * slope(act3)).astype(BF)
    d_act3[...] = d
    d = (dot_nn(w3[...], d) * slope(act2)).astype(BF)
    d_act2[...] = d
    d = (dot_nn(w2[...], d) * slope(act1)).astype(BF)
    d_act1[...] = d
    puts = [
        pltpu.make_async_copy(near, far, out_sems.at[2 + k])
        for k, (near, far) in enumerate((
            (top_in, top_in_far), (hid1, hid1_far), (hid2, hid2_far), (hid3, hid3_far),
            (d_act1, d_act1_far), (d_act2, d_act2_far), (d_act3, d_act3_far),
        ))
    ]
    for put in puts:
        put.start()
    d_top[...] = dot_nn(w1[...], d)

    at = EMB
    for a in range(TABLES):
        count = TABLES - a
        block = d_top[at : at + count, :]
        for half in range(2):
            part = block[:, 128 * half : 128 * half + 128]
            pair_grads[half, a * 33 + a + 1 : a * 33 + a + 1 + count, :] = part
            pair_grads[half, pl.ds((a + 1) * 33 + a, count, stride=33), :] = part
        at += count
    for a in range(TABLES + 1):
        for half in range(2):
            pair_grads[half, a * 33 + a : a * 33 + a + 1, :] = jnp.zeros((1, 128), F32)

    def vector_grads(places, half, lanes):
        grads = [pair_grads[half, pl.ds(a * 33, 32), :] for a in places]
        vector = feats[0, :, lanes]
        totals = [grad[0:1] * vector for grad in grads]
        for c in range(1, TABLES + 1):
            vector = feats[c, :, lanes]
            totals = [total + grad[c : c + 1] * vector for total, grad in zip(totals, grads)]
        return totals

    halves = [(half, slice(128 * half, 128 * half + 128)) for half in range(2)]

    def table_grads(step, _):
        for half, lanes in halves:
            for i, total in enumerate(vector_grads([4 * step + i for i in range(1, 5)], half, lanes)):
                d_pooled[4 * step + i, :, lanes] = total.astype(BF)
        put_tables(4 * step, 4, 9 + step).start()
        return 0

    lax.fori_loop(0, TABLES // 4, table_grads, 0)
    for half, lanes in halves:
        rest = vector_grads([0, TABLES - 1, TABLES], half, lanes)
        d_bottom[:, lanes] = d_top[0:EMB, lanes] + rest[0]
        d_pooled[TABLES - 2, :, lanes] = rest[1].astype(BF)
        d_pooled[TABLES - 1, :, lanes] = rest[2].astype(BF)
    put_tables(TABLES - 2, 2, 1).start()
    for put in puts:
        put.wait()
    put_tables(TABLES, SLOTS - TABLES, 0).wait()
    put_tables(TABLES - 2, 2, 1).wait()
    for step in range(TABLES // 4):
        put_tables(4 * step, 4, 9 + step).wait()


def event_step(*args, after):
    outs = [
        ((SLOTS, EMB, EV), BF), ((W1_ROWS, EV), BF), ((512, EV), BF), ((512, EV), BF), ((256, EV), BF),
        ((512, EV), BF), ((512, EV), BF), ((256, EV), BF), ((EMB, EV), F32), ((8, EV), F32),
    ]
    scratch = [pltpu.VMEM(*out) for out in outs[:8]]
    scratch += [
        pltpu.VMEM((TABLES, EMB, EV), BF),
        pltpu.VMEM((TABLES + 1, EMB, EV), F32),
        pltpu.VMEM((W1_ROWS, 512), BF),
        pltpu.VMEM((512, 512), BF),
        pltpu.VMEM((W1_ROWS, EV), F32),
        pltpu.VMEM((2, (TABLES + 1) * 33, 128), F32),
        pltpu.SemaphoreType.DMA((21,)),
        pltpu.SemaphoreType.DMA((9 + TABLES // 4,)),
    ]
    return call(
        event_kernel, "event_step", outs, args, scratch, flops=10_000_000_000, after=after,
        near=(0, 2, 3, 4, 5), out_left=tuple(range(8)),
    )


def weight_grad_kernel(
    feats, hb1, hb2, slope1, slope2, slope3, bw2, bw3, d_bottom,
    top_in, hid1, hid2, hid3, d_act1, d_act2, d_act3, scalars, keep, send, out,
):
    def blocks(grad, half, at, count):
        for m in range(4):
            for c in range(count):
                out[half, m, at + 128 * c : at + 128 * (c + 1), :] = grad[
                    128 * m : 128 * (m + 1), 128 * c : 128 * (c + 1)
                ]

    ones = jnp.ones((16, EV), BF)
    g = dot_nt(top_in[...], d_act1[...]).astype(BF)
    for m in range(4):
        out[0, m, 0:W1_ROWS, :] = g[:, 128 * m : 128 * (m + 1)]
    blocks(dot_nt(hid1[...], d_act2[...]).astype(BF), 1, 0, 4)
    blocks(dot_nt(hid2[...], d_act3[...]).astype(BF), 1, COPY1, 2)

    d3 = (d_bottom[...] * slope3[...]).astype(BF)
    d2 = (dot_tn(bw3[...], d3) * slope2[...]).astype(BF)
    d1 = (dot_nn(bw2[...], d2) * slope1[...]).astype(BF)
    blocks(dot_nt(hb1[...], d2).astype(BF), 0, COPY0, 2)
    at = COPY0 + 256
    g = dot_nt(d3, hb2[...]).astype(BF)
    for m in range(4):
        column = 128 * (m // 2)
        out[0, m, at : at + 64, :] = g[:, column : column + 128]
    at += 64
    g = dot_nt(feats[...], d1).astype(BF)
    for m in range(2):
        for c in range(2):
            out[0, m, at + 16 * c : at + 16 * (c + 1), :] = g[
                :, 128 * (2 * m + c) : 128 * (2 * m + c + 1)
            ]

    d_logit = scalars[0:1, :]
    coarse = d_logit.astype(BF)
    fine = (d_logit - coarse.astype(F32)).astype(BF)
    sub = iota((16, EV), 0)
    both = jnp.where(sub == 0, coarse.astype(F32), jnp.where(sub == 1, fine.astype(F32), 0.0))
    g4 = dot_nt(both.astype(BF), hid3[...])
    g4 = g4[0:1] + g4[1:2]
    s2 = dot_nt(ones, d_act2[...])[0:1]
    s3 = dot_nt(ones, d_act3[...])[0:1]
    sb2 = dot_nt(ones, d2)[0:1]
    sb3 = dot_nt(ones, d3)[0:1]
    rows = [s2[:, 128 * c : 128 * (c + 1)] for c in range(4)]
    rows += [s3[:, 0:128], s3[:, 128:], g4[:, 0:128], g4[:, 128:], sb2[:, 0:128], sb2[:, 128:]]
    rows.append(jnp.concatenate([sb3, jnp.zeros((1, 64), F32)], axis=1))
    lane = iota((1, 128), 1)
    tail = jnp.zeros((1, 128), F32)
    for k in range(2):
        value = jnp.sum(scalars[k : k + 1, :], axis=1, keepdims=True)
        high = value.astype(BF).astype(F32)
        tail = jnp.where(lane == 2 * k, high, tail)
        tail = jnp.where(lane == 2 * k + 1, value - high, tail)
    rows.append(tail)
    rows.append(jnp.zeros((4, 128), F32))
    empty = jnp.zeros((16, 128), BF)
    out[0, 2, at : at + 16, :] = jnp.concatenate(rows, axis=0).astype(BF)
    out[0, 2, at + 16 : at + 32, :] = empty
    out[0, 3, at : at + 16, :] = empty
    out[0, 3, at + 16 : at + 32, :] = empty

    core = lax.axis_index("core")
    for m in range(4):
        keep[m] = out[core, m]
        send[m] = out[1 - core, m]


def weight_grads(*args, after):
    shape = (4, HALF_ROWS, 128)
    return call(
        weight_grad_kernel, "weight_grads", [(shape, BF), (shape, BF)], args,
        [pltpu.VMEM((2,) + shape, BF)], flops=6_000_000_000, after=after,
    )


def pair_kernel(keep, got, out):
    for m in range(4):
        out[m] = (keep[m].astype(F32) + got[m].astype(F32)).astype(BF)

    @pl.when(lax.axis_index("core") == 0)
    def _():
        rows = slice(COPY0 + 320, COPY0 + 336)
        total = keep[2, rows, :].astype(F32) + got[2, rows, :].astype(F32)
        sub, lane = iota((16, 128), 0), iota((16, 128), 1)
        fixed = total
        for k in range(2):
            here = (sub == TAIL) & ((lane >> 1) == k)
            value = jnp.sum(jnp.where(here, total, 0.0))
            high = value.astype(BF).astype(F32)
            fixed = jnp.where(here, jnp.where(lane == 2 * k, high, value - high), fixed)
        out[2, rows, :] = fixed.astype(BF)


def sum_pair(keep, got):
    return call(pair_kernel, "sum_pair", (keep.shape, BF), [keep, got])


def sum_kernel(parts, out):
    def step(k, total):
        for i in range(8):
            total = total + parts[k * 8 + i].astype(F32)
        return total

    total = lax.fori_loop(0, parts.shape[0] // 8, step, jnp.zeros(parts.shape[1:], F32)).astype(BF)

    def put(k, _):
        for i in range(8):
            out[k * 8 + i] = total
        return 0

    lax.fori_loop(0, out.shape[0] // 8, put, 0)


def sum_parts(parts, copies, after):
    return call(sum_kernel, "sum_parts", ((copies,) + parts.shape[1:], BF), [parts], after=after)


def unpack_kernel(
    own, other, n0, n1, n2, n3,
    tw1, tb1, tw2, bw1, bb1, bw2, bb2, bw3, bb3, tb2, tw3, tb3, tw4, tb4, loss, core_first, core_last,
    halves, sems,
):
    core = lax.axis_index("core")
    copies = [
        pltpu.make_async_copy(own, halves.at[core], sems.at[0]),
        pltpu.make_async_copy(other, halves.at[1 - core], sems.at[1]),
    ]
    for copy in copies:
        copy.start()
    total = (n0[...].astype(F32) + n1[...].astype(F32)) + (n2[...].astype(F32) + n3[...].astype(F32))
    core_first[0] = total[0:R1]
    core_last[:, 0, :] = total[256 : 256 + R3]
    for copy in copies:
        copy.wait()

    me = lax.axis_index("mp")
    tw1[...] = halves[0, me, 0:415, :].astype(F32)
    tb1[...] = halves[0, me, 400:416, :].astype(F32)[15:16]
    for c in range(4):
        tw2[:, 128 * c : 128 * (c + 1)] = halves[1, me, 128 * c : 128 * (c + 1), :].astype(F32)
    for m in range(4):
        for c in range(2):
            at = slice(128 * m, 128 * (m + 1)), slice(128 * c, 128 * (c + 1))
            bw2[at] = halves[0, m, COPY0 + 128 * c : COPY0 + 128 * (c + 1), :].astype(F32)
            tw3[at] = halves[1, m, COPY1 + 128 * c : COPY1 + 128 * (c + 1), :].astype(F32)
    for m in range(2):
        bw3[:, 128 * m : 128 * (m + 1)] = halves[0, 2 * m, COPY0 + 256 : COPY0 + 320, :].astype(F32)
        for c in range(2):
            at = COPY0 + 320 + 16 * c
            part = halves[0, m, at : at + 16, :].astype(F32)
            lanes = slice(128 * (2 * m + c), 128 * (2 * m + c + 1))
            bw1[:, lanes] = part[0:13]
            bb1[:, lanes] = part[13:14]
    small = halves[0, 2, COPY0 + 320 : COPY0 + 336, :].astype(F32)
    for c in range(4):
        tb2[:, 128 * c : 128 * (c + 1)] = small[c : c + 1]
    for c in range(2):
        lanes = slice(128 * c, 128 * (c + 1))
        tb3[:, lanes] = small[4 + c : 5 + c]
        tw4[:, lanes] = small[6 + c : 7 + c]
        bb2[:, lanes] = small[8 + c : 9 + c]
    bb3[...] = small[10:11, 0:64]
    pick = small[11:12]
    half = iota((1, 128), 1) >> 1
    tb4[...] = jnp.sum(jnp.where(half == 0, pick, 0.0), axis=1, keepdims=True)
    loss[...] = jnp.sum(jnp.where(half == 1, pick, 0.0), axis=1, keepdims=True)


def unpack(args, after):
    shapes = [
        (415, 128), (1, 128), (128, 512), (13, 512), (1, 512), (512, 256), (1, 256), (64, 256), (1, 64),
        (1, 512), (512, 256), (1, 256), (1, 256), (1, 1), (1, 1), (1, R1, 128), (R3, 1, 128),
    ]
    scratch = [pltpu.VMEM((2, 4, HALF_ROWS, 128), BF), pltpu.SemaphoreType.DMA((2,))]
    return call(
        unpack_kernel, "unpack", [(s, F32) for s in shapes], args, scratch, after=after, near=(0, 1)
    )


def scatter_kernel(returned, place, out, acc):
    acc[...] = jnp.zeros((256, 512), F32)

    def block(k, _):
        row = place[:, pl.ds(pl.multiple_of(k * 4096, 4096), 4096)]
        grads = jnp.concatenate([returned[16 * k + i] for i in range(16)], axis=1).astype(F32)
        high = row >> 9
        spread = [jnp.where(high == g, grads, 0.0).astype(BF) for g in range(4)]
        acc[...] += dot_nt(jnp.concatenate(spread, axis=0), one_hot(row & 511, 512))
        return 0

    lax.fori_loop(0, EV_GRP // 4096, block, 0)
    for g in range(4):
        out[:, 512 * g : 512 * (g + 1)] = acc[EMB * g : EMB * (g + 1), :].astype(BF)


def scatter_grads(*args):
    return call(
        scatter_kernel, "scatter_grads", ((EMB, UNIQ), BF), args, [pltpu.VMEM((256, 512), F32)],
        flops=4_000_000_000,
    )


def inner_grad(row_grads, last):
    columns = []
    for a in range(4):
        blocks = []
        for s2 in range(4):
            total = None
            for t in range(4):
                k = a * 16 + s2 * 4 + t
                term = row_grads[k : k + 1] * last[t * RANK : (t + 1) * RANK]
                total = term if total is None else total + term
            blocks.append(total)
        columns.append(jnp.concatenate(blocks, axis=0))
    return jnp.concatenate(columns, axis=1).astype(BF)


def swap_last(rows):
    i, k = iota((128, 128), 0), iota((128, 128), 1)
    return dot_nn(rows, ((i % 4) * RANK + i // 4 == k).astype(F32).astype(BF)).astype(BF)


def core_rows_kernel(s0, s1, s2, s3, cf, cl, first, last, middle, edges, pad, lasts):
    pad[...] = jnp.zeros((256, 128), BF)
    pad[0:R3, :] = cl[0]
    lasts[...] = swap_last(pad[...])
    pad[...] = jnp.zeros((256, 128), BF)
    pad[0:R1, :] = cf[0]
    for g, share in enumerate((s0, s1, s2, s3)):
        factors = []
        for k in (0, 2):
            block = share[ID_AT + 16 * k : ID_AT + 16 * (k + 1), :].astype(F32)
            row = jnp.concatenate([block[c : c + 1] for c in range(CHUNKS)], axis=1)
            factors.append(row.astype(I32))
        first[g] = dot_tn(pad[...], one_hot(factors[0], 256)).astype(BF)
        last[g] = dot_tn(lasts[...], one_hot(factors[1], 256)).astype(BF)
        middle[g] = share[ID_AT + 16 : ID_AT + 32, :].astype(F32)
        edges[8 * g : 8 * (g + 1), :] = share[EDGE_AT : EDGE_AT + 16, :].astype(F32)[0:8].astype(I32)


def core_rows(*args, after):
    outs = [
        ((4, 128, UNIQ), BF), ((4, 128, UNIQ), BF), ((4, CHUNKS, CH), F32), ((32, 128), I32),
    ]
    scratch = [pltpu.VMEM((256, 128), BF), pltpu.VMEM((256, 128), BF)]
    return call(
        core_rows_kernel, "core_rows", outs, args, scratch, flops=6_000_000_000, after=after
    )


def own_kernel(
    row_grads, inner_far, ids, bounds, mid_far, lasts_far, out,
    inner, mid, last_s, d_last, d_first, d_halves, acc, hot_first, hot_last, sems,
):
    copies = [
        pltpu.make_async_copy(lasts_far.at[0], last_s, sems.at[0]),
        pltpu.make_async_copy(mid_far, mid, sems.at[1]),
    ]

    def get_inner(step):
        at = pl.ds(step * UNROLL, UNROLL)
        return pltpu.make_async_copy(inner_far.at[at], inner.at[at], sems.at[2 + step])

    for copy in copies:
        copy.start()
    for step in range(CHUNKS // UNROLL):
        get_inner(step).start()
    hot_first[...] = one_hot(ids[0:1, :].astype(I32), 256)
    hot_last[...] = one_hot(ids[2:3, :].astype(I32), 256)
    for copy in copies:
        copy.wait()

    def first_grad(c, h, low, d_half):
        at = pl.ds(pl.multiple_of(c * CH, CH), CH)
        q_here = jnp.concatenate([ids[1:2, at].astype(I32)[:, h * HALF : (h + 1) * HALF]] * 4, axis=1)
        hit = window_hits(q_here, low, HWIN)
        product = dot_nn(mid[window_rows(low, HWIN), :], d_half)
        total = jnp.where(hit[0:1], product[0:RANK], 0.0)
        for q in range(1, HWIN):
            total = total + jnp.where(hit[q : q + 1], product[q * RANK : (q + 1) * RANK], 0.0)
        return total

    def chunks(step, _):
        for u in range(UNROLL):
            c = step * UNROLL + u
            at = pl.ds(pl.multiple_of(c * CH, CH), CH)
            grads = row_grads[:, at].astype(F32)
            d_inner = inner_grad(grads, last_s[:, at].astype(F32))
            for h in range(2):
                d_half = half_lanes(d_inner, h)
                d_halves[2 * u + h] = d_half
                acc[2 * u + h] = first_grad(c, h, bounds[0, 2 * c + h], d_half)
        get_inner(step).wait()
        for u in range(UNROLL):
            c = step * UNROLL + u
            at = pl.ds(pl.multiple_of(c * CH, CH), CH)
            grads = row_grads[:, at].astype(F32)
            wide = inner[c].astype(F32)
            for t in range(4):
                total = None
                for a in range(4):
                    for s2 in range(4):
                        k = a * 16 + s2 * 4 + t
                        term = grads[k : k + 1] * wide[
                            s2 * RANK : (s2 + 1) * RANK, a * CH : (a + 1) * CH
                        ]
                        total = term if total is None else total + term
                d_last[t * RANK : (t + 1) * RANK, at] = total.astype(BF)
        lows = [bounds[0, step * 2 * UNROLL + i] for i in range(2 * UNROLL)]
        spans = [bounds[1, step * 2 * UNROLL + i] - lows[i] for i in range(2 * UNROLL)]

        @pl.when(functools.reduce(jnp.maximum, spans) >= HWIN)
        def _():
            for i in range(2 * UNROLL):

                def more(j, _):
                    low = lows[i] + j * HWIN
                    acc[i] += first_grad(step * UNROLL + i // 2, i % 2, low, d_halves[i])
                    return 0

                lax.fori_loop(1, spans[i] // HWIN + 1, more, 0)

        for u in range(UNROLL):
            c = step * UNROLL + u
            at = pl.ds(pl.multiple_of(c * CH, CH), CH)
            both = [acc[2 * u], acc[2 * u + 1]]
            for a in range(4):
                d_first[a * RANK : (a + 1) * RANK, at] = jnp.concatenate(
                    [part[:, a * HALF : (a + 1) * HALF] for part in both], axis=1
                ).astype(BF)
        return 0

    lax.fori_loop(0, CHUNKS // UNROLL, chunks, 0)
    g_first = dot_nt(hot_first[...], d_first[...]).astype(BF)
    g_last = dot_nt(hot_last[...], d_last[...]).astype(BF)
    i, k = iota((128, 128), 0), iota((128, 128), 1)
    back = ((k % 4) * RANK + k // 4 == i).astype(F32).astype(BF)
    g_last = dot_nn(g_last, back).astype(BF)
    out[0:256, :] = g_first
    out[256:512, :] = g_last


def own_core_grads(*args):
    scratch = [
        pltpu.VMEM((CHUNKS, 128, 512), BF),
        pltpu.VMEM((R2 * RANK, 128), BF),
        pltpu.VMEM((128, UNIQ), BF),
        pltpu.VMEM((128, UNIQ), BF),
        pltpu.VMEM((128, UNIQ), BF),
        pltpu.VMEM((2 * UNROLL, 128, 256), BF),
        pltpu.VMEM((2 * UNROLL, RANK, 256), F32),
        pltpu.VMEM((256, UNIQ), BF),
        pltpu.VMEM((256, UNIQ), BF),
        pltpu.SemaphoreType.DMA((2 + CHUNKS // UNROLL,)),
    ]
    return call(
        own_kernel, "own_core_grads", ((512, 128), BF), args, scratch, flops=10_000_000_000, smem=(3,),
        left=(1, 4, 5),
    )


def mid_grad_kernel(
    g0, g1, g2, g3, firsts_far, lasts_far, middle, edges, out_far,
    out, grads, firsts, lasts, d_halves, sems,
):
    copies = []
    for g, far in enumerate((g0, g1, g2, g3)):
        pairs = ((far, grads), (firsts_far.at[g], firsts), (lasts_far.at[g], lasts))
        copies.append([
            pltpu.make_async_copy(source, target.at[g], sems.at[3 * g + k])
            for k, (source, target) in enumerate(pairs)
        ])
    for group in copies:
        for copy in group:
            copy.start()

    def clear(k, _):
        at = pl.ds(pl.multiple_of(k * 640, 640), 640)
        out[at, :] = jnp.zeros((640, 128), F32)
        return 0

    lax.fori_loop(0, R2 * RANK // 640, clear, 0)

    def put(k):
        at = pl.ds(k * (R2 // PARTS) * RANK, R2 // PARTS * RANK)
        return pltpu.make_async_copy(out.at[at, :], out_far.at[at, :], sems.at[12 + k])

    for g in range(4):
        for copy in copies[g]:
            copy.wait()

        def mid_grad(c, h, low, d_half):
            at = pl.ds(pl.multiple_of(c * CH, CH), CH)
            q_here = middle[g, pl.ds(c, 1), :].astype(I32)
            q_here = jnp.concatenate([q_here[:, h * HALF : (h + 1) * HALF]] * 4, axis=1)
            first = half_lanes(side_by_side(firsts[g, :, at]), h)
            return dot_nt(masked_block(first, q_here, low, HWIN), d_half)

        def chunks(step, _):
            products = []
            for u in range(UNROLL):
                c = step * UNROLL + u
                at = pl.ds(pl.multiple_of(c * CH, CH), CH)
                d_inner = inner_grad(grads[g, :, at].astype(F32), lasts[g, :, at].astype(F32))
                for h in range(2):
                    d_half = half_lanes(d_inner, h)
                    d_halves[2 * u + h] = d_half
                    low_q = edges[8 * g, 2 * c + h]
                    products.append((low_q, mid_grad(c, h, low_q, d_half)))
            for low_q, product in products:
                out[window_rows(low_q, HWIN), :] += product
            lows = [edges[8 * g, step * 2 * UNROLL + v] for v in range(2 * UNROLL)]
            spans = [edges[8 * g + 1, step * 2 * UNROLL + v] - lows[v] for v in range(2 * UNROLL)]

            @pl.when(functools.reduce(jnp.maximum, spans) >= HWIN)
            def _():
                for v in range(2 * UNROLL):

                    def more(j, _):
                        low = lows[v] + j * HWIN
                        out[window_rows(low, HWIN), :] += mid_grad(
                            step * UNROLL + v // 2, v % 2, low, d_halves[v]
                        )
                        return 0

                    lax.fori_loop(1, spans[v] // HWIN + 1, more, 0)

            if g == 3:
                after = jnp.minimum(step + 1, CHUNKS // UNROLL - 1)
                done = jnp.where(step == CHUNKS // UNROLL - 1, R2, edges[8 * g, after * 2 * UNROLL])
                for k in range(PARTS):

                    @pl.when((lows[0] < (k + 1) * R2 // PARTS) & (done >= (k + 1) * R2 // PARTS))
                    def _():
                        put(k).start()

            return 0

        if g == 3:
            for k in range(PARTS):

                @pl.when(edges[8 * g, 0] >= (k + 1) * R2 // PARTS)
                def _():
                    put(k).start()

        lax.fori_loop(0, CHUNKS // UNROLL, chunks, 0)

    for k in range(PARTS):
        put(k).wait()


def mid_core_grad(row_grads, rows, after):
    scratch = [
        pltpu.VMEM((R2 * RANK, 128), F32),
        pltpu.VMEM((4, EMB, UNIQ), BF),
        pltpu.VMEM((4, 128, UNIQ), BF),
        pltpu.VMEM((4, 128, UNIQ), BF),
        pltpu.VMEM((2 * UNROLL, 128, 256), BF),
        pltpu.SemaphoreType.DMA((12 + PARTS,)),
    ]
    return call(
        mid_grad_kernel, "mid_core_grad", ((R2 * RANK, 128), F32), [*row_grads, *rows], scratch,
        flops=40_000_000_000, after=after, smem=(7,), left=(4, 5), near=(0, 1, 2, 3), out_left=(0,),
    )


BATCH = ("xz", "core")


def exchange(value, axes=BATCH):
    return lax.all_to_all(value, axes, 0, 0, tiled=True)


def from_before(value, places):
    return lax.ppermute(value, "mp", [(i, (i + places) % 4) for i in range(4)])


def gather_mp(value):
    return [value] + [from_before(value, k) for k in (1, 2, 3)]


def from_other_core(value):
    return lax.ppermute(value, "core", [(0, 1), (1, 0)])


def body(
    dense_feats, labels, session_lengths, uniq_rows, dedup_map, core_first, core_mid, core_last,
    bot_w1, bot_b1, bot_w2, bot_b2, bot_w3, bot_b3,
    top_w1, top_b1, top_w2, top_b2, top_w3, top_b3, top_w4, top_b4,
):
    row = lambda v: v.reshape(1, -1)
    pooled, inner, ids, rank, mid, bounds = rebuild(
        uniq_rows.transpose(0, 2, 1, 3), dedup_map, core_first, core_mid, core_last
    )
    arrived = exchange(pooled)
    share = share_prep(top_w1, row(top_b1), top_w2, ids)
    shares = gather_mp(share)
    place = lookup_places(rank, dedup_map, after=[share])
    feats, hb1, hb2, slope1, slope2, slope3, bottom = bottom_forward(
        dense_feats.transpose(0, 2, 1), bot_w1, row(bot_b1), bot_w2, row(bot_b2), bot_w3.T, row(bot_b3)
    )
    d_pooled, top_in, hid1, hid2, hid3, d_act1, d_act2, d_act3, d_bottom, scalars = event_step(
        arrived, bottom, *shares, top_w3, top_w4.T, row(top_b2), row(top_b3), row(top_b4),
        labels, session_lengths, after=[place],
    )
    returned = exchange(d_pooled)
    rows = core_rows(*shares, core_first, core_last, after=[d_pooled])
    keep, send = weight_grads(
        feats, hb1, hb2, slope1, slope2, slope3, bot_w2, bot_w3.T, d_bottom,
        top_in, hid1, hid2, hid3, d_act1, d_act2, d_act3, scalars, after=[rows[0]],
    )
    grads = sum_pair(keep, from_other_core(send))
    parts = exchange(grads.reshape(64, HALF_ROWS // 16, 128), ("mp", "xz"))

    row_grads = scatter_grads(returned, place)
    one, three = from_before(row_grads, 1), from_before(row_grads, 3)
    own = own_core_grads(row_grads, inner, ids, bounds, mid, rows[1])
    later, own = lax.optimization_barrier((row_grads, own))
    all_rows = [row_grads, one, from_before(later, 2), three]
    small = gather_mp(own)
    summed = sum_parts(parts, 64, after=[own, all_rows[1], all_rows[3]])
    half = exchange(summed, ("mp", "xz")).reshape(4, HALF_ROWS, 128)
    grad_mid = mid_core_grad(all_rows, rows, after=[summed, *small[1:]])
    half, grad_mid = lax.optimization_barrier((half, grad_mid))
    outs = unpack([half, from_other_core(half), *small], after=[grad_mid])
    tw1, tb1, tw2, bw1, bb1, bw2, bb2, bw3, bb3, tb2, tw3, tb3, tw4, tb4, loss, grad_first, grad_last = outs

    flat = lambda v: v.reshape(-1)
    return (
        loss[0, 0], grad_first, grad_mid.reshape(R2, 1, 4096).transpose(1, 0, 2),
        grad_last.transpose(1, 0, 2),
        bw1, flat(bb1), bw2, flat(bb2), bw3.T, flat(bb3),
        tw1, flat(tb1), tw2, flat(tb2), tw3, flat(tb3), tw4.T, flat(tb4),
    )


def solution(mesh):
    fine = jax.sharding.Mesh(mesh.devices.reshape(16, 2, 4), ("xz", "core", "mp"))
    split = (
        P("mp", BATCH, None), P("mp", BATCH), P("mp", BATCH, None),
        P(BATCH, "mp", None, None), P(BATCH, "mp", None),
        P(BATCH, None, None), P(BATCH, None, None), P(BATCH, None, None),
        P(), P(), P(), P(), P(), P(),
        P(None, "mp"), P("mp"), P("mp", None), P(), P(), P(), P(), P(),
    )
    out = (
        P(), P(BATCH, None, None), P(BATCH, None, None), P(BATCH, None, None),
        P(), P(), P(), P(), P(), P(),
        P(None, "mp"), P("mp"), P("mp", None), P(), P(), P(), P(), P(),
    )
    return jax.shard_map(body, mesh=fine, in_specs=split, out_specs=out, check_vma=False)
```
